32 devices in a mesh: space: 8 (over y, x, core), tm: 4 (over z).
Axes of the slice: x: 2, y: 2, z: 4, core: 2. Of those that a mesh axis runs over, the one named last changes fastest.
Arguments:
- velocity: bfloat16 [4288, 3, 16384], P('tm', None, 'space'), may hold values from -6 to 6
- rotor_mask: int32 [16384], P('space'), may hold values 0 or 1
- rotor_angle: float32 [4288], P('tm'), may hold values from -3.140625 to 3.140625
- block_starts: int32 [32], replicated, may hold values from 0 to 4031, as said below
- frequencies: int32 [8], replicated, may hold values from 1 to 127, as said below
Outputs:
- spectra: float32 [8, 2, 32, 3, 16384], P('tm', None, None, None, 'space')
- factors: float32 [8, 64, 64], P('tm')
The draws below stay inside these ranges and needn't reach their ends.
Inputs may be any that keep to these rules, and one draw needn't show every extreme that they name: `block_starts`: block b starts at b * 128 plus an offset of 0 to 63 samples; the last block's offset is 63. `frequencies`: distinct; 1 and 127 are always among them.
All inputs are finite; a program needn't handle non-finite values. No bound on the sum of `rotor_mask` on one device may be relied on, other than what follows from the above.
Results may differ from the reference program's by a relative error of at most 0.0033.
Values may be sent and summed in bfloat16 or wider, within the bound.
No kernel may reach another device: no remote copies, remote signals or barrier semaphores. Data moves between devices by JAX's collectives and lax.ppermute only.
A program may use at most 128 MiB of HBM per device.

```python
import math
import jax
import jax.numpy as jnp
from jax import lax

COMPS = 3
NFFT = 256
NB = 32
NF = 8
JIT = 64
HOP = 128
NP = 16384
TS = 4288


def draw_block_starts(key, part):
    offsets = jax.random.randint(key, (NB,), 0, JIT)
    block_index = jnp.arange(NB, dtype=jnp.int32)
    offsets = jnp.where(block_index == NB - 1, JIT - 1, offsets)
    return (block_index * HOP + offsets).astype(jnp.int32)


def draw_frequencies(key, part):
    middle_values = jax.random.permutation(jax.random.fold_in(key, 1), NFFT // 2 - 3) + 2
    picked = jnp.concatenate([jnp.array([1, NFFT // 2 - 1], dtype=jnp.int32), middle_values[:NF - 2].astype(jnp.int32)])
    return jax.random.permutation(jax.random.fold_in(key, 2), picked).astype(jnp.int32)


def place_ends(values, stream_key, least, largest):
    longest = values.shape.index(max(values.shape))
    spots = []
    for shift in (0, 1):
        where = [jax.random.randint(jax.random.fold_in(stream_key, axis), (), 0, length) for axis, length in enumerate(values.shape)]
        where[longest] = (where[longest] + shift) % values.shape[longest]
        spots.append(tuple(where))
    return values.at[spots[0]].set(least).at[spots[1]].set(largest)


def level_of(rng, shape, cuts, least, largest):
    def one(position, parts):
        heights = jax.random.uniform(jax.random.fold_in(jax.random.fold_in(rng, 6), position), (parts,), jnp.float32, least / len(cuts), largest / len(cuts))
        return jnp.repeat(jnp.exp(heights), shape[position] // parts).reshape((-1,) + (1,) * (len(shape) - position - 1))

    loudness = one(*cuts[0])
    for cut in cuts[1:]:
        loudness = loudness * one(*cut)
    return loudness


def gaussian(stream_key, dims, scale, most, split=(), held_as=jnp.bfloat16):
    entries = scale * jax.random.normal(stream_key, dims, jnp.float32)
    if split:
        entries = entries * level_of(stream_key, dims, split, -0.22, 0.18)
    return jnp.clip(entries, -most, most).astype(held_as)


def setup_inputs(seed: int = 0) -> dict:
    keys = jax.random.split(jax.random.key(seed), 6)
    return {
        "velocity": gaussian(keys[0], (TS, COMPS, NP), 1.0, 6.0, ((0, 4), (2, 8))),
        "rotor_mask": place_ends((jax.random.randint(keys[1], (NP,), 0, 2) < 1).astype(jnp.int32), jax.random.fold_in(keys[1], 1), 0, 1),
        "rotor_angle": jnp.clip(jax.random.uniform(keys[2], (TS,), jnp.float32, -3.140625, 3.140625), -3.140625, 3.140625),
        "block_starts": draw_block_starts(jax.random.fold_in(keys[5], 71), 0),
        "frequencies": draw_frequencies(jax.random.fold_in(keys[5], 71), 0),
    }


TWO_PI = 2.0 * math.pi

def to_stator(samples, angles, rotor_mask):
    along_x = samples[:, 0, :].astype(jnp.float32)
    along_y = samples[:, 1, :].astype(jnp.float32)
    cosine = jnp.cos(angles)[:, None]
    sine = jnp.sin(angles)[:, None]
    turning = (rotor_mask == 1)[None, :]
    new_x = jnp.where(turning, cosine * along_x - sine * along_y, along_x)
    new_y = jnp.where(turning, sine * along_x + cosine * along_y, along_y)
    third = samples[:, 2, :].astype(jnp.float32)
    return jnp.stack([new_x, new_y, third], axis=1).astype(jnp.bfloat16)

def window_rows(frequencies, block_starts, sample_ids, length):
    offsets = sample_ids[None, :] - block_starts[:, None]
    inside = (offsets >= 0) & (offsets < length)
    clipped = jnp.clip(offsets, 0, length - 1).astype(jnp.int32)
    phases = frequencies[:, None, None] * clipped[None, :, :] % length
    turns = phases.astype(jnp.float32) * (TWO_PI / length)
    taper = (0.5 - 0.5 * jnp.cos(clipped.astype(jnp.float32) * (TWO_PI / length))) * (8.0 / (3.0 * length)) ** 0.5
    real_part = jnp.where(inside[None], taper[None] * jnp.cos(turns), 0.0)
    imag_part = jnp.where(inside[None], -(taper[None] * jnp.sin(turns)), 0.0)
    return jnp.stack([real_part, imag_part], axis=1).astype(jnp.bfloat16)

def reference(velocity, rotor_mask, rotor_angle, block_starts, frequencies):
    basis_rows = window_rows(frequencies, jnp.zeros((1,), jnp.int32), jnp.arange(NFFT, dtype=jnp.int32), NFFT)
    basis_rows = basis_rows.reshape(NF * 2, NFFT)

    def one_block(start):
        samples = lax.dynamic_slice_in_dim(velocity, start, NFFT, 0)
        angles = lax.dynamic_slice_in_dim(rotor_angle, start, NFFT, 0)
        rotated = to_stator(samples, angles, rotor_mask)
        return jnp.dot(basis_rows.astype(jnp.float32), rotated.reshape(NFFT, COMPS * NP).astype(jnp.float32), preferred_element_type=jnp.float32)
    blocks = lax.map(one_block, block_starts)
    spectra = blocks.reshape(NB, NF, 2, COMPS, NP).transpose(1, 2, 0, 3, 4)

    def one_factor(rows):
        flat_rows = rows.reshape(2 * NB, COMPS * NP)
        gram = jnp.dot(flat_rows.astype(jnp.float32), flat_rows.T.astype(jnp.float32), precision=lax.Precision.HIGHEST, preferred_element_type=jnp.float32) / (COMPS * NP)
        return jnp.linalg.cholesky(gram).T
    factors = lax.map(one_factor, spectra)
    return (spectra, factors)
```

```python
import functools
import math

import jax
import jax.numpy as jnp
from jax import lax
from jax.experimental import pallas as pl
from jax.experimental.pallas import tpu as pltpu
from jax.sharding import PartitionSpec as P

COMPS = 3
NFFT = 256
JIT = 64
HOP = 128
LANES = 128
TILE = 256
SCALE = (8.0 / (3.0 * NFFT)) ** 0.5
HIGHEST = lax.Precision.HIGHEST


def first_block(shard, span):
    return jnp.maximum((shard * span - (NFFT + JIT - 1) + HOP) // HOP, 0)


def slot_count(shards, span, blocks, rows_per_slot):
    most = 0
    for s in range(shards):
        lo = max((s * span - (NFFT + JIT - 1) + HOP) // HOP, 0)
        hi = min((span * (s + 1) - 1) // HOP, blocks - 1)
        most = max(most, hi - lo + 1)
    step = 16 // math.gcd(16, rows_per_slot)
    return -(-most // step) * step


def half_turn_sine(x):
    z = x * x
    c = [math.pi ** (2 * i + 1) * (-1) ** i / math.factorial(2 * i + 1) for i in range(7)]
    acc = jnp.full_like(z, c[-1])
    for term in c[-2::-1]:
        acc = acc * z + term
    return acc * x


def build_rows(n, owned, slots, span, blocks, me, starts_ref, freqs_ref, a_ref):
    group = owned * 2
    rid = lax.broadcasted_iota(jnp.int32, (n * group, 1), 0)
    k_of, j_of, r_of = rid // group, (rid // 2) % owned, rid % 2
    f_of = lax.rem(me + k_of, n) * owned + j_of
    freq = jnp.zeros((n * group, 1), jnp.float32)
    for f in range(n * owned):
        freq = jnp.where(f_of == f, freqs_ref[f].astype(jnp.float32), freq)
    step = freq * (1.0 / NFFT)
    quarter = r_of.astype(jnp.float32) * 0.25
    lo = first_block(me, span)
    sample = lax.broadcasted_iota(jnp.int32, (1, span), 1) + me * span
    pieces = [[] for _ in range(n)]
    for s in range(slots):
        b = lo + s
        start = starts_ref[jnp.minimum(b, blocks - 1)]
        ni = sample - start
        inside = (ni >= 0) & (ni < NFFT) & (b < blocks)
        nf = ni.astype(jnp.float32)
        w = half_turn_sine(jnp.minimum(nf, NFFT - nf) * (1.0 / NFFT))
        w = jnp.where(inside, w * w * SCALE, 0.0)
        nf = jnp.where(inside, nf, 0.0)
        turns = nf * step + quarter
        turns = turns - jnp.floor(turns + 0.5)
        h = half_turn_sine(turns)
        rows = w * (1.0 - 2.0 * h * h)
        for k in range(n):
            pieces[k].append(rows[k * group:(k + 1) * group])
    for k in range(n):
        a_ref[k] = jnp.concatenate(pieces[k], axis=0).astype(jnp.bfloat16)


def spread_column(row, span, out_ref):
    for at in range(0, span, LANES):
        width = min(LANES, span - at)
        part = row[:, at:at + width]
        if width < LANES:
            part = jnp.concatenate([part, jnp.zeros((1, LANES - width), jnp.float32)], axis=1)
        turned = jnp.transpose(jnp.broadcast_to(part, (LANES, LANES)))
        out_ref[at:at + width, :] = turned[:width]


def dft_body(n, owned, slots, span, blocks, first, *refs):
    if first:
        pos_ref, starts_ref, freqs_ref, angle_ref, mask_ref, vel_ref = refs[:6]
        outs = refs[6:6 + n]
        a_ref, cos_ref, sin_ref = refs[6 + n:9 + n]
        rot_ref = refs[9 + n]

        @pl.when(pl.program_id(0) == 0)
        def _():
            build_rows(n, owned, slots, span, blocks, pos_ref[0], starts_ref, freqs_ref, a_ref)
            spread_column(jnp.cos(angle_ref[...]), span, cos_ref)
            spread_column(jnp.sin(angle_ref[...]), span, sin_ref)
    else:
        mask_ref, vel_ref, a_ref, cos_ref, sin_ref = refs[:5]
        outs = refs[5:5 + n]
        rot_ref = refs[5 + n]
    width = vel_ref.shape[2]
    turning = mask_ref[...] == 1
    for at in range(0, span, 16):
        rows = min(16, span - at)
        here = pl.ds(at, rows)
        cosine = jnp.concatenate([cos_ref[here, :]] * (width // LANES), axis=1)
        sine = jnp.concatenate([sin_ref[here, :]] * (width // LANES), axis=1)
        x = vel_ref[0, here, :].astype(jnp.float32)
        y = vel_ref[1, here, :].astype(jnp.float32)
        rot_ref[0, here, :] = jnp.where(turning, cosine * x - sine * y, x).astype(jnp.bfloat16)
        rot_ref[1, here, :] = jnp.where(turning, sine * x + cosine * y, y).astype(jnp.bfloat16)
    rows = a_ref.shape[1]
    a = a_ref[...].reshape(n * rows, span)
    for c in range(COMPS):
        samples = rot_ref[c] if c < 2 else vel_ref[2]
        sums = jnp.dot(a, samples, preferred_element_type=jnp.float32).astype(jnp.bfloat16)
        for k in range(n):
            outs[k][c * rows:(c + 1) * rows, :] = sums[k * rows:(k + 1) * rows]


def dft_call(n, owned, slots, blocks, first, offset, points, position, starts, freqs, angles, mask, velocity, shared):
    span = velocity.shape[1]
    rows = slots * owned * 2
    shift = offset // TILE
    whole = lambda shape: pl.BlockSpec(shape, lambda i: (0,) * len(shape))
    smem = pl.BlockSpec(memory_space=pltpu.SMEM)
    data_specs = [
        pl.BlockSpec((1, TILE), lambda i: (0, i + shift)),
        pl.BlockSpec((COMPS, span, TILE), lambda i: (0, 0, i + shift)),
    ]
    shared_types = [
        jax.ShapeDtypeStruct((n, rows, span), jnp.bfloat16),
        jax.ShapeDtypeStruct((span, LANES), jnp.float32),
        jax.ShapeDtypeStruct((span, LANES), jnp.float32),
    ]
    shared_specs = [whole(t.shape) for t in shared_types]
    out_types = [jax.ShapeDtypeStruct((COMPS * rows, points), jnp.bfloat16)] * n
    out_specs = [pl.BlockSpec((COMPS * rows, TILE), lambda i: (0, i))] * n
    if first:
        args = (position, starts, freqs, angles, mask, velocity)
        in_specs = [smem] * 3 + [whole((1, span))] + data_specs
        out_types = out_types + shared_types
        out_specs = out_specs + shared_specs
    else:
        args = (mask, velocity) + tuple(shared)
        in_specs = data_specs + shared_specs
    out = pl.pallas_call(
        functools.partial(dft_body, n, owned, slots, span, blocks, first),
        grid=(points // TILE,),
        out_shape=out_types,
        in_specs=in_specs,
        out_specs=out_specs,
        scratch_shapes=[pltpu.VMEM((2, span, TILE), jnp.bfloat16)],
        compiler_params=pltpu.CompilerParams(vmem_limit_bytes=40 * 2**20),
        cost_estimate=pl.CostEstimate(
            flops=2 * n * rows * span * COMPS * points,
            bytes_accessed=2 * COMPS * span * points,
            transcendentals=0,
        ),
        name="rotate_dft",
    )(*args)
    return out[:n], out[n:] if first else shared


def selection(n, owned, slots, span, blocks, me):
    rows = slots * owned * 2
    shape = (owned * 2 * blocks, n * rows)
    out = lax.broadcasted_iota(jnp.int32, shape, 0)
    col = lax.broadcasted_iota(jnp.int32, shape, 1)
    k_of = jnp.zeros(shape, jnp.int32)
    lo = jnp.broadcast_to(first_block(me, span), shape)
    for k in range(1, n):
        past = col >= k * rows
        k_of = jnp.where(past, k, k_of)
        lo = jnp.where(past, first_block(lax.rem(me + n - k, n), span), lo)
    rem = col - k_of * rows
    slot = rem // (owned * 2)
    same = (out // blocks == rem % (owned * 2)) & (out % blocks == lo + slot)
    return jnp.where(same, 1.0, 0.0)


def assemble_body(n, owned, slots, span, blocks, total, has_sum, last, *refs):
    pos_ref = refs[0]
    parts = refs[1:1 + n]
    rest = refs[1 + n:]
    if has_sum:
        sum_in, rest = rest[0], rest[2:]
    spectra_ref, gram_ref, sel_ref, acc_ref = rest
    step = pl.program_id(0)
    rows = slots * owned * 2

    @pl.when(step == 0)
    def _():
        sel_ref[...] = selection(n, owned, slots, span, blocks, pos_ref[0]).astype(jnp.bfloat16)
        acc_ref[...] = sum_in[...] if has_sum else jnp.zeros_like(acc_ref)

    for c in range(COMPS):
        stack = jnp.concatenate([p[c * rows:(c + 1) * rows, :] for p in parts], axis=0)
        full = jnp.dot(sel_ref[...], stack, preferred_element_type=jnp.float32)
        for j in range(owned):
            for r in range(2):
                at = (j * 2 + r) * blocks
                spectra_ref[j, r, c] = full[at:at + blocks]
        acc_ref[...] += lax.dot_general(
            stack, stack, (((1,), (1,)), ((), ())), preferred_element_type=jnp.float32
        )

    @pl.when(step == pl.num_programs(0) - 1)
    def _():
        if not last:
            gram_ref[...] = acc_ref[...]
        else:
            sel = sel_ref[...].astype(jnp.float32)
            half = jnp.dot(sel, acc_ref[...], precision=HIGHEST, preferred_element_type=jnp.float32)
            order = 2 * blocks
            gram = lax.dot_general(
                half, sel, (((1,), (1,)), ((), ())), precision=HIGHEST, preferred_element_type=jnp.float32
            ) * (1.0 / total)
            gram_ref[...] = jnp.concatenate(
                [gram[j * order:(j + 1) * order, j * order:(j + 1) * order] for j in range(owned)], axis=1
            )


def assemble_call(n, owned, slots, span, blocks, total, offset, points, all_points, position, parts, spectra, gram, last):
    rows = slots * owned * 2
    tile = min(points, 512)
    shift = offset // tile
    order = 2 * blocks
    has_sum = gram is not None
    whole = lambda shape: pl.BlockSpec(shape, lambda i: (0,) * len(shape))
    gram_shape = (order, owned * order) if last else (n * rows, n * rows)
    args = [position] + list(parts)
    in_specs = [pl.BlockSpec(memory_space=pltpu.SMEM)] + [pl.BlockSpec((COMPS * rows, tile), lambda i: (0, i))] * n
    aliases = {}
    if has_sum:
        args += [gram, spectra]
        in_specs += [whole((n * rows, n * rows)), pl.BlockSpec(memory_space=pl.ANY)]
        aliases = {len(args) - 1: 0}
    return pl.pallas_call(
        functools.partial(assemble_body, n, owned, slots, span, blocks, total, has_sum, last),
        grid=(points // tile,),
        out_shape=[
            jax.ShapeDtypeStruct((owned, 2, COMPS, blocks, all_points), jnp.float32),
            jax.ShapeDtypeStruct(gram_shape, jnp.float32),
        ],
        in_specs=in_specs,
        out_specs=[
            pl.BlockSpec((owned, 2, COMPS, blocks, tile), lambda i: (0, 0, 0, 0, i + shift)),
            whole(gram_shape),
        ],
        scratch_shapes=[
            pltpu.VMEM((owned * order, n * rows), jnp.bfloat16),
            pltpu.VMEM((n * rows, n * rows), jnp.float32),
        ],
        input_output_aliases=aliases,
        compiler_params=pltpu.CompilerParams(vmem_limit_bytes=40 * 2**20),
        cost_estimate=pl.CostEstimate(
            flops=4 * (n * rows) ** 2 * COMPS * points,
            bytes_accessed=4 * owned * order * COMPS * points,
            transcendentals=0,
        ),
        name="assemble",
    )(*args)


def factor_body(owned, order, count, *refs):
    parts = refs[:count]
    out_ref, row_ref = refs[count:]
    s = parts[0][...]
    for p in parts[1:]:
        s = s + p[...]
    lane = lax.broadcasted_iota(jnp.int32, (1, owned * order), 1)
    for k in range(order):
        base = k // 8 * 8
        s = s[base - (k - 1) // 8 * 8:] if k else s
        column = jnp.broadcast_to(s[:, k:k + 1], s.shape)
        for j in range(1, owned):
            column = jnp.where(lane >= j * order, s[:, j * order + k:j * order + k + 1], column)
        at = k - base
        pivot = column[at:at + 1]
        inverse_root = lax.rsqrt(pivot)
        row = s[at:at + 1] * inverse_root
        row_ref[k:k + 1, :] = jnp.where(lane % order >= k, row, 0.0)
        s = s - column * (row * inverse_root)
    for j in range(owned):
        out_ref[j] = row_ref[:, j * order:(j + 1) * order]


def factor_call(owned, order, parts):
    return pl.pallas_call(
        functools.partial(factor_body, owned, order, len(parts)),
        out_shape=jax.ShapeDtypeStruct((owned, order, order), jnp.float32),
        scratch_shapes=[pltpu.VMEM((order, owned * order), jnp.float32)],
        name="factor",
    )(*parts)


def chunks_of(points):
    tile = 512
    return [(at, tile) for at in range(0, points, tile)]


def per_device(velocity, rotor_mask, rotor_angle, block_starts, frequencies):
    span, _, points = velocity.shape
    n = lax.axis_size("tm")
    groups = lax.axis_size("space")
    blocks = block_starts.shape[0]
    owned = frequencies.shape[0] // n
    order = 2 * blocks
    slots = slot_count(n, span, blocks, owned * 2)
    position = lax.axis_index("tm").astype(jnp.int32).reshape(1)
    samples = velocity.transpose(1, 0, 2)
    mask = rotor_mask.reshape(1, points)
    angles = rotor_angle.reshape(1, span)

    pieces = []
    shared = None
    for at, count in chunks_of(points):
        sums, shared = dft_call(
            n, owned, slots, blocks, shared is None, at, count,
            position, block_starts, frequencies, angles, mask, samples, shared,
        )
        moved = [sums[0]] + [
            lax.ppermute(sums[k], "tm", [(i, (i + k) % n) for i in range(n)]) for k in range(1, n)
        ]
        pieces.append((at, count, moved))

    spectra, gram = None, None
    total = COMPS * points * groups
    for at, count, moved in pieces:
        last = at + count == points
        spectra, gram = assemble_call(
            n, owned, slots, span, blocks, total, at, count, points, position, moved, spectra, gram, last
        )
    if groups <= 8:
        grams = [gram] + [
            lax.ppermute(gram, "space", [(i, (i + k) % groups) for i in range(groups)]) for k in range(1, groups)
        ]
    else:
        grams = [lax.psum(gram, "space")]
    factors = factor_call(owned, order, grams)
    return spectra.transpose(0, 1, 3, 2, 4), factors


def solution(mesh):
    in_specs = (P("tm", None, "space"), P("space"), P("tm"), P(), P())
    out_specs = (P("tm", None, None, None, "space"), P("tm", None, None))
    return jax.shard_map(
        per_device, mesh=mesh, in_specs=in_specs, out_specs=out_specs, check_vma=False
    )
```

```python
import functools
import math

import jax
import jax.numpy as jnp
from jax import lax
from jax.experimental import pallas as pl
from jax.experimental.pallas import tpu as pltpu
from jax.sharding import PartitionSpec as P

COMPS = 3
NFFT = 256
JIT = 64
HOP = 128
LANES = 128
TILE = 256
PIVOT = 4
SCALE = (8.0 / (3.0 * NFFT)) ** 0.5
HIGHEST = lax.Precision.HIGHEST


def first_block(shard, span):
    return jnp.maximum((shard * span - (NFFT + JIT - 1) + HOP) // HOP, 0)


def slot_count(shards, span, blocks, rows_per_slot):
    most = 0
    for s in range(shards):
        lo = max((s * span - (NFFT + JIT - 1) + HOP) // HOP, 0)
        hi = min((span * (s + 1) - 1) // HOP, blocks - 1)
        most = max(most, hi - lo + 1)
    step = 16 // math.gcd(16, rows_per_slot)
    return -(-most // step) * step


def half_turn_sine(x):
    z = x * x
    c = [math.pi ** (2 * i + 1) * (-1) ** i / math.factorial(2 * i + 1) for i in range(7)]
    acc = jnp.full_like(z, c[-1])
    for term in c[-2::-1]:
        acc = acc * z + term
    return acc * x


def build_rows(n, owned, slots, span, blocks, me, starts_ref, freqs_ref, a_ref):
    group = owned * 2
    rid = lax.broadcasted_iota(jnp.int32, (n * group, 1), 0)
    k_of, j_of, r_of = rid // group, (rid // 2) % owned, rid % 2
    f_of = lax.rem(me + k_of, n) * owned + j_of
    freq = jnp.zeros((n * group, 1), jnp.float32)
    for f in range(n * owned):
        freq = jnp.where(f_of == f, freqs_ref[f].astype(jnp.float32), freq)
    step = freq * (1.0 / NFFT)
    quarter = r_of.astype(jnp.float32) * 0.25
    lo = first_block(me, span)
    sample = lax.broadcasted_iota(jnp.int32, (1, span), 1) + me * span
    pieces = [[] for _ in range(n)]
    for s in range(slots):
        b = lo + s
        start = starts_ref[jnp.minimum(b, blocks - 1)]
        ni = sample - start
        inside = (ni >= 0) & (ni < NFFT) & (b < blocks)
        nf = ni.astype(jnp.float32)
        w = half_turn_sine(jnp.minimum(nf, NFFT - nf) * (1.0 / NFFT))
        w = jnp.where(inside, w * w * SCALE, 0.0)
        nf = jnp.where(inside, nf, 0.0)
        turns = nf * step + quarter
        turns = turns - jnp.floor(turns + 0.5)
        h = half_turn_sine(turns)
        rows = w * (1.0 - 2.0 * h * h)
        for k in range(n):
            pieces[k].append(rows[k * group:(k + 1) * group])
    for k in range(n):
        a_ref[k] = jnp.concatenate(pieces[k], axis=0).astype(jnp.bfloat16)


def spread_column(row, span, out_ref):
    for at in range(0, span, LANES):
        width = min(LANES, span - at)
        part = row[:, at:at + width]
        if width < LANES:
            part = jnp.concatenate([part, jnp.zeros((1, LANES - width), jnp.float32)], axis=1)
        turned = jnp.transpose(jnp.broadcast_to(part, (LANES, LANES)))
        out_ref[at:at + width, :] = turned[:width]


def dft_body(n, owned, slots, span, blocks, first, *refs):
    if first:
        pos_ref, starts_ref, freqs_ref, angle_ref, mask_ref, vel_ref = refs[:6]
        outs = refs[6:6 + n]
        a_ref, cos_ref, sin_ref = refs[6 + n:9 + n]
        rot_ref = refs[9 + n]

        @pl.when(pl.program_id(0) == 0)
        def _():
            build_rows(n, owned, slots, span, blocks, pos_ref[0], starts_ref, freqs_ref, a_ref)
            spread_column(jnp.cos(angle_ref[...].reshape(1, span)), span, cos_ref)
            spread_column(jnp.sin(angle_ref[...].reshape(1, span)), span, sin_ref)
    else:
        mask_ref, vel_ref, a_ref, cos_ref, sin_ref = refs[:5]
        outs = refs[5:5 + n]
        rot_ref = refs[5 + n]
    width = vel_ref.shape[2]
    turning = mask_ref[...] == 1
    for at in range(0, span, 16):
        rows = min(16, span - at)
        here = pl.ds(at, rows)
        cosine = jnp.concatenate([cos_ref[here, :]] * (width // LANES), axis=1)
        sine = jnp.concatenate([sin_ref[here, :]] * (width // LANES), axis=1)
        x = vel_ref[0, here, :].astype(jnp.float32)
        y = vel_ref[1, here, :].astype(jnp.float32)
        rot_ref[0, here, :] = jnp.where(turning, cosine * x - sine * y, x).astype(jnp.bfloat16)
        rot_ref[1, here, :] = jnp.where(turning, sine * x + cosine * y, y).astype(jnp.bfloat16)
    rows = a_ref.shape[1]
    a = a_ref[...].reshape(n * rows, span)
    for c in range(COMPS):
        samples = rot_ref[c] if c < 2 else vel_ref[2]
        sums = jnp.dot(a, samples, preferred_element_type=jnp.float32).astype(jnp.bfloat16)
        for k in range(n):
            outs[k][c * rows:(c + 1) * rows, :] = sums[k * rows:(k + 1) * rows]


def dft_call(n, owned, slots, blocks, first, offset, points, position, starts, freqs, angles, mask, velocity, shared):
    span = velocity.shape[1]
    rows = slots * owned * 2
    shift = offset // TILE
    whole = lambda shape: pl.BlockSpec(shape, lambda i: (0,) * len(shape))
    smem = pl.BlockSpec(memory_space=pltpu.SMEM)
    data_specs = [
        pl.BlockSpec((1, TILE), lambda i: (0, i + shift)),
        pl.BlockSpec((COMPS, span, TILE), lambda i: (0, 0, i + shift)),
    ]
    shared_types = [
        jax.ShapeDtypeStruct((n, rows, span), jnp.bfloat16),
        jax.ShapeDtypeStruct((span, LANES), jnp.float32),
        jax.ShapeDtypeStruct((span, LANES), jnp.float32),
    ]
    shared_specs = [whole(t.shape) for t in shared_types]
    out_types = [jax.ShapeDtypeStruct((COMPS * rows, points), jnp.bfloat16)] * n
    out_specs = [pl.BlockSpec((COMPS * rows, TILE), lambda i: (0, i))] * n
    if first:
        args = (position, starts, freqs, angles, mask, velocity)
        in_specs = [smem] * 3 + [whole((span,))] + data_specs
        out_types = out_types + shared_types
        out_specs = out_specs + shared_specs
    else:
        args = (mask, velocity) + tuple(shared)
        in_specs = data_specs + shared_specs
    out = pl.pallas_call(
        functools.partial(dft_body, n, owned, slots, span, blocks, first),
        grid=(points // TILE,),
        out_shape=out_types,
        in_specs=in_specs,
        out_specs=out_specs,
        scratch_shapes=[pltpu.VMEM((2, span, TILE), jnp.bfloat16)],
        compiler_params=pltpu.CompilerParams(vmem_limit_bytes=(60 if first else 40) * 2**20),
        cost_estimate=pl.CostEstimate(
            flops=2 * n * rows * span * COMPS * points,
            bytes_accessed=2 * COMPS * span * points,
            transcendentals=0,
        ),
        name="rotate_dft",
    )(*args)
    return out[:n], out[n:] if first else shared


def selection(n, owned, slots, span, blocks, me):
    rows = slots * owned * 2
    shape = (owned * 2 * blocks, n * rows)
    out = lax.broadcasted_iota(jnp.int32, shape, 0)
    col = lax.broadcasted_iota(jnp.int32, shape, 1)
    k_of = jnp.zeros(shape, jnp.int32)
    lo = jnp.broadcast_to(first_block(me, span), shape)
    for k in range(1, n):
        past = col >= k * rows
        k_of = jnp.where(past, k, k_of)
        lo = jnp.where(past, first_block(lax.rem(me + n - k, n), span), lo)
    rem = col - k_of * rows
    slot = rem // (owned * 2)
    same = (out // blocks == rem % (owned * 2)) & (out % blocks == lo + slot)
    return jnp.where(same, 1.0, 0.0)


def assemble_body(n, owned, slots, span, blocks, total, has_sum, last, *refs):
    pos_ref = refs[0]
    parts = refs[1:1 + n]
    rest = refs[1 + n:]
    if has_sum:
        sum_in, rest = rest[0], rest[2:]
    spectra_ref, gram_ref, sel_ref, acc_ref = rest
    step = pl.program_id(0)
    rows = slots * owned * 2

    @pl.when(step == 0)
    def _():
        sel_ref[...] = selection(n, owned, slots, span, blocks, pos_ref[0]).astype(jnp.bfloat16)
        acc_ref[...] = sum_in[...] if has_sum else jnp.zeros_like(acc_ref)

    for c in range(COMPS):
        stack = jnp.concatenate([p[c * rows:(c + 1) * rows, :] for p in parts], axis=0)
        full = jnp.dot(sel_ref[...], stack, preferred_element_type=jnp.float32)
        for j in range(owned):
            for r in range(2):
                at = (j * 2 + r) * blocks
                spectra_ref[j, r, c] = full[at:at + blocks]
        acc_ref[...] += lax.dot_general(
            stack, stack, (((1,), (1,)), ((), ())), preferred_element_type=jnp.float32
        )

    @pl.when(step == pl.num_programs(0) - 1)
    def _():
        if not last:
            gram_ref[...] = acc_ref[...]
        else:
            sel = sel_ref[...].astype(jnp.float32)
            half = jnp.dot(sel, acc_ref[...], precision=HIGHEST, preferred_element_type=jnp.float32)
            order = 2 * blocks
            gram = lax.dot_general(
                half, sel, (((1,), (1,)), ((), ())), precision=HIGHEST, preferred_element_type=jnp.float32
            ) * (1.0 / total)
            gram = jnp.concatenate(
                [gram[j * order:(j + 1) * order, j * order:(j + 1) * order] for j in range(owned)], axis=1
            )
            for at in range(0, gram_ref.shape[0], order):
                gram_ref[at:at + order, :] = gram


def assemble_call(n, owned, slots, span, blocks, total, offset, points, all_points, position, parts, spectra, gram, last, copies):
    rows = slots * owned * 2
    tile = min(points, 512)
    shift = offset // tile
    order = 2 * blocks
    has_sum = gram is not None
    whole = lambda shape: pl.BlockSpec(shape, lambda i: (0,) * len(shape))
    gram_shape = (copies * order, owned * order) if last else (n * rows, n * rows)
    args = [position] + list(parts)
    in_specs = [pl.BlockSpec(memory_space=pltpu.SMEM)] + [pl.BlockSpec((COMPS * rows, tile), lambda i: (0, i))] * n
    aliases = {}
    if has_sum:
        args += [gram, spectra]
        in_specs += [whole((n * rows, n * rows)), pl.BlockSpec(memory_space=pl.ANY)]
        aliases = {len(args) - 1: 0}
    return pl.pallas_call(
        functools.partial(assemble_body, n, owned, slots, span, blocks, total, has_sum, last),
        grid=(points // tile,),
        out_shape=[
            jax.ShapeDtypeStruct((owned, 2, COMPS, blocks, all_points), jnp.float32),
            jax.ShapeDtypeStruct(gram_shape, jnp.float32),
        ],
        in_specs=in_specs,
        out_specs=[
            pl.BlockSpec((owned, 2, COMPS, blocks, tile), lambda i: (0, 0, 0, 0, i + shift)),
            whole(gram_shape),
        ],
        scratch_shapes=[
            pltpu.VMEM((owned * order, n * rows), jnp.bfloat16),
            pltpu.VMEM((n * rows, n * rows), jnp.float32),
        ],
        input_output_aliases=aliases,
        compiler_params=pltpu.CompilerParams(vmem_limit_bytes=40 * 2**20),
        cost_estimate=pl.CostEstimate(
            flops=4 * (n * rows) ** 2 * COMPS * points,
            bytes_accessed=4 * owned * order * COMPS * points,
            transcendentals=0,
        ),
        name="assemble",
    )(*args)


def factor_body(owned, order, count, *refs):
    parts = refs[:count]
    out_ref, row_ref = refs[count:]
    s = parts[0][...]
    if len(s.shape) == 3:
        s = sum(s[i] for i in range(s.shape[0]))
    lane = lax.broadcasted_iota(jnp.int32, (1, owned * order), 1)
    for k in range(0, order, PIVOT):
        base = k // 8 * 8
        s = s[base - max(k - PIVOT, 0) // 8 * 8:]
        columns = []
        for i in range(k, k + PIVOT):
            column = jnp.broadcast_to(s[:, i:i + 1], s.shape)
            for j in range(1, owned):
                column = jnp.where(lane >= j * order, s[:, j * order + i:j * order + i + 1], column)
            columns.append(column)
        at = k - base
        rows = [s[at + i:at + i + 1] for i in range(PIVOT)]
        for i in range(PIVOT):
            inverse_root = lax.rsqrt(columns[i][at + i:at + i + 1])
            columns[i] = columns[i] * inverse_root
            rows[i] = rows[i] * inverse_root
            for j in range(i + 1, PIVOT):
                weight = columns[i][at + j:at + j + 1]
                columns[j] = columns[j] - columns[i] * weight
                rows[j] = rows[j] - rows[i] * weight
            row_ref[k + i:k + i + 1, :] = jnp.where(lane % order >= k + i, rows[i], 0.0)
            s = s - columns[i] * rows[i]
    for j in range(owned):
        out_ref[j] = row_ref[:, j * order:(j + 1) * order]


def factor_call(owned, order, parts):
    return pl.pallas_call(
        functools.partial(factor_body, owned, order, len(parts)),
        out_shape=jax.ShapeDtypeStruct((owned, order, order), jnp.float32),
        scratch_shapes=[pltpu.VMEM((order, owned * order), jnp.float32)],
        name="factor",
    )(*parts)


def chunks_of(points):
    tile = 512
    return [(at, tile) for at in range(0, points, tile)]


def per_device(velocity, rotor_mask, rotor_angle, block_starts, frequencies):
    span, _, points = velocity.shape
    n = lax.axis_size("tm")
    groups = lax.axis_size("space")
    blocks = block_starts.shape[0]
    owned = frequencies.shape[0] // n
    order = 2 * blocks
    slots = slot_count(n, span, blocks, owned * 2)
    position = lax.axis_index("tm").astype(jnp.int32).reshape(1)
    samples = velocity.transpose(1, 0, 2)
    mask = rotor_mask.reshape(1, points)
    angles = rotor_angle

    pieces = []
    shared = None
    for at, count in chunks_of(points):
        sums, shared = dft_call(
            n, owned, slots, blocks, shared is None, at, count,
            position, block_starts, frequencies, angles, mask, samples, shared,
        )
        moved = [sums[0]] + [
            lax.ppermute(sums[k], "tm", [(i, (i + k) % n) for i in range(n)]) for k in range(1, n)
        ]
        pieces.append((at, count, moved))

    spectra, gram = None, None
    total = COMPS * points * groups
    for at, count, moved in pieces:
        last = at + count == points
        spectra, gram = assemble_call(
            n, owned, slots, span, blocks, total, at, count, points, position, moved, spectra, gram, last, groups if groups <= 8 else 1
        )
    if groups <= 8:
        gram = lax.all_to_all(gram, "space", 0, 0, tiled=True).reshape(groups, order, owned * order)
    else:
        gram = lax.psum(gram, "space")
    factors = factor_call(owned, order, [gram])
    return spectra.transpose(0, 1, 3, 2, 4), factors


def solution(mesh):
    in_specs = (P("tm", None, "space"), P("space"), P("tm"), P(), P())
    out_specs = (P("tm", None, None, None, "space"), P("tm", None, None))
    return jax.shard_map(
        per_device, mesh=mesh, in_specs=in_specs, out_specs=out_specs, check_vma=False
    )
```

```python
import functools
import math

import jax
import jax.numpy as jnp
from jax import lax
from jax.experimental import pallas as pl
from jax.experimental.pallas import tpu as pltpu
from jax.sharding import PartitionSpec as P

COMPS = 3
NFFT = 256
JIT = 64
HOP = 128
LANES = 128
TILE = 256
PIVOT = 4
SCALE = (8.0 / (3.0 * NFFT)) ** 0.5
HIGHEST = lax.Precision.HIGHEST
SHORT = pl.CostEstimate(flops=1000, bytes_accessed=1000, transcendentals=0)


def first_block(shard, span):
    return jnp.maximum((shard * span - (NFFT + JIT - 1) + HOP) // HOP, 0)


def slot_count(shards, span, blocks, rows_per_slot):
    most = 0
    for s in range(shards):
        lo = max((s * span - (NFFT + JIT - 1) + HOP) // HOP, 0)
        hi = min((span * (s + 1) - 1) // HOP, blocks - 1)
        most = max(most, hi - lo + 1)
    step = 16 // math.gcd(16, rows_per_slot)
    return -(-most // step) * step


def half_turn_sine(x):
    z = x * x
    c = [math.pi ** (2 * i + 1) * (-1) ** i / math.factorial(2 * i + 1) for i in range(7)]
    acc = jnp.full_like(z, c[-1])
    for term in c[-2::-1]:
        acc = acc * z + term
    return acc * x


def build_rows(n, owned, slots, span, blocks, me, starts_ref, freqs_ref, a_ref):
    group = owned * 2
    rid = lax.broadcasted_iota(jnp.int32, (n * group, 1), 0)
    k_of, j_of, r_of = rid // group, (rid // 2) % owned, rid % 2
    f_of = lax.rem(me + k_of, n) * owned + j_of
    freq = jnp.zeros((n * group, 1), jnp.float32)
    for f in range(n * owned):
        freq = jnp.where(f_of == f, freqs_ref[f].astype(jnp.float32), freq)
    step = freq * (1.0 / NFFT)
    quarter = r_of.astype(jnp.float32) * 0.25
    lo = first_block(me, span)
    sample = lax.broadcasted_iota(jnp.int32, (1, span), 1) + me * span
    pieces = [[] for _ in range(n)]
    for s in range(slots):
        b = lo + s
        start = starts_ref[jnp.minimum(b, blocks - 1)]
        ni = sample - start
        inside = (ni >= 0) & (ni < NFFT) & (b < blocks)
        nf = ni.astype(jnp.float32)
        w = half_turn_sine(jnp.minimum(nf, NFFT - nf) * (1.0 / NFFT))
        w = jnp.where(inside, w * w * SCALE, 0.0)
        nf = jnp.where(inside, nf, 0.0)
        turns = nf * step + quarter
        turns = turns - jnp.floor(turns + 0.5)
        h = half_turn_sine(turns)
        rows = w * (1.0 - 2.0 * h * h)
        for k in range(n):
            pieces[k].append(rows[k * group:(k + 1) * group])
    for k in range(n):
        a_ref[k] = jnp.concatenate(pieces[k], axis=0).astype(jnp.bfloat16)


def spread_column(row, span, out_ref):
    for at in range(0, span, LANES):
        width = min(LANES, span - at)
        part = row[:, at:at + width]
        if width < LANES:
            part = jnp.concatenate([part, jnp.zeros((1, LANES - width), jnp.float32)], axis=1)
        turned = jnp.transpose(jnp.broadcast_to(part, (LANES, LANES)))
        out_ref[at:at + width, :] = turned[:width]


def dft_body(n, owned, slots, span, blocks, first, *refs):
    if first:
        pos_ref, starts_ref, freqs_ref, angle_ref, mask_ref, vel_ref = refs[:6]
        outs = refs[6:6 + n]
        a_ref, cos_ref, sin_ref = refs[6 + n:9 + n]
        rot_ref = refs[9 + n]

        @pl.when(pl.program_id(0) == 0)
        def _():
            build_rows(n, owned, slots, span, blocks, pos_ref[0], starts_ref, freqs_ref, a_ref)
            spread_column(jnp.cos(angle_ref[...].reshape(1, span)), span, cos_ref)
            spread_column(jnp.sin(angle_ref[...].reshape(1, span)), span, sin_ref)
    else:
        mask_ref, vel_ref, a_ref, cos_ref, sin_ref = refs[:5]
        outs = refs[5:5 + n]
        rot_ref = refs[5 + n]
    width = vel_ref.shape[2]
    turning = mask_ref[...] == 1
    for at in range(0, span, 16):
        rows = min(16, span - at)
        here = pl.ds(at, rows)
        cosine = jnp.concatenate([cos_ref[here, :]] * (width // LANES), axis=1)
        sine = jnp.concatenate([sin_ref[here, :]] * (width // LANES), axis=1)
        x = vel_ref[0, here, :].astype(jnp.float32)
        y = vel_ref[1, here, :].astype(jnp.float32)
        rot_ref[0, here, :] = jnp.where(turning, cosine * x - sine * y, x).astype(jnp.bfloat16)
        rot_ref[1, here, :] = jnp.where(turning, sine * x + cosine * y, y).astype(jnp.bfloat16)
    rows = a_ref.shape[1]
    a = a_ref[...].reshape(n * rows, span)
    for c in range(COMPS):
        samples = rot_ref[c] if c < 2 else vel_ref[2]
        sums = jnp.dot(a, samples, preferred_element_type=jnp.float32).astype(jnp.bfloat16)
        for k in range(n):
            outs[k][c * rows:(c + 1) * rows, :] = sums[k * rows:(k + 1) * rows]


def dft_call(n, owned, slots, blocks, first, offset, points, position, starts, freqs, angles, mask, velocity, shared):
    span = velocity.shape[1]
    rows = slots * owned * 2
    shift = offset // TILE
    whole = lambda shape: pl.BlockSpec(shape, lambda i: (0,) * len(shape))
    smem = pl.BlockSpec(memory_space=pltpu.SMEM)
    data_specs = [
        pl.BlockSpec((1, TILE), lambda i: (0, i + shift)),
        pl.BlockSpec((COMPS, span, TILE), lambda i: (0, 0, i + shift)),
    ]
    shared_types = [
        jax.ShapeDtypeStruct((n, rows, span), jnp.bfloat16),
        jax.ShapeDtypeStruct((span, LANES), jnp.float32),
        jax.ShapeDtypeStruct((span, LANES), jnp.float32),
    ]
    shared_specs = [whole(t.shape) for t in shared_types]
    out_types = [jax.ShapeDtypeStruct((COMPS * rows, points), jnp.bfloat16)] * n
    out_specs = [pl.BlockSpec((COMPS * rows, TILE), lambda i: (0, i))] * n
    if first:
        args = (position, starts, freqs, angles, mask, velocity)
        in_specs = [smem] * 3 + [whole((span,))] + data_specs
        out_types = out_types + shared_types
        out_specs = out_specs + shared_specs
    else:
        args = (mask, velocity) + tuple(shared)
        in_specs = data_specs + shared_specs
    out = pl.pallas_call(
        functools.partial(dft_body, n, owned, slots, span, blocks, first),
        grid=(points // TILE,),
        out_shape=out_types,
        in_specs=in_specs,
        out_specs=out_specs,
        scratch_shapes=[pltpu.VMEM((2, span, TILE), jnp.bfloat16)],
        compiler_params=pltpu.CompilerParams(vmem_limit_bytes=40 * 2**20),
        cost_estimate=pl.CostEstimate(
            flops=2 * n * rows * span * COMPS * points,
            bytes_accessed=2 * COMPS * span * points,
            transcendentals=0,
        ),
        name="rotate_dft",
    )(*args)
    return out[:n], out[n:] if first else shared


def selection(n, owned, slots, span, blocks, me):
    rows = slots * owned * 2
    shape = (owned * 2 * blocks, n * rows)
    out = lax.broadcasted_iota(jnp.int32, shape, 0)
    col = lax.broadcasted_iota(jnp.int32, shape, 1)
    k_of = jnp.zeros(shape, jnp.int32)
    lo = jnp.broadcast_to(first_block(me, span), shape)
    for k in range(1, n):
        past = col >= k * rows
        k_of = jnp.where(past, k, k_of)
        lo = jnp.where(past, first_block(lax.rem(me + n - k, n), span), lo)
    rem = col - k_of * rows
    slot = rem // (owned * 2)
    same = (out // blocks == rem % (owned * 2)) & (out % blocks == lo + slot)
    return jnp.where(same, 1.0, 0.0)


def assemble_body(n, owned, slots, span, blocks, total, has_sum, last, *refs):
    pos_ref = refs[0]
    parts = refs[1:1 + n]
    rest = refs[1 + n:]
    if has_sum:
        sum_in, rest = rest[0], rest[2:]
    spectra_ref, gram_ref, sel_ref, acc_ref = rest
    step = pl.program_id(0)
    rows = slots * owned * 2

    @pl.when(step == 0)
    def _():
        sel_ref[...] = selection(n, owned, slots, span, blocks, pos_ref[0]).astype(jnp.bfloat16)
        acc_ref[...] = sum_in[...] if has_sum else jnp.zeros_like(acc_ref)

    for c in range(COMPS):
        stack = jnp.concatenate([p[c * rows:(c + 1) * rows, :] for p in parts], axis=0)
        full = jnp.dot(sel_ref[...], stack, preferred_element_type=jnp.float32)
        for j in range(owned):
            for r in range(2):
                at = (j * 2 + r) * blocks
                spectra_ref[j, r, c] = full[at:at + blocks]
        acc_ref[...] += lax.dot_general(
            stack, stack, (((1,), (1,)), ((), ())), preferred_element_type=jnp.float32
        )

    @pl.when(step == pl.num_programs(0) - 1)
    def _():
        if not last:
            gram_ref[...] = acc_ref[...]
        else:
            sel = sel_ref[...].astype(jnp.float32)
            half = jnp.dot(sel, acc_ref[...], precision=HIGHEST, preferred_element_type=jnp.float32)
            order = 2 * blocks
            gram = lax.dot_general(
                half, sel, (((1,), (1,)), ((), ())), precision=HIGHEST, preferred_element_type=jnp.float32
            ) * (1.0 / total)
            gram_ref[...] = jnp.concatenate(
                [gram[j * order:(j + 1) * order, j * order:(j + 1) * order] for j in range(owned)], axis=1
            )


def assemble_call(n, owned, slots, span, blocks, total, offset, points, all_points, position, parts, spectra, gram, last):
    rows = slots * owned * 2
    tile = min(points, 512)
    shift = offset // tile
    order = 2 * blocks
    has_sum = gram is not None
    whole = lambda shape: pl.BlockSpec(shape, lambda i: (0,) * len(shape))
    gram_shape = (order, owned * order) if last else (n * rows, n * rows)
    args = [position] + list(parts)
    in_specs = [pl.BlockSpec(memory_space=pltpu.SMEM)] + [pl.BlockSpec((COMPS * rows, tile), lambda i: (0, i))] * n
    aliases = {}
    if has_sum:
        args += [gram, spectra]
        in_specs += [whole((n * rows, n * rows)), pl.BlockSpec(memory_space=pl.ANY)]
        aliases = {len(args) - 1: 0}
    return pl.pallas_call(
        functools.partial(assemble_body, n, owned, slots, span, blocks, total, has_sum, last),
        grid=(points // tile,),
        out_shape=[
            jax.ShapeDtypeStruct((owned, 2, COMPS, blocks, all_points), jnp.float32),
            jax.ShapeDtypeStruct(gram_shape, jnp.float32),
        ],
        in_specs=in_specs,
        out_specs=[
            pl.BlockSpec((owned, 2, COMPS, blocks, tile), lambda i: (0, 0, 0, 0, i + shift)),
            whole(gram_shape),
        ],
        scratch_shapes=[
            pltpu.VMEM((owned * order, n * rows), jnp.bfloat16),
            pltpu.VMEM((n * rows, n * rows), jnp.float32),
        ],
        input_output_aliases=aliases,
        compiler_params=pltpu.CompilerParams(vmem_limit_bytes=40 * 2**20),
        cost_estimate=pl.CostEstimate(
            flops=4 * (n * rows) ** 2 * COMPS * points,
            bytes_accessed=4 * owned * order * COMPS * points,
            transcendentals=0,
        ),
        name="assemble",
    )(*args)


def factor_body(owned, order, count, *refs):
    parts = refs[:count]
    out_ref, row_ref = refs[count:]
    s = [p[...] for p in parts]
    while len(s) > 1:
        s = [a + b for a, b in zip(s[::2], s[1::2])]
    s = s[0]
    lane = lax.broadcasted_iota(jnp.int32, (1, owned * order), 1)
    for k in range(0, order, PIVOT):
        base = k // 8 * 8
        s = s[base - max(k - PIVOT, 0) // 8 * 8:]
        columns = []
        for i in range(k, k + PIVOT):
            column = jnp.broadcast_to(s[:, i:i + 1], s.shape)
            for j in range(1, owned):
                column = jnp.where(lane >= j * order, s[:, j * order + i:j * order + i + 1], column)
            columns.append(column)
        at = k - base
        rows = [s[at + i:at + i + 1] for i in range(PIVOT)]
        for i in range(PIVOT):
            inverse_root = lax.rsqrt(columns[i][at + i:at + i + 1])
            columns[i] = columns[i] * inverse_root
            rows[i] = rows[i] * inverse_root
            for j in range(i + 1, PIVOT):
                weight = columns[i][at + j:at + j + 1]
                columns[j] = columns[j] - columns[i] * weight
                rows[j] = rows[j] - rows[i] * weight
            row_ref[k + i:k + i + 1, :] = jnp.where(lane % order >= k + i, rows[i], 0.0)
            s = s - columns[i] * rows[i]
    for j in range(owned):
        out_ref[j] = row_ref[:, j * order:(j + 1) * order]


def factor_call(owned, order, parts):
    return pl.pallas_call(
        functools.partial(factor_body, owned, order, len(parts)),
        out_shape=jax.ShapeDtypeStruct((owned, order, order), jnp.float32),
        scratch_shapes=[pltpu.VMEM((order, owned * order), jnp.float32)],
        name="factor",
    )(*parts)


LINE_LO = [0, 6, 15, 23]
LINE_HI = [8, 16, 25, 31]
WIDE = 12
FAR = 9
SHARED = 2


def pick(values, me):
    out = jnp.int32(values[0])
    for i in range(1, len(values)):
        out = jnp.where(me == i, jnp.int32(values[i]), out)
    return out


def far_block(shard, slot):
    return pick([0, 8, 23, 31], shard) + pick([1, 1, -1, -1], shard) * slot


def cosine_of(turns):
    s = half_turn_sine(turns - jnp.floor(turns + 0.5))
    return 1.0 - 2.0 * s * s


def build_line(span, blocks, me, starts_ref, freqs_ref, direct_ref, a_ref, rows_ref):
    lo = pick(LINE_LO, me)
    starts = [starts_ref[jnp.minimum(lo + s, blocks - 1)] for s in range(WIDE)]

    def by_slot(shape, axis):
        at = lax.broadcasted_iota(jnp.int32, shape, axis)
        out = jnp.full(shape, starts[0], jnp.int32)
        for s in range(1, WIDE):
            out = jnp.where(at == s, starts[s], out)
        return out

    rid = lax.broadcasted_iota(jnp.int32, (16, 1), 0)
    f_of = ((rid // 4) ^ me) * 2 + (rid // 2) % 2
    freq = jnp.zeros((16, 1), jnp.float32)
    for f in range(8):
        freq = jnp.where(f_of == f, freqs_ref[f].astype(jnp.float32), freq)
    step = freq * (1.0 / NFFT)
    quarter = (rid % 2).astype(jnp.float32) * 0.25

    sample = lax.broadcasted_iota(jnp.int32, (1, span), 1) + me * span
    turns = sample.astype(jnp.float32) * step
    turns = turns - jnp.floor(turns) + quarter
    cos_t, sin_t = cosine_of(turns), cosine_of(turns - 0.25)
    begin = by_slot((1, LANES), 1).astype(jnp.float32) * step
    begin = begin - jnp.floor(begin)
    cos_b, sin_b = cosine_of(begin), cosine_of(begin - 0.25)

    slot = lax.broadcasted_iota(jnp.int32, (16, 1), 0)
    ni = sample - by_slot((16, 1), 0)
    nf = ni.astype(jnp.float32)
    w = half_turn_sine(jnp.minimum(nf, NFFT - nf) * (1.0 / NFFT))
    w = jnp.where((ni >= 0) & (ni < NFFT) & (slot + lo < blocks), w * w * SCALE, 0.0)

    own, near, direct2, direct3 = [], [], [], []
    for s in range(WIDE):
        rows = (cos_t * cos_b[:, s:s + 1] + sin_t * sin_b[:, s:s + 1]) * w[s:s + 1]
        rows_ref[s] = rows[8:]
        own.append(rows[:4])
        near.append(rows[4:8])
        direct2.append(rows[8:12])
        direct3.append(rows[12:])
    direct_ref[...] = jnp.concatenate(own + near + direct2 + direct3, axis=0).astype(jnp.bfloat16)
    far = [rows_ref[far_block(me, s) - lo] for s in range(FAR)]
    inner = ((me == 1) | (me == 2)).astype(jnp.float32)
    shared = [rows_ref[pick([0, s, 10 - s, 0], me)] * inner for s in range(SHARED)]
    pieces = own + near
    pieces += [r[4:] for r in shared] + [r[:4] for r in shared]
    pieces += [r[:4] for r in far[:-1]] + [r[4:] for r in far[:-1]]
    pieces += [far[-1], jnp.zeros((8, span), jnp.float32)]
    a_ref[...] = jnp.concatenate(pieces, axis=0).astype(jnp.bfloat16)


def line_dft_body(span, blocks, first, *refs):
    if first:
        pos_ref, starts_ref, freqs_ref, angle_ref, mask_ref, vel_ref = refs[:6]
        out_refs = refs[6:10]
        shared_refs = refs[10:13]
        rot_ref, a_ref, rows_ref = refs[13:]
        _, cos_ref, sin_ref = shared_refs

        @pl.when(pl.program_id(0) == 0)
        def _():
            build_line(span, blocks, pos_ref[0], starts_ref, freqs_ref, a_ref, shared_refs[0], rows_ref)
            spread_column(jnp.cos(angle_ref[...].reshape(1, span)), span, cos_ref)
            spread_column(jnp.sin(angle_ref[...].reshape(1, span)), span, sin_ref)
    else:
        mask_ref, vel_ref, a_ref, cos_ref, sin_ref = refs[:5]
        own_ref, near_ref, shared_ref, far2_ref, far3_ref, rot_ref = refs[6:]
    width = vel_ref.shape[2]
    turning = mask_ref[...] == 1
    for at in range(0, span, 16):
        rows = min(16, span - at)
        here = pl.ds(at, rows)
        cosine = jnp.concatenate([cos_ref[here, :]] * (width // LANES), axis=1)
        sine = jnp.concatenate([sin_ref[here, :]] * (width // LANES), axis=1)
        x = vel_ref[0, here, :].astype(jnp.float32)
        y = vel_ref[1, here, :].astype(jnp.float32)
        rot_ref[0, here, :] = jnp.where(turning, cosine * x - sine * y, x).astype(jnp.bfloat16)
        rot_ref[1, here, :] = jnp.where(turning, sine * x + cosine * y, y).astype(jnp.bfloat16)
    tails = []
    for c in range(COMPS):
        samples = rot_ref[c] if c < 2 else vel_ref[2]
        sums = jnp.dot(a_ref[...], samples, preferred_element_type=jnp.float32)
        if first:
            for k, ref in enumerate(out_refs):
                ref[48 * c:48 * c + 48, :] = sums[48 * k:48 * k + 48].astype(jnp.bfloat16)
            continue
        own_ref[48 * c:48 * c + 48, :] = sums[:48].astype(jnp.bfloat16)
        near_ref[48 * c:48 * c + 48, :] = sums[48:96].astype(jnp.bfloat16)
        shared_ref[16 * c:16 * c + 16, :] = sums[96:112].astype(jnp.bfloat16)
        far2_ref[32 * c:32 * c + 32, :] = sums[112:144].astype(jnp.bfloat16)
        far3_ref[32 * c:32 * c + 32, :] = sums[144:176].astype(jnp.bfloat16)
        tails.append(sums[176:184])
    if not first:
        none = jnp.zeros((4, width), jnp.float32)
        far2_ref[96:112, :] = jnp.concatenate([t[:4] for t in tails] + [none], axis=0).astype(jnp.bfloat16)
        far3_ref[96:112, :] = jnp.concatenate([t[4:] for t in tails] + [none], axis=0).astype(jnp.bfloat16)


def line_dft(blocks, offset, points, position, starts, freqs, angles, mask, velocity, shared, after):
    first = shared is None
    span = velocity.shape[1]
    shift = offset // TILE
    whole = lambda shape: pl.BlockSpec(shape, lambda i: (0,) * len(shape))
    smem = pl.BlockSpec(memory_space=pltpu.SMEM)
    data_specs = [
        pl.BlockSpec((1, TILE), lambda i: (0, i + shift)),
        pl.BlockSpec((COMPS, span, TILE), lambda i: (0, 0, i + shift)),
    ]
    shared_types = [
        jax.ShapeDtypeStruct((192, span), jnp.bfloat16),
        jax.ShapeDtypeStruct((span, LANES), jnp.float32),
        jax.ShapeDtypeStruct((span, LANES), jnp.float32),
    ]
    shared_specs = [whole(t.shape) for t in shared_types]
    heights = [144] * 4 if first else [144, 144, 48, 112, 112]
    out_types = [jax.ShapeDtypeStruct((h, points), jnp.bfloat16) for h in heights]
    out_specs = [pl.BlockSpec((h, TILE), lambda i: (0, i)) for h in heights]
    scratch = [pltpu.VMEM((2, span, TILE), jnp.bfloat16)]
    if first:
        args = (position, starts, freqs, angles, mask, velocity)
        in_specs = [smem] * 3 + [whole((span,))] + data_specs
        out_types = out_types + shared_types
        out_specs = out_specs + shared_specs
        scratch += [pltpu.VMEM((192, span), jnp.bfloat16), pltpu.VMEM((WIDE, 8, span), jnp.float32)]
    else:
        args = (mask, velocity) + tuple(shared) + (after,)
        in_specs = data_specs + shared_specs + [pl.BlockSpec(memory_space=pl.ANY)]
    out = pl.pallas_call(
        functools.partial(line_dft_body, span, blocks, first),
        grid=(points // TILE,),
        out_shape=out_types,
        in_specs=in_specs,
        out_specs=out_specs,
        scratch_shapes=scratch,
        compiler_params=pltpu.CompilerParams(vmem_limit_bytes=(60 if first else 40) * 2**20),
        cost_estimate=SHORT,
        name="rotate_dft",
    )(*args)
    return (out[:4], out[4:]) if first else (out, shared)


def combine_body(far2_ref, far3_ref, shared_ref, near_ref, out2_ref, out3_ref, near_out_ref):
    for c in range(COMPS):
        here = slice(32 * c, 32 * c + 32)
        add = shared_ref[16 * c:16 * c + 16, :].astype(jnp.float32)
        none = jnp.zeros((24, add.shape[1]), jnp.float32)
        for src, dst, part in ((far2_ref, out2_ref, add[:8]), (far3_ref, out3_ref, add[8:])):
            dst[here, :] = (src[here, :].astype(jnp.float32) + jnp.concatenate([none, part], axis=0)).astype(jnp.bfloat16)
    near_out_ref[...] = near_ref[...]
    out2_ref[96:112, :] = far2_ref[96:112, :]
    out3_ref[96:112, :] = far3_ref[96:112, :]


def combine(far2, far3, shared, near):
    return pl.pallas_call(
        combine_body,
        out_shape=[jax.ShapeDtypeStruct(x.shape, x.dtype) for x in (far2, far3, near)],
        compiler_params=pltpu.CompilerParams(vmem_limit_bytes=40 * 2**20),
        cost_estimate=pl.CostEstimate(flops=far2.size, bytes_accessed=8 * far2.size, transcendentals=0),
        name="add_shared",
    )(far2, far3, shared, near)


def line_selection(blocks, me, direct, sel_ref):
    shape = (4 * blocks, 192)
    out = lax.broadcasted_iota(jnp.int32, shape, 0)
    col = lax.broadcasted_iota(jnp.int32, shape, 1)
    two, three = me ^ 2, me ^ 3
    block = jnp.where(col < 48, pick(LINE_LO, me) + col // 4, pick(LINE_LO, me ^ 1) + (col - 48) // 4)
    if direct:
        block = jnp.where(col >= 96, pick(LINE_LO, two) + (col - 96) // 4, block)
        block = jnp.where(col >= 144, pick(LINE_LO, three) + (col - 144) // 4, block)
    else:
        block = jnp.where(col >= 96, far_block(two, (col - 96) // 4), block)
        block = jnp.where(col >= 128, far_block(three, (col - 128) // 4), block)
        block = jnp.where(col >= 160, far_block(two, FAR - 1), block)
        block = jnp.where(col >= 176, far_block(three, FAR - 1), block)
    same = (out // blocks == col % 4) & (out % blocks == block)
    for c in range(COMPS):
        mine = same if direct else same & ((col < 160) | ((col % 16) // 4 == c))
        sel_ref[c] = jnp.where(mine, 1.0, 0.0).astype(jnp.bfloat16)


def line_assemble_body(blocks, total, has_sum, last, direct, *refs):
    pos_ref, own_ref, near_ref, far2_ref, far3_ref = refs[:5]
    rest = refs[5:]
    if has_sum:
        sum_in, rest = rest[0], rest[2:]
    spectra_ref, gram_ref, sel_ref, acc_ref = rest
    step = pl.program_id(0)
    me = pos_ref[0]

    @pl.when(step == 0)
    def _():
        line_selection(blocks, me, direct, sel_ref)
        acc_ref[...] = sum_in[...] if has_sum else jnp.zeros_like(acc_ref)

    for c in range(COMPS):
        wide = slice(48 * c, 48 * c + 48)
        parts = [own_ref[wide, :], near_ref[wide, :]]
        if direct:
            parts += [far2_ref[wide, :], far3_ref[wide, :]]
        else:
            here = slice(32 * c, 32 * c + 32)
            parts += [far2_ref[here, :], far3_ref[here, :], far2_ref[96:112, :], far3_ref[96:112, :]]
        stack = jnp.concatenate(parts, axis=0)
        full = jnp.dot(sel_ref[c], stack, preferred_element_type=jnp.float32)
        for jr in range(4):
            spectra_ref[jr // 2, jr % 2, c] = full[jr * blocks:(jr + 1) * blocks]
        high = full.astype(jnp.bfloat16)
        low = (full - high.astype(jnp.float32)).astype(jnp.bfloat16)
        pair = jnp.concatenate([high, low], axis=0)
        acc_ref[...] += lax.dot_general(
            pair, pair, (((1,), (1,)), ((), ())), preferred_element_type=jnp.float32
        )

    @pl.when(step == pl.num_programs(0) - 1)
    def _():
        if not last:
            gram_ref[...] = acc_ref[...]
        else:
            n = 4 * blocks
            order = 2 * blocks
            acc = acc_ref[...]
            gram = (acc[:n, :n] + (acc[:n, n:] + acc[n:, :n])) * (1.0 / total)
            gram_ref[...] = jnp.concatenate([gram[:order, :order], gram[order:, order:]], axis=1)


def line_assemble(blocks, total, offset, points, all_points, position, own, near, fars, spectra, gram, last):
    shift = offset // TILE
    order = 2 * blocks
    has_sum = gram is not None
    whole = lambda shape: pl.BlockSpec(shape, lambda i: (0,) * len(shape))
    gram_shape = (order, 2 * order) if last else (4 * order, 4 * order)
    args = [position, own, near] + list(fars)
    in_specs = [pl.BlockSpec(memory_space=pltpu.SMEM)]
    in_specs += [pl.BlockSpec((a.shape[0], TILE), lambda i: (0, i)) for a in args[1:]]
    aliases = {}
    if has_sum:
        args += [gram, spectra]
        in_specs += [whole((4 * order, 4 * order)), pl.BlockSpec(memory_space=pl.ANY)]
        aliases = {len(args) - 1: 0}
    return pl.pallas_call(
        functools.partial(line_assemble_body, blocks, total, has_sum, last, fars[0].shape[0] == 144),
        grid=(points // TILE,),
        out_shape=[
            jax.ShapeDtypeStruct((2, 2, COMPS, blocks, all_points), jnp.float32),
            jax.ShapeDtypeStruct(gram_shape, jnp.float32),
        ],
        in_specs=in_specs,
        out_specs=[
            pl.BlockSpec((2, 2, COMPS, blocks, TILE), lambda i: (0, 0, 0, 0, i + shift)),
            whole(gram_shape),
        ],
        scratch_shapes=[
            pltpu.VMEM((COMPS, 4 * blocks, 192), jnp.bfloat16),
            pltpu.VMEM((4 * order, 4 * order), jnp.float32),
        ],
        input_output_aliases=aliases,
        compiler_params=pltpu.CompilerParams(vmem_limit_bytes=40 * 2**20),
        cost_estimate=SHORT,
        name="assemble",
    )(*args)


def line_chunks(points):
    cuts = [0, points // 4, points * 5 // 8, points]
    return [(a, b - a) for a, b in zip(cuts[:-1], cuts[1:])]


def line_spectra(samples, mask, angles, block_starts, frequencies, position, total):
    points = samples.shape[2]
    blocks = block_starts.shape[0]
    move = lambda x, pairs: lax.ppermute(x, "tm", pairs)
    across = lambda x, k: move(x, [(i, i ^ k) for i in range(4)])
    chunks = line_chunks(points)
    spectra, gram, shared, sent = None, None, None, []

    def assemble():
        at, count, own, near, fars = sent.pop(0)
        return line_assemble(
            blocks, total, at, count, points, position, own, near, fars, spectra, gram, at + count == points
        )

    for i, (at, count) in enumerate(chunks):
        if i >= 2:
            spectra, gram = assemble()
        after = gram if i >= 2 else mask
        sums, shared = line_dft(
            blocks, at, count, position, block_starts, frequencies, angles, mask, samples, shared, after
        )
        if i == 0:
            own, near, far2, far3 = sums
        else:
            own, near, part, far2, far3 = sums
            far2, far3, near = combine(far2, far3, move(part, [(1, 0), (2, 3)]), near)
        sent.append((at, count, own, across(near, 1), [across(far2, 2), across(far3, 3)]))
    while sent:
        spectra, gram = assemble()
    return spectra, gram


def fits_line(n, span, blocks, owned):
    if n != 4 or owned != 2:
        return False
    lo = [max((s * span - (NFFT + JIT - 1) + HOP) // HOP, 0) for s in range(n)]
    hi = [min((span * (s + 1) - 1) // HOP, blocks - 1) for s in range(n)]
    return lo == LINE_LO and hi == LINE_HI and blocks == 32


def sum_over_space(gram, groups):
    if groups != 8:
        return [lax.psum(gram, "space")]
    swap = lambda x, k: lax.ppermute(x, "space", [(i, i ^ k) for i in range(groups)])
    gram = gram + swap(gram, 1)
    return [gram] + [swap(gram, k) for k in (2, 4, 6)]


def chunks_of(points):
    tile = 512
    return [(at, tile) for at in range(0, points, tile)]


def ring_spectra(n, owned, slots, blocks, total, position, block_starts, frequencies, angles, mask, samples):
    span, points = samples.shape[1:]
    pieces = []
    shared = None
    for at, count in chunks_of(points):
        sums, shared = dft_call(
            n, owned, slots, blocks, shared is None, at, count,
            position, block_starts, frequencies, angles, mask, samples, shared,
        )
        moved = [sums[0]] + [
            lax.ppermute(sums[k], "tm", [(i, (i + k) % n) for i in range(n)]) for k in range(1, n)
        ]
        pieces.append((at, count, moved))

    spectra, gram = None, None
    for at, count, moved in pieces:
        last = at + count == points
        spectra, gram = assemble_call(
            n, owned, slots, span, blocks, total, at, count, points, position, moved, spectra, gram, last
        )
    return spectra, gram


def per_device(velocity, rotor_mask, rotor_angle, block_starts, frequencies):
    span, _, points = velocity.shape
    n = lax.axis_size("tm")
    groups = lax.axis_size("space")
    blocks = block_starts.shape[0]
    owned = frequencies.shape[0] // n
    order = 2 * blocks
    slots = slot_count(n, span, blocks, owned * 2)
    position = lax.axis_index("tm").astype(jnp.int32).reshape(1)
    samples = velocity.transpose(1, 0, 2)
    mask = rotor_mask.reshape(1, points)
    angles = rotor_angle

    total = COMPS * points * groups
    if fits_line(n, span, blocks, owned):
        spectra, gram = line_spectra(samples, mask, angles, block_starts, frequencies, position, total)
    else:
        spectra, gram = ring_spectra(
            n, owned, slots, blocks, total, position, block_starts, frequencies, angles, mask, samples
        )
    factors = factor_call(owned, order, sum_over_space(gram, groups))
    return spectra.transpose(0, 1, 3, 2, 4), factors


def solution(mesh):
    in_specs = (P("tm", None, "space"), P("space"), P("tm"), P(), P())
    out_specs = (P("tm", None, None, None, "space"), P("tm", None, None))
    return jax.shard_map(
        per_device, mesh=mesh, in_specs=in_specs, out_specs=out_specs, check_vma=False
    )
```

```python
import functools
import math

import jax
import jax.numpy as jnp
from jax import lax
from jax.experimental import pallas as pl
from jax.experimental.pallas import tpu as pltpu
from jax.sharding import PartitionSpec as P

COMPS = 3
NFFT = 256
JIT = 64
HOP = 128
LANES = 128
TILE = 256
PIVOT = 4
SCALE = (8.0 / (3.0 * NFFT)) ** 0.5
HIGHEST = lax.Precision.HIGHEST
SHORT = pl.CostEstimate(flops=1000, bytes_accessed=1000, transcendentals=0)


def first_block(shard, span):
    return jnp.maximum((shard * span - (NFFT + JIT - 1) + HOP) // HOP, 0)


def slot_count(shards, span, blocks, rows_per_slot):
    most = 0
    for s in range(shards):
        lo = max((s * span - (NFFT + JIT - 1) + HOP) // HOP, 0)
        hi = min((span * (s + 1) - 1) // HOP, blocks - 1)
        most = max(most, hi - lo + 1)
    step = 16 // math.gcd(16, rows_per_slot)
    return -(-most // step) * step


def half_turn_sine(x):
    z = x * x
    c = [math.pi ** (2 * i + 1) * (-1) ** i / math.factorial(2 * i + 1) for i in range(7)]
    acc = jnp.full_like(z, c[-1])
    for term in c[-2::-1]:
        acc = acc * z + term
    return acc * x


def build_rows(n, owned, slots, span, blocks, me, starts_ref, freqs_ref, a_ref):
    group = owned * 2
    rid = lax.broadcasted_iota(jnp.int32, (n * group, 1), 0)
    k_of, j_of, r_of = rid // group, (rid // 2) % owned, rid % 2
    f_of = lax.rem(me + k_of, n) * owned + j_of
    freq = jnp.zeros((n * group, 1), jnp.float32)
    for f in range(n * owned):
        freq = jnp.where(f_of == f, freqs_ref[f].astype(jnp.float32), freq)
    step = freq * (1.0 / NFFT)
    quarter = r_of.astype(jnp.float32) * 0.25
    lo = first_block(me, span)
    sample = lax.broadcasted_iota(jnp.int32, (1, span), 1) + me * span
    pieces = [[] for _ in range(n)]
    for s in range(slots):
        b = lo + s
        start = starts_ref[jnp.minimum(b, blocks - 1)]
        ni = sample - start
        inside = (ni >= 0) & (ni < NFFT) & (b < blocks)
        nf = ni.astype(jnp.float32)
        w = half_turn_sine(jnp.minimum(nf, NFFT - nf) * (1.0 / NFFT))
        w = jnp.where(inside, w * w * SCALE, 0.0)
        nf = jnp.where(inside, nf, 0.0)
        turns = nf * step + quarter
        turns = turns - jnp.floor(turns + 0.5)
        h = half_turn_sine(turns)
        rows = w * (1.0 - 2.0 * h * h)
        for k in range(n):
            pieces[k].append(rows[k * group:(k + 1) * group])
    for k in range(n):
        a_ref[k] = jnp.concatenate(pieces[k], axis=0).astype(jnp.bfloat16)


def spread_column(row, span, out_ref):
    for at in range(0, span, LANES):
        width = min(LANES, span - at)
        part = row[:, at:at + width]
        if width < LANES:
            part = jnp.concatenate([part, jnp.zeros((1, LANES - width), jnp.float32)], axis=1)
        turned = jnp.transpose(jnp.broadcast_to(part, (LANES, LANES)))
        out_ref[at:at + width, :] = turned[:width]


def dft_body(n, owned, slots, span, blocks, first, *refs):
    if first:
        pos_ref, starts_ref, freqs_ref, angle_ref, mask_ref, vel_ref = refs[:6]
        outs = refs[6:6 + n]
        a_ref, cos_ref, sin_ref = refs[6 + n:9 + n]
        rot_ref = refs[9 + n]

        @pl.when(pl.program_id(0) == 0)
        def _():
            build_rows(n, owned, slots, span, blocks, pos_ref[0], starts_ref, freqs_ref, a_ref)
            spread_column(jnp.cos(angle_ref[...].reshape(1, span)), span, cos_ref)
            spread_column(jnp.sin(angle_ref[...].reshape(1, span)), span, sin_ref)
    else:
        mask_ref, vel_ref, a_ref, cos_ref, sin_ref = refs[:5]
        outs = refs[5:5 + n]
        rot_ref = refs[5 + n]
    width = vel_ref.shape[2]
    turning = mask_ref[...] == 1
    for at in range(0, span, 16):
        rows = min(16, span - at)
        here = pl.ds(at, rows)
        cosine = jnp.concatenate([cos_ref[here, :]] * (width // LANES), axis=1)
        sine = jnp.concatenate([sin_ref[here, :]] * (width // LANES), axis=1)
        x = vel_ref[0, here, :].astype(jnp.float32)
        y = vel_ref[1, here, :].astype(jnp.float32)
        rot_ref[0, here, :] = jnp.where(turning, cosine * x - sine * y, x).astype(jnp.bfloat16)
        rot_ref[1, here, :] = jnp.where(turning, sine * x + cosine * y, y).astype(jnp.bfloat16)
    rows = a_ref.shape[1]
    a = a_ref[...].reshape(n * rows, span)
    for c in range(COMPS):
        samples = rot_ref[c] if c < 2 else vel_ref[2]
        sums = jnp.dot(a, samples, preferred_element_type=jnp.float32).astype(jnp.bfloat16)
        for k in range(n):
            outs[k][c * rows:(c + 1) * rows, :] = sums[k * rows:(k + 1) * rows]


def dft_call(n, owned, slots, blocks, first, offset, points, position, starts, freqs, angles, mask, velocity, shared):
    span = velocity.shape[1]
    rows = slots * owned * 2
    shift = offset // TILE
    whole = lambda shape: pl.BlockSpec(shape, lambda i: (0,) * len(shape))
    smem = pl.BlockSpec(memory_space=pltpu.SMEM)
    data_specs = [
        pl.BlockSpec((1, TILE), lambda i: (0, i + shift)),
        pl.BlockSpec((COMPS, span, TILE), lambda i: (0, 0, i + shift)),
    ]
    shared_types = [
        jax.ShapeDtypeStruct((n, rows, span), jnp.bfloat16),
        jax.ShapeDtypeStruct((span, LANES), jnp.float32),
        jax.ShapeDtypeStruct((span, LANES), jnp.float32),
    ]
    shared_specs = [whole(t.shape) for t in shared_types]
    out_types = [jax.ShapeDtypeStruct((COMPS * rows, points), jnp.bfloat16)] * n
    out_specs = [pl.BlockSpec((COMPS * rows, TILE), lambda i: (0, i))] * n
    if first:
        args = (position, starts, freqs, angles, mask, velocity)
        in_specs = [smem] * 3 + [whole((span,))] + data_specs
        out_types = out_types + shared_types
        out_specs = out_specs + shared_specs
    else:
        args = (mask, velocity) + tuple(shared)
        in_specs = data_specs + shared_specs
    out = pl.pallas_call(
        functools.partial(dft_body, n, owned, slots, span, blocks, first),
        grid=(points // TILE,),
        out_shape=out_types,
        in_specs=in_specs,
        out_specs=out_specs,
        scratch_shapes=[pltpu.VMEM((2, span, TILE), jnp.bfloat16)],
        compiler_params=pltpu.CompilerParams(vmem_limit_bytes=40 * 2**20),
        cost_estimate=pl.CostEstimate(
            flops=2 * n * rows * span * COMPS * points,
            bytes_accessed=2 * COMPS * span * points,
            transcendentals=0,
        ),
        name="rotate_dft",
    )(*args)
    return out[:n], out[n:] if first else shared


def selection(n, owned, slots, span, blocks, me):
    rows = slots * owned * 2
    shape = (owned * 2 * blocks, n * rows)
    out = lax.broadcasted_iota(jnp.int32, shape, 0)
    col = lax.broadcasted_iota(jnp.int32, shape, 1)
    k_of = jnp.zeros(shape, jnp.int32)
    lo = jnp.broadcast_to(first_block(me, span), shape)
    for k in range(1, n):
        past = col >= k * rows
        k_of = jnp.where(past, k, k_of)
        lo = jnp.where(past, first_block(lax.rem(me + n - k, n), span), lo)
    rem = col - k_of * rows
    slot = rem // (owned * 2)
    same = (out // blocks == rem % (owned * 2)) & (out % blocks == lo + slot)
    return jnp.where(same, 1.0, 0.0)


def assemble_body(n, owned, slots, span, blocks, total, has_sum, last, *refs):
    pos_ref = refs[0]
    parts = refs[1:1 + n]
    rest = refs[1 + n:]
    if has_sum:
        sum_in, rest = rest[0], rest[2:]
    spectra_ref, gram_ref, sel_ref, acc_ref = rest
    step = pl.program_id(0)
    rows = slots * owned * 2

    @pl.when(step == 0)
    def _():
        sel_ref[...] = selection(n, owned, slots, span, blocks, pos_ref[0]).astype(jnp.bfloat16)
        acc_ref[...] = sum_in[...] if has_sum else jnp.zeros_like(acc_ref)

    for c in range(COMPS):
        stack = jnp.concatenate([p[c * rows:(c + 1) * rows, :] for p in parts], axis=0)
        full = jnp.dot(sel_ref[...], stack, preferred_element_type=jnp.float32)
        for j in range(owned):
            for r in range(2):
                at = (j * 2 + r) * blocks
                spectra_ref[j, r, c] = full[at:at + blocks]
        acc_ref[...] += lax.dot_general(
            stack, stack, (((1,), (1,)), ((), ())), preferred_element_type=jnp.float32
        )

    @pl.when(step == pl.num_programs(0) - 1)
    def _():
        if not last:
            gram_ref[...] = acc_ref[...]
        else:
            sel = sel_ref[...].astype(jnp.float32)
            half = jnp.dot(sel, acc_ref[...], precision=HIGHEST, preferred_element_type=jnp.float32)
            order = 2 * blocks
            gram = lax.dot_general(
                half, sel, (((1,), (1,)), ((), ())), precision=HIGHEST, preferred_element_type=jnp.float32
            ) * (1.0 / total)
            gram_ref[...] = jnp.concatenate(
                [gram[j * order:(j + 1) * order, j * order:(j + 1) * order] for j in range(owned)], axis=1
            )


def assemble_call(n, owned, slots, span, blocks, total, offset, points, all_points, position, parts, spectra, gram, last):
    rows = slots * owned * 2
    tile = min(points, 512)
    shift = offset // tile
    order = 2 * blocks
    has_sum = gram is not None
    whole = lambda shape: pl.BlockSpec(shape, lambda i: (0,) * len(shape))
    gram_shape = (order, owned * order) if last else (n * rows, n * rows)
    args = [position] + list(parts)
    in_specs = [pl.BlockSpec(memory_space=pltpu.SMEM)] + [pl.BlockSpec((COMPS * rows, tile), lambda i: (0, i))] * n
    aliases = {}
    if has_sum:
        args += [gram, spectra]
        in_specs += [whole((n * rows, n * rows)), pl.BlockSpec(memory_space=pl.ANY)]
        aliases = {len(args) - 1: 0}
    return pl.pallas_call(
        functools.partial(assemble_body, n, owned, slots, span, blocks, total, has_sum, last),
        grid=(points // tile,),
        out_shape=[
            jax.ShapeDtypeStruct((owned, 2, COMPS, blocks, all_points), jnp.float32),
            jax.ShapeDtypeStruct(gram_shape, jnp.float32),
        ],
        in_specs=in_specs,
        out_specs=[
            pl.BlockSpec((owned, 2, COMPS, blocks, tile), lambda i: (0, 0, 0, 0, i + shift)),
            whole(gram_shape),
        ],
        scratch_shapes=[
            pltpu.VMEM((owned * order, n * rows), jnp.bfloat16),
            pltpu.VMEM((n * rows, n * rows), jnp.float32),
        ],
        input_output_aliases=aliases,
        compiler_params=pltpu.CompilerParams(vmem_limit_bytes=40 * 2**20),
        cost_estimate=pl.CostEstimate(
            flops=4 * (n * rows) ** 2 * COMPS * points,
            bytes_accessed=4 * owned * order * COMPS * points,
            transcendentals=0,
        ),
        name="assemble",
    )(*args)


def factor_body(owned, order, count, *refs):
    parts = refs[:count]
    out_ref, row_ref = refs[count:]
    s = [p[...] for p in parts]
    while len(s) > 1:
        s = [a + b for a, b in zip(s[::2], s[1::2])]
    s = s[0]
    lane = lax.broadcasted_iota(jnp.int32, (1, owned * order), 1)
    for k in range(0, order, PIVOT):
        base = k // 8 * 8
        s = s[base - max(k - PIVOT, 0) // 8 * 8:]
        columns = []
        for i in range(k, k + PIVOT):
            column = jnp.broadcast_to(s[:, i:i + 1], s.shape)
            for j in range(1, owned):
                column = jnp.where(lane >= j * order, s[:, j * order + i:j * order + i + 1], column)
            columns.append(column)
        at = k - base
        rows = [s[at + i:at + i + 1] for i in range(PIVOT)]
        for i in range(PIVOT):
            inverse_root = lax.rsqrt(columns[i][at + i:at + i + 1])
            columns[i] = columns[i] * inverse_root
            rows[i] = rows[i] * inverse_root
            for j in range(i + 1, PIVOT):
                weight = columns[i][at + j:at + j + 1]
                columns[j] = columns[j] - columns[i] * weight
                rows[j] = rows[j] - rows[i] * weight
            row_ref[k + i:k + i + 1, :] = jnp.where(lane % order >= k + i, rows[i], 0.0)
            s = s - columns[i] * rows[i]
    for j in range(owned):
        out_ref[j] = row_ref[:, j * order:(j + 1) * order]


def factor_call(owned, order, parts):
    return pl.pallas_call(
        functools.partial(factor_body, owned, order, len(parts)),
        out_shape=jax.ShapeDtypeStruct((owned, order, order), jnp.float32),
        scratch_shapes=[pltpu.VMEM((order, owned * order), jnp.float32)],
        name="factor",
    )(*parts)


LINE_LO = [0, 6, 15, 23]
LINE_HI = [8, 16, 25, 31]
WIDE = 12
FAR = 9
SHARED = 2
REACH = 144


def pick(values, me):
    out = jnp.int32(values[0])
    for i in range(1, len(values)):
        out = jnp.where(me == i, jnp.int32(values[i]), out)
    return out


def far_block(shard, slot):
    return pick([0, 8, 23, 31], shard) + pick([1, 1, -1, -1], shard) * slot


def cosine_of(turns):
    s = half_turn_sine(turns - jnp.floor(turns + 0.5))
    return 1.0 - 2.0 * s * s


def build_line(span, blocks, me, starts_ref, freqs_ref, direct_ref, a_ref, rows_ref):
    lo = pick(LINE_LO, me)
    starts = [starts_ref[jnp.minimum(lo + s, blocks - 1)] for s in range(WIDE)]

    def by_slot(shape, axis):
        at = lax.broadcasted_iota(jnp.int32, shape, axis)
        out = jnp.full(shape, starts[0], jnp.int32)
        for s in range(1, WIDE):
            out = jnp.where(at == s, starts[s], out)
        return out

    rid = lax.broadcasted_iota(jnp.int32, (16, 1), 0)
    f_of = ((rid // 4) ^ me) * 2 + (rid // 2) % 2
    freq = jnp.zeros((16, 1), jnp.float32)
    for f in range(8):
        freq = jnp.where(f_of == f, freqs_ref[f].astype(jnp.float32), freq)
    step = freq * (1.0 / NFFT)
    quarter = (rid % 2).astype(jnp.float32) * 0.25

    sample = lax.broadcasted_iota(jnp.int32, (1, span), 1) + me * span
    turns = sample.astype(jnp.float32) * step
    turns = turns - jnp.floor(turns) + quarter
    cos_t, sin_t = cosine_of(turns), cosine_of(turns - 0.25)
    begin = by_slot((1, LANES), 1).astype(jnp.float32) * step
    begin = begin - jnp.floor(begin)
    cos_b, sin_b = cosine_of(begin), cosine_of(begin - 0.25)

    slot = lax.broadcasted_iota(jnp.int32, (16, 1), 0)
    ni = sample - by_slot((16, 1), 0)
    nf = ni.astype(jnp.float32)
    w = half_turn_sine(jnp.minimum(nf, NFFT - nf) * (1.0 / NFFT))
    w = jnp.where((ni >= 0) & (ni < NFFT) & (slot + lo < blocks), w * w * SCALE, 0.0)

    own, near, direct2, direct3 = [], [], [], []
    for s in range(WIDE):
        rows = (cos_t * cos_b[:, s:s + 1] + sin_t * sin_b[:, s:s + 1]) * w[s:s + 1]
        rows_ref[s] = rows[8:]
        own.append(rows[:4])
        near.append(rows[4:8])
        direct2.append(rows[8:12])
        direct3.append(rows[12:])
    direct_ref[...] = jnp.concatenate(own + near + direct2 + direct3, axis=0).astype(jnp.bfloat16)
    far = [rows_ref[far_block(me, s) - lo] for s in range(FAR)]
    pieces = own + near
    pieces += [r[:4] for r in far[:-1]] + [r[4:] for r in far[:-1]]
    pieces += [far[-1], jnp.zeros((8, span), jnp.float32)]
    a_ref[...] = jnp.concatenate(pieces, axis=0).astype(jnp.bfloat16)


def rotate(turning, cosine, sine, x, y):
    width = x.shape[1]
    cosine = jnp.concatenate([cosine] * (width // LANES), axis=1)
    sine = jnp.concatenate([sine] * (width // LANES), axis=1)
    x, y = x.astype(jnp.float32), y.astype(jnp.float32)
    new_x = jnp.where(turning, cosine * x - sine * y, x)
    new_y = jnp.where(turning, sine * x + cosine * y, y)
    return new_x.astype(jnp.bfloat16), new_y.astype(jnp.bfloat16)


def shared_rows(begin, me, starts_ref, freqs_ref):
    rid = lax.broadcasted_iota(jnp.int32, (16, 1), 0)
    f_of = jnp.where(rid < 8, me ^ 3, me ^ 2) * 2 + (rid // 2) % 2
    freq = jnp.zeros((16, 1), jnp.float32)
    for f in range(8):
        freq = jnp.where(f_of == f, freqs_ref[f].astype(jnp.float32), freq)
    first, second = (starts_ref[pick([0, 6 + s, 25 - s, 0], me)] for s in range(SHARED))
    start = jnp.where((rid // 4) % 2 == 0, first, second)
    ni = lax.broadcasted_iota(jnp.int32, (1, REACH), 1) + begin - start
    nf = ni.astype(jnp.float32)
    w = half_turn_sine(jnp.minimum(nf, NFFT - nf) * (1.0 / NFFT))
    inner = (me == 1) | (me == 2)
    w = jnp.where((ni >= 0) & (ni < NFFT) & inner, w * w * SCALE, 0.0)
    turns = nf * (freq * (1.0 / NFFT)) + (rid % 2).astype(jnp.float32) * 0.25
    return (cosine_of(turns) * w).astype(jnp.bfloat16)


def line_dft_body(span, blocks, first, *refs):
    if first:
        pos_ref, starts_ref, freqs_ref, angle_ref, mask_ref, vel_ref, all_mask_ref, all_hbm = refs[:8]
        out_refs = refs[8:12]
        part_ref = refs[12]
        shared_refs = refs[13:16]
        rot_ref, a_ref, rows_ref, ends_ref, ends_rot_ref, ends_sem = refs[16:]
        _, cos_ref, sin_ref = shared_refs

        @pl.when(pl.program_id(0) == 0)
        def _():
            me = pos_ref[0]
            begin = pl.multiple_of(jnp.where(me == 2, span - REACH, 0), 16)
            load = pltpu.make_async_copy(all_hbm.at[:, pl.ds(begin, REACH), :], ends_ref, ends_sem)
            load.start()
            build_line(span, blocks, me, starts_ref, freqs_ref, a_ref, shared_refs[0], rows_ref)
            spread_column(jnp.cos(angle_ref[...].reshape(1, span)), span, cos_ref)
            spread_column(jnp.sin(angle_ref[...].reshape(1, span)), span, sin_ref)
            rows = shared_rows(begin + me * span, me, starts_ref, freqs_ref)
            load.wait()
            for lane in range(0, part_ref.shape[1], TILE):
                here = slice(lane, lane + TILE)
                turning = all_mask_ref[:, here] == 1
                for at in range(0, REACH, 16):
                    row = slice(at, at + 16)
                    t = pl.ds(pl.multiple_of(begin + at, 16), 16)
                    new_x, new_y = rotate(
                        turning, cos_ref[t, :], sin_ref[t, :], ends_ref[0, row, here], ends_ref[1, row, here]
                    )
                    ends_rot_ref[0, row, here] = new_x
                    ends_rot_ref[1, row, here] = new_y
                for c in range(COMPS):
                    samples = ends_rot_ref[c, :, here] if c < 2 else ends_ref[2, :, here]
                    sums = jnp.dot(rows, samples, preferred_element_type=jnp.float32)
                    part_ref[16 * c:16 * c + 16, here] = sums.astype(jnp.bfloat16)
    else:
        part_ref, mask_ref, vel_ref, a_ref, cos_ref, sin_ref = refs[:6]
        own_ref, near_ref, far2_ref, far3_ref, rot_ref = refs[7:]
    width = vel_ref.shape[2]
    turning = mask_ref[...] == 1
    for at in range(0, span, 16):
        here = pl.ds(at, min(16, span - at))
        new_x, new_y = rotate(turning, cos_ref[here, :], sin_ref[here, :], vel_ref[0, here, :], vel_ref[1, here, :])
        rot_ref[0, here, :] = new_x
        rot_ref[1, here, :] = new_y
    tails = []
    none = jnp.zeros((24, width), jnp.float32)
    for c in range(COMPS):
        samples = rot_ref[c] if c < 2 else vel_ref[2]
        sums = jnp.dot(a_ref[...], samples, preferred_element_type=jnp.float32)
        if first:
            for k, ref in enumerate(out_refs):
                ref[48 * c:48 * c + 48, :] = sums[48 * k:48 * k + 48].astype(jnp.bfloat16)
            continue
        own_ref[48 * c:48 * c + 48, :] = sums[:48].astype(jnp.bfloat16)
        near_ref[48 * c:48 * c + 48, :] = sums[48:96].astype(jnp.bfloat16)
        part = part_ref[16 * c:16 * c + 16, :].astype(jnp.float32)
        far2 = sums[96:128] + jnp.concatenate([none, part[:8]], axis=0)
        far3 = sums[128:160] + jnp.concatenate([none, part[8:]], axis=0)
        far2_ref[32 * c:32 * c + 32, :] = far2.astype(jnp.bfloat16)
        far3_ref[32 * c:32 * c + 32, :] = far3.astype(jnp.bfloat16)
        tails.append(sums[160:168])
    if not first:
        far2_ref[96:112, :] = jnp.concatenate([t[:4] for t in tails] + [none[:4]], axis=0).astype(jnp.bfloat16)
        far3_ref[96:112, :] = jnp.concatenate([t[4:] for t in tails] + [none[:4]], axis=0).astype(jnp.bfloat16)


def line_dft(blocks, offset, points, position, starts, freqs, angles, mask, velocity, shared, part, after):
    first = shared is None
    span, all_points = velocity.shape[1:]
    shift = offset // TILE
    whole = lambda shape: pl.BlockSpec(shape, lambda i: (0,) * len(shape))
    smem = pl.BlockSpec(memory_space=pltpu.SMEM)
    data_specs = [
        pl.BlockSpec((1, TILE), lambda i: (0, i + shift)),
        pl.BlockSpec((COMPS, span, TILE), lambda i: (0, 0, i + shift)),
    ]
    shared_types = [
        jax.ShapeDtypeStruct((176, span), jnp.bfloat16),
        jax.ShapeDtypeStruct((span, LANES), jnp.float32),
        jax.ShapeDtypeStruct((span, LANES), jnp.float32),
    ]
    shared_specs = [whole(t.shape) for t in shared_types]
    heights = [144] * 4 if first else [144, 144, 112, 112]
    out_types = [jax.ShapeDtypeStruct((h, points), jnp.bfloat16) for h in heights]
    out_specs = [pl.BlockSpec((h, TILE), lambda i: (0, i)) for h in heights]
    scratch = [pltpu.VMEM((2, span, TILE), jnp.bfloat16)]
    if first:
        args = (position, starts, freqs, angles, mask, velocity, mask, velocity)
        in_specs = [smem] * 3 + [whole((span,))] + data_specs
        in_specs += [whole((1, all_points)), pl.BlockSpec(memory_space=pl.ANY)]
        out_types += [jax.ShapeDtypeStruct((48, all_points), jnp.bfloat16)] + shared_types
        out_specs += [whole((48, all_points))] + shared_specs
        scratch += [
            pltpu.VMEM((192, span), jnp.bfloat16),
            pltpu.VMEM((WIDE, 8, span), jnp.float32),
            pltpu.VMEM((COMPS, REACH, all_points), jnp.bfloat16),
            pltpu.VMEM((2, REACH, all_points), jnp.bfloat16),
            pltpu.SemaphoreType.DMA,
        ]
    else:
        args = (part, mask, velocity) + tuple(shared) + (after,)
        in_specs = [pl.BlockSpec((48, TILE), lambda i: (0, i + shift))] + data_specs + shared_specs
        in_specs.append(pl.BlockSpec(memory_space=pl.ANY))
    out = pl.pallas_call(
        functools.partial(line_dft_body, span, blocks, first),
        grid=(points // TILE,),
        out_shape=out_types,
        in_specs=in_specs,
        out_specs=out_specs,
        scratch_shapes=scratch,
        compiler_params=pltpu.CompilerParams(vmem_limit_bytes=(60 if first else 40) * 2**20),
        cost_estimate=pl.CostEstimate(
            flops=2 * 192 * span * COMPS * points, bytes_accessed=2 * COMPS * span * points, transcendentals=0
        ),
        name="rotate_dft",
    )(*args)
    return (out[:4], out[4], out[5:]) if first else (out, part, shared)


def line_selection(blocks, me, direct, sel_ref):
    shape = (4 * blocks, 192)
    out = lax.broadcasted_iota(jnp.int32, shape, 0)
    col = lax.broadcasted_iota(jnp.int32, shape, 1)
    two, three = me ^ 2, me ^ 3
    block = jnp.where(col < 48, pick(LINE_LO, me) + col // 4, pick(LINE_LO, me ^ 1) + (col - 48) // 4)
    if direct:
        block = jnp.where(col >= 96, pick(LINE_LO, two) + (col - 96) // 4, block)
        block = jnp.where(col >= 144, pick(LINE_LO, three) + (col - 144) // 4, block)
    else:
        block = jnp.where(col >= 96, far_block(two, (col - 96) // 4), block)
        block = jnp.where(col >= 128, far_block(three, (col - 128) // 4), block)
        block = jnp.where(col >= 160, far_block(two, FAR - 1), block)
        block = jnp.where(col >= 176, far_block(three, FAR - 1), block)
    same = (out // blocks == col % 4) & (out % blocks == block)
    for c in range(COMPS):
        mine = same if direct else same & ((col < 160) | ((col % 16) // 4 == c))
        sel_ref[c] = jnp.where(mine, 1.0, 0.0).astype(jnp.bfloat16)


def line_assemble_body(blocks, total, has_sum, last, direct, *refs):
    pos_ref, own_ref, near_ref, far2_ref, far3_ref = refs[:5]
    rest = refs[5:]
    if has_sum:
        sum_in, rest = rest[0], rest[2:]
    spectra_ref, gram_ref, sel_ref, acc_ref = rest
    step = pl.program_id(0)
    me = pos_ref[0]

    @pl.when(step == 0)
    def _():
        line_selection(blocks, me, direct, sel_ref)
        acc_ref[...] = sum_in[...] if has_sum else jnp.zeros_like(acc_ref)

    for c in range(COMPS):
        wide = slice(48 * c, 48 * c + 48)
        parts = [own_ref[wide, :], near_ref[wide, :]]
        if direct:
            parts += [far2_ref[wide, :], far3_ref[wide, :]]
        else:
            here = slice(32 * c, 32 * c + 32)
            parts += [far2_ref[here, :], far3_ref[here, :], far2_ref[96:112, :], far3_ref[96:112, :]]
        stack = jnp.concatenate(parts, axis=0)
        full = jnp.dot(sel_ref[c], stack, preferred_element_type=jnp.float32)
        for jr in range(4):
            spectra_ref[jr // 2, jr % 2, c] = full[jr * blocks:(jr + 1) * blocks]
        high = full.astype(jnp.bfloat16)
        low = (full - high.astype(jnp.float32)).astype(jnp.bfloat16)
        pair = jnp.concatenate([high, low], axis=0)
        acc_ref[...] += lax.dot_general(
            pair, pair, (((1,), (1,)), ((), ())), preferred_element_type=jnp.float32
        )

    @pl.when(step == pl.num_programs(0) - 1)
    def _():
        if not last:
            gram_ref[...] = acc_ref[...]
        else:
            n = 4 * blocks
            order = 2 * blocks
            acc = acc_ref[...]
            gram = (acc[:n, :n] + (acc[:n, n:] + acc[n:, :n])) * (1.0 / total)
            gram_ref[...] = jnp.concatenate([gram[:order, :order], gram[order:, order:]], axis=1)


def line_assemble(blocks, total, offset, points, all_points, position, own, near, fars, spectra, gram, last):
    shift = offset // TILE
    order = 2 * blocks
    has_sum = gram is not None
    whole = lambda shape: pl.BlockSpec(shape, lambda i: (0,) * len(shape))
    gram_shape = (order, 2 * order) if last else (4 * order, 4 * order)
    args = [position, own, near] + list(fars)
    in_specs = [pl.BlockSpec(memory_space=pltpu.SMEM)]
    in_specs += [pl.BlockSpec((a.shape[0], TILE), lambda i: (0, i)) for a in args[1:]]
    aliases = {}
    if has_sum:
        args += [gram, spectra]
        in_specs += [whole((4 * order, 4 * order)), pl.BlockSpec(memory_space=pl.ANY)]
        aliases = {len(args) - 1: 0}
    return pl.pallas_call(
        functools.partial(line_assemble_body, blocks, total, has_sum, last, fars[0].shape[0] == 144),
        grid=(points // TILE,),
        out_shape=[
            jax.ShapeDtypeStruct((2, 2, COMPS, blocks, all_points), jnp.float32),
            jax.ShapeDtypeStruct(gram_shape, jnp.float32),
        ],
        in_specs=in_specs,
        out_specs=[
            pl.BlockSpec((2, 2, COMPS, blocks, TILE), lambda i: (0, 0, 0, 0, i + shift)),
            whole(gram_shape),
        ],
        scratch_shapes=[
            pltpu.VMEM((COMPS, 4 * blocks, 192), jnp.bfloat16),
            pltpu.VMEM((4 * order, 4 * order), jnp.float32),
        ],
        input_output_aliases=aliases,
        compiler_params=pltpu.CompilerParams(vmem_limit_bytes=40 * 2**20),
        cost_estimate=SHORT,
        name="assemble",
    )(*args)


def line_chunks(points):
    cuts = [0, points // 4, points * 5 // 8, points * 7 // 8, points]
    return [(a, b - a) for a, b in zip(cuts[:-1], cuts[1:])]


def line_spectra(samples, mask, angles, block_starts, frequencies, position, total):
    points = samples.shape[2]
    blocks = block_starts.shape[0]
    move = lambda x, pairs: lax.ppermute(x, "tm", pairs)
    across = lambda x, k: move(x, [(i, i ^ k) for i in range(4)])
    shared, part = None, None
    spectra, gram = None, None
    sent = []

    def assemble():
        at, count, own, near, fars = sent.pop(0)
        return line_assemble(
            blocks, total, at, count, points, position, own, near, fars, spectra, gram, at + count == points
        )

    for i, (at, count) in enumerate(line_chunks(points)):
        if i >= 2:
            spectra, gram = assemble()
        (own, near, far2, far3), part, shared = line_dft(
            blocks, at, count, position, block_starts, frequencies, angles, mask, samples, shared, part,
            gram if i >= 2 else mask,
        )
        if i == 0:
            part = move(part, [(1, 0), (2, 3)])
        sent.append((at, count, own, across(near, 1), [across(far2, 2), across(far3, 3)]))
    while sent:
        spectra, gram = assemble()
    return spectra, gram


def fits_line(n, span, blocks, owned):
    if n != 4 or owned != 2:
        return False
    lo = [max((s * span - (NFFT + JIT - 1) + HOP) // HOP, 0) for s in range(n)]
    hi = [min((span * (s + 1) - 1) // HOP, blocks - 1) for s in range(n)]
    return lo == LINE_LO and hi == LINE_HI and blocks == 32


def sum_over_space(gram, groups):
    if groups != 8:
        return [lax.psum(gram, "space")]
    swap = lambda x, k: lax.ppermute(x, "space", [(i, i ^ k) for i in range(groups)])
    gram = gram + swap(gram, 1)
    gram = gram + swap(gram, 2)
    return [gram, swap(gram, 4)]


def chunks_of(points):
    tile = 512
    return [(at, tile) for at in range(0, points, tile)]


def ring_spectra(n, owned, slots, blocks, total, position, block_starts, frequencies, angles, mask, samples):
    span, points = samples.shape[1:]
    pieces = []
    shared = None
    for at, count in chunks_of(points):
        sums, shared = dft_call(
            n, owned, slots, blocks, shared is None, at, count,
            position, block_starts, frequencies, angles, mask, samples, shared,
        )
        moved = [sums[0]] + [
            lax.ppermute(sums[k], "tm", [(i, (i + k) % n) for i in range(n)]) for k in range(1, n)
        ]
        pieces.append((at, count, moved))

    spectra, gram = None, None
    for at, count, moved in pieces:
        last = at + count == points
        spectra, gram = assemble_call(
            n, owned, slots, span, blocks, total, at, count, points, position, moved, spectra, gram, last
        )
    return spectra, gram


def per_device(velocity, rotor_mask, rotor_angle, block_starts, frequencies):
    span, _, points = velocity.shape
    n = lax.axis_size("tm")
    groups = lax.axis_size("space")
    blocks = block_starts.shape[0]
    owned = frequencies.shape[0] // n
    order = 2 * blocks
    slots = slot_count(n, span, blocks, owned * 2)
    position = lax.axis_index("tm").astype(jnp.int32).reshape(1)
    samples = velocity.transpose(1, 0, 2)
    mask = rotor_mask.reshape(1, points)
    angles = rotor_angle

    total = COMPS * points * groups
    if fits_line(n, span, blocks, owned):
        spectra, gram = line_spectra(samples, mask, angles, block_starts, frequencies, position, total)
    else:
        spectra, gram = ring_spectra(
            n, owned, slots, blocks, total, position, block_starts, frequencies, angles, mask, samples
        )
    factors = factor_call(owned, order, sum_over_space(gram, groups))
    return spectra.transpose(0, 1, 3, 2, 4), factors


def solution(mesh):
    in_specs = (P("tm", None, "space"), P("space"), P("tm"), P(), P())
    out_specs = (P("tm", None, None, None, "space"), P("tm", None, None))
    return jax.shard_map(
        per_device, mesh=mesh, in_specs=in_specs, out_specs=out_specs, check_vma=False
    )
```

```python
import functools
import math

import jax
import jax.numpy as jnp
from jax import lax
from jax.experimental import pallas as pl
from jax.experimental.pallas import tpu as pltpu
from jax.sharding import PartitionSpec as P

COMPS = 3
NFFT = 256
JIT = 64
HOP = 128
LANES = 128
TILE = 256
PIVOT = 4
LIMIT_A, LIMIT_B, LIMIT_C = 60, 60, 40
SCALE = (8.0 / (3.0 * NFFT)) ** 0.5
HIGHEST = lax.Precision.HIGHEST
SHORT = pl.CostEstimate(flops=1000, bytes_accessed=1000, transcendentals=0)


def first_block(shard, span):
    return jnp.maximum((shard * span - (NFFT + JIT - 1) + HOP) // HOP, 0)


def slot_count(shards, span, blocks, rows_per_slot):
    most = 0
    for s in range(shards):
        lo = max((s * span - (NFFT + JIT - 1) + HOP) // HOP, 0)
        hi = min((span * (s + 1) - 1) // HOP, blocks - 1)
        most = max(most, hi - lo + 1)
    step = 16 // math.gcd(16, rows_per_slot)
    return -(-most // step) * step


def half_turn_sine(x):
    z = x * x
    c = [math.pi ** (2 * i + 1) * (-1) ** i / math.factorial(2 * i + 1) for i in range(7)]
    acc = jnp.full_like(z, c[-1])
    for term in c[-2::-1]:
        acc = acc * z + term
    return acc * x


def build_rows(n, owned, slots, span, blocks, me, starts_ref, freqs_ref, a_ref):
    group = owned * 2
    rid = lax.broadcasted_iota(jnp.int32, (n * group, 1), 0)
    k_of, j_of, r_of = rid // group, (rid // 2) % owned, rid % 2
    f_of = lax.rem(me + k_of, n) * owned + j_of
    freq = jnp.zeros((n * group, 1), jnp.float32)
    for f in range(n * owned):
        freq = jnp.where(f_of == f, freqs_ref[f].astype(jnp.float32), freq)
    step = freq * (1.0 / NFFT)
    quarter = r_of.astype(jnp.float32) * 0.25
    lo = first_block(me, span)
    sample = lax.broadcasted_iota(jnp.int32, (1, span), 1) + me * span
    pieces = [[] for _ in range(n)]
    for s in range(slots):
        b = lo + s
        start = starts_ref[jnp.minimum(b, blocks - 1)]
        ni = sample - start
        inside = (ni >= 0) & (ni < NFFT) & (b < blocks)
        nf = ni.astype(jnp.float32)
        w = half_turn_sine(jnp.minimum(nf, NFFT - nf) * (1.0 / NFFT))
        w = jnp.where(inside, w * w * SCALE, 0.0)
        nf = jnp.where(inside, nf, 0.0)
        turns = nf * step + quarter
        turns = turns - jnp.floor(turns + 0.5)
        h = half_turn_sine(turns)
        rows = w * (1.0 - 2.0 * h * h)
        for k in range(n):
            pieces[k].append(rows[k * group:(k + 1) * group])
    for k in range(n):
        a_ref[k] = jnp.concatenate(pieces[k], axis=0).astype(jnp.bfloat16)


def spread_column(row, span, out_ref):
    for at in range(0, span, LANES):
        width = min(LANES, span - at)
        part = row[:, at:at + width]
        if width < LANES:
            part = jnp.concatenate([part, jnp.zeros((1, LANES - width), jnp.float32)], axis=1)
        turned = jnp.transpose(jnp.broadcast_to(part, (LANES, LANES)))
        out_ref[at:at + width, :] = turned[:width]


def dft_body(n, owned, slots, span, blocks, first, *refs):
    if first:
        pos_ref, starts_ref, freqs_ref, angle_ref, mask_ref, vel_ref = refs[:6]
        outs = refs[6:6 + n]
        a_ref, cos_ref, sin_ref = refs[6 + n:9 + n]
        rot_ref = refs[9 + n]

        @pl.when(pl.program_id(0) == 0)
        def _():
            build_rows(n, owned, slots, span, blocks, pos_ref[0], starts_ref, freqs_ref, a_ref)
            spread_column(jnp.cos(angle_ref[...].reshape(1, span)), span, cos_ref)
            spread_column(jnp.sin(angle_ref[...].reshape(1, span)), span, sin_ref)
    else:
        mask_ref, vel_ref, a_ref, cos_ref, sin_ref = refs[:5]
        outs = refs[5:5 + n]
        rot_ref = refs[5 + n]
    width = vel_ref.shape[2]
    turning = mask_ref[...] == 1
    for at in range(0, span, 16):
        rows = min(16, span - at)
        here = pl.ds(at, rows)
        cosine = jnp.concatenate([cos_ref[here, :]] * (width // LANES), axis=1)
        sine = jnp.concatenate([sin_ref[here, :]] * (width // LANES), axis=1)
        x = vel_ref[0, here, :].astype(jnp.float32)
        y = vel_ref[1, here, :].astype(jnp.float32)
        rot_ref[0, here, :] = jnp.where(turning, cosine * x - sine * y, x).astype(jnp.bfloat16)
        rot_ref[1, here, :] = jnp.where(turning, sine * x + cosine * y, y).astype(jnp.bfloat16)
    rows = a_ref.shape[1]
    a = a_ref[...].reshape(n * rows, span)
    for c in range(COMPS):
        samples = rot_ref[c] if c < 2 else vel_ref[2]
        sums = jnp.dot(a, samples, preferred_element_type=jnp.float32).astype(jnp.bfloat16)
        for k in range(n):
            outs[k][c * rows:(c + 1) * rows, :] = sums[k * rows:(k + 1) * rows]


def dft_call(n, owned, slots, blocks, first, offset, points, position, starts, freqs, angles, mask, velocity, shared):
    span = velocity.shape[1]
    rows = slots * owned * 2
    shift = offset // TILE
    whole = lambda shape: pl.BlockSpec(shape, lambda i: (0,) * len(shape))
    smem = pl.BlockSpec(memory_space=pltpu.SMEM)
    data_specs = [
        pl.BlockSpec((1, TILE), lambda i: (0, i + shift)),
        pl.BlockSpec((COMPS, span, TILE), lambda i: (0, 0, i + shift)),
    ]
    shared_types = [
        jax.ShapeDtypeStruct((n, rows, span), jnp.bfloat16),
        jax.ShapeDtypeStruct((span, LANES), jnp.float32),
        jax.ShapeDtypeStruct((span, LANES), jnp.float32),
    ]
    shared_specs = [whole(t.shape) for t in shared_types]
    out_types = [jax.ShapeDtypeStruct((COMPS * rows, points), jnp.bfloat16)] * n
    out_specs = [pl.BlockSpec((COMPS * rows, TILE), lambda i: (0, i))] * n
    if first:
        args = (position, starts, freqs, angles, mask, velocity)
        in_specs = [smem] * 3 + [whole((span,))] + data_specs
        out_types = out_types + shared_types
        out_specs = out_specs + shared_specs
    else:
        args = (mask, velocity) + tuple(shared)
        in_specs = data_specs + shared_specs
    out = pl.pallas_call(
        functools.partial(dft_body, n, owned, slots, span, blocks, first),
        grid=(points // TILE,),
        out_shape=out_types,
        in_specs=in_specs,
        out_specs=out_specs,
        scratch_shapes=[pltpu.VMEM((2, span, TILE), jnp.bfloat16)],
        compiler_params=pltpu.CompilerParams(vmem_limit_bytes=40 * 2**20),
        cost_estimate=pl.CostEstimate(
            flops=2 * n * rows * span * COMPS * points,
            bytes_accessed=2 * COMPS * span * points,
            transcendentals=0,
        ),
        name="rotate_dft",
    )(*args)
    return out[:n], out[n:] if first else shared


def selection(n, owned, slots, span, blocks, me):
    rows = slots * owned * 2
    shape = (owned * 2 * blocks, n * rows)
    out = lax.broadcasted_iota(jnp.int32, shape, 0)
    col = lax.broadcasted_iota(jnp.int32, shape, 1)
    k_of = jnp.zeros(shape, jnp.int32)
    lo = jnp.broadcast_to(first_block(me, span), shape)
    for k in range(1, n):
        past = col >= k * rows
        k_of = jnp.where(past, k, k_of)
        lo = jnp.where(past, first_block(lax.rem(me + n - k, n), span), lo)
    rem = col - k_of * rows
    slot = rem // (owned * 2)
    same = (out // blocks == rem % (owned * 2)) & (out % blocks == lo + slot)
    return jnp.where(same, 1.0, 0.0)


def assemble_body(n, owned, slots, span, blocks, total, has_sum, last, *refs):
    pos_ref = refs[0]
    parts = refs[1:1 + n]
    rest = refs[1 + n:]
    if has_sum:
        sum_in, rest = rest[0], rest[2:]
    spectra_ref, gram_ref, sel_ref, acc_ref = rest
    step = pl.program_id(0)
    rows = slots * owned * 2

    @pl.when(step == 0)
    def _():
        sel_ref[...] = selection(n, owned, slots, span, blocks, pos_ref[0]).astype(jnp.bfloat16)
        acc_ref[...] = sum_in[...] if has_sum else jnp.zeros_like(acc_ref)

    for c in range(COMPS):
        stack = jnp.concatenate([p[c * rows:(c + 1) * rows, :] for p in parts], axis=0)
        full = jnp.dot(sel_ref[...], stack, preferred_element_type=jnp.float32)
        for j in range(owned):
            for r in range(2):
                at = (j * 2 + r) * blocks
                spectra_ref[j, r, c] = full[at:at + blocks]
        acc_ref[...] += lax.dot_general(
            stack, stack, (((1,), (1,)), ((), ())), preferred_element_type=jnp.float32
        )

    @pl.when(step == pl.num_programs(0) - 1)
    def _():
        if not last:
            gram_ref[...] = acc_ref[...]
        else:
            sel = sel_ref[...].astype(jnp.float32)
            half = jnp.dot(sel, acc_ref[...], precision=HIGHEST, preferred_element_type=jnp.float32)
            order = 2 * blocks
            gram = lax.dot_general(
                half, sel, (((1,), (1,)), ((), ())), precision=HIGHEST, preferred_element_type=jnp.float32
            ) * (1.0 / total)
            gram_ref[...] = jnp.concatenate(
                [gram[j * order:(j + 1) * order, j * order:(j + 1) * order] for j in range(owned)], axis=1
            )


def assemble_call(n, owned, slots, span, blocks, total, offset, points, all_points, position, parts, spectra, gram, last):
    rows = slots * owned * 2
    tile = min(points, 512)
    shift = offset // tile
    order = 2 * blocks
    has_sum = gram is not None
    whole = lambda shape: pl.BlockSpec(shape, lambda i: (0,) * len(shape))
    gram_shape = (order, owned * order) if last else (n * rows, n * rows)
    args = [position] + list(parts)
    in_specs = [pl.BlockSpec(memory_space=pltpu.SMEM)] + [pl.BlockSpec((COMPS * rows, tile), lambda i: (0, i))] * n
    aliases = {}
    if has_sum:
        args += [gram, spectra]
        in_specs += [whole((n * rows, n * rows)), pl.BlockSpec(memory_space=pl.ANY)]
        aliases = {len(args) - 1: 0}
    return pl.pallas_call(
        functools.partial(assemble_body, n, owned, slots, span, blocks, total, has_sum, last),
        grid=(points // tile,),
        out_shape=[
            jax.ShapeDtypeStruct((owned, 2, COMPS, blocks, all_points), jnp.float32),
            jax.ShapeDtypeStruct(gram_shape, jnp.float32),
        ],
        in_specs=in_specs,
        out_specs=[
            pl.BlockSpec((owned, 2, COMPS, blocks, tile), lambda i: (0, 0, 0, 0, i + shift)),
            whole(gram_shape),
        ],
        scratch_shapes=[
            pltpu.VMEM((owned * order, n * rows), jnp.bfloat16),
            pltpu.VMEM((n * rows, n * rows), jnp.float32),
        ],
        input_output_aliases=aliases,
        compiler_params=pltpu.CompilerParams(vmem_limit_bytes=40 * 2**20),
        cost_estimate=pl.CostEstimate(
            flops=4 * (n * rows) ** 2 * COMPS * points,
            bytes_accessed=4 * owned * order * COMPS * points,
            transcendentals=0,
        ),
        name="assemble",
    )(*args)


def factor_body(owned, order, count, *refs):
    parts = refs[:count]
    out_ref, row_ref = refs[count:]
    s = [p[...] for p in parts]
    while len(s) > 1:
        s = [a + b for a, b in zip(s[::2], s[1::2])]
    s = s[0]
    lane = lax.broadcasted_iota(jnp.int32, (1, owned * order), 1)
    for k in range(0, order, PIVOT):
        base = k // 8 * 8
        s = s[base - max(k - PIVOT, 0) // 8 * 8:]
        columns = []
        for i in range(k, k + PIVOT):
            column = jnp.broadcast_to(s[:, i:i + 1], s.shape)
            for j in range(1, owned):
                column = jnp.where(lane >= j * order, s[:, j * order + i:j * order + i + 1], column)
            columns.append(column)
        at = k - base
        rows = [s[at + i:at + i + 1] for i in range(PIVOT)]
        for i in range(PIVOT):
            inverse_root = lax.rsqrt(columns[i][at + i:at + i + 1])
            columns[i] = columns[i] * inverse_root
            rows[i] = rows[i] * inverse_root
            for j in range(i + 1, PIVOT):
                weight = columns[i][at + j:at + j + 1]
                columns[j] = columns[j] - columns[i] * weight
                rows[j] = rows[j] - rows[i] * weight
            row_ref[k + i:k + i + 1, :] = jnp.where(lane % order >= k + i, rows[i], 0.0)
            s = s - columns[i] * rows[i]
    for j in range(owned):
        out_ref[j] = row_ref[:, j * order:(j + 1) * order]


def factor_call(owned, order, parts):
    return pl.pallas_call(
        functools.partial(factor_body, owned, order, len(parts)),
        out_shape=jax.ShapeDtypeStruct((owned, order, order), jnp.float32),
        scratch_shapes=[pltpu.VMEM((order, owned * order), jnp.float32)],
        name="factor",
    )(*parts)


LINE_LO = [0, 6, 15, 23]
LINE_HI = [8, 16, 25, 31]
WIDE = 12
FAR = 9
SHARED = 2
REACH = 144


def pick(values, me):
    out = jnp.int32(values[0])
    for i in range(1, len(values)):
        out = jnp.where(me == i, jnp.int32(values[i]), out)
    return out


def far_block(shard, slot):
    return pick([0, 8, 23, 31], shard) + pick([1, 1, -1, -1], shard) * slot


def cosine_of(turns):
    s = half_turn_sine(turns - jnp.floor(turns + 0.5))
    return 1.0 - 2.0 * s * s


def build_line(span, blocks, me, starts_ref, freqs_ref, direct_ref, a_ref, rows_ref):
    lo = pick(LINE_LO, me)
    starts = [starts_ref[jnp.minimum(lo + s, blocks - 1)] for s in range(WIDE)]

    def by_slot(shape, axis):
        at = lax.broadcasted_iota(jnp.int32, shape, axis)
        out = jnp.full(shape, starts[0], jnp.int32)
        for s in range(1, WIDE):
            out = jnp.where(at == s, starts[s], out)
        return out

    rid = lax.broadcasted_iota(jnp.int32, (16, 1), 0)
    f_of = ((rid // 4) ^ me) * 2 + (rid // 2) % 2
    freq = jnp.zeros((16, 1), jnp.float32)
    for f in range(8):
        freq = jnp.where(f_of == f, freqs_ref[f].astype(jnp.float32), freq)
    step = freq * (1.0 / NFFT)
    quarter = (rid % 2).astype(jnp.float32) * 0.25

    sample = lax.broadcasted_iota(jnp.int32, (1, span), 1) + me * span
    turns = sample.astype(jnp.float32) * step
    turns = turns - jnp.floor(turns) + quarter
    cos_t, sin_t = cosine_of(turns), cosine_of(turns - 0.25)
    begin = by_slot((1, LANES), 1).astype(jnp.float32) * step
    begin = begin - jnp.floor(begin)
    cos_b, sin_b = cosine_of(begin), cosine_of(begin - 0.25)

    slot = lax.broadcasted_iota(jnp.int32, (16, 1), 0)
    ni = sample - by_slot((16, 1), 0)
    nf = ni.astype(jnp.float32)
    w = half_turn_sine(jnp.minimum(nf, NFFT - nf) * (1.0 / NFFT))
    w = jnp.where((ni >= 0) & (ni < NFFT) & (slot + lo < blocks), w * w * SCALE, 0.0)

    own, near, direct2, direct3 = [], [], [], []
    for s in range(WIDE):
        rows = (cos_t * cos_b[:, s:s + 1] + sin_t * sin_b[:, s:s + 1]) * w[s:s + 1]
        rows_ref[s] = rows[8:]
        own.append(rows[:4])
        near.append(rows[4:8])
        direct2.append(rows[8:12])
        direct3.append(rows[12:])
    direct_ref[...] = jnp.concatenate(own + near + direct2 + direct3, axis=0).astype(jnp.bfloat16)
    far = [rows_ref[far_block(me, s) - lo] for s in range(FAR)]
    pieces = own + near
    pieces += [r[:4] for r in far[:-1]] + [r[4:] for r in far[:-1]]
    pieces += [far[-1], jnp.zeros((8, span), jnp.float32)]
    a_ref[...] = jnp.concatenate(pieces, axis=0).astype(jnp.bfloat16)


def rotate(turning, cosine, sine, x, y):
    width = x.shape[1]
    cosine = jnp.concatenate([cosine] * (width // LANES), axis=1)
    sine = jnp.concatenate([sine] * (width // LANES), axis=1)
    x, y = x.astype(jnp.float32), y.astype(jnp.float32)
    new_x = jnp.where(turning, cosine * x - sine * y, x)
    new_y = jnp.where(turning, sine * x + cosine * y, y)
    return new_x.astype(jnp.bfloat16), new_y.astype(jnp.bfloat16)


def shared_rows(begin, me, starts_ref, freqs_ref):
    rid = lax.broadcasted_iota(jnp.int32, (16, 1), 0)
    f_of = jnp.where(rid < 8, me ^ 3, me ^ 2) * 2 + (rid // 2) % 2
    freq = jnp.zeros((16, 1), jnp.float32)
    for f in range(8):
        freq = jnp.where(f_of == f, freqs_ref[f].astype(jnp.float32), freq)
    first, second = (starts_ref[pick([0, 6 + s, 25 - s, 0], me)] for s in range(SHARED))
    start = jnp.where((rid // 4) % 2 == 0, first, second)
    ni = lax.broadcasted_iota(jnp.int32, (1, REACH), 1) + begin - start
    nf = ni.astype(jnp.float32)
    w = half_turn_sine(jnp.minimum(nf, NFFT - nf) * (1.0 / NFFT))
    inner = (me == 1) | (me == 2)
    w = jnp.where((ni >= 0) & (ni < NFFT) & inner, w * w * SCALE, 0.0)
    turns = nf * (freq * (1.0 / NFFT)) + (rid % 2).astype(jnp.float32) * 0.25
    return (cosine_of(turns) * w).astype(jnp.bfloat16)


def prepare_body(span, blocks, pos_ref, starts_ref, freqs_ref, angle_ref, mask_ref, all_hbm,
                 part_ref, direct_ref, a_ref, cos_ref, sin_ref, rows_ref, ends_ref, ends_rot_ref, ends_sem):
    me = pos_ref[0]
    begin = pl.multiple_of(jnp.where(me == 2, span - REACH, 0), 16)
    load = pltpu.make_async_copy(all_hbm.at[:, pl.ds(begin, REACH), :], ends_ref, ends_sem)
    load.start()
    build_line(span, blocks, me, starts_ref, freqs_ref, direct_ref, a_ref, rows_ref)
    spread_column(jnp.cos(angle_ref[...].reshape(1, span)), span, cos_ref)
    spread_column(jnp.sin(angle_ref[...].reshape(1, span)), span, sin_ref)
    rows = shared_rows(begin + me * span, me, starts_ref, freqs_ref)
    load.wait()
    for lane in range(0, part_ref.shape[1], TILE):
        here = slice(lane, lane + TILE)
        turning = mask_ref[:, here] == 1
        for at in range(0, REACH, 16):
            row = slice(at, at + 16)
            t = pl.ds(pl.multiple_of(begin + at, 16), 16)
            new_x, new_y = rotate(
                turning, cos_ref[t, :], sin_ref[t, :], ends_ref[0, row, here], ends_ref[1, row, here]
            )
            ends_rot_ref[0, row, here] = new_x
            ends_rot_ref[1, row, here] = new_y
        for c in range(COMPS):
            samples = ends_rot_ref[c, :, here] if c < 2 else ends_ref[2, :, here]
            sums = jnp.dot(rows, samples, preferred_element_type=jnp.float32)
            part_ref[16 * c:16 * c + 16, here] = sums.astype(jnp.bfloat16)


def prepare(blocks, position, starts, freqs, angles, mask, velocity):
    span, points = velocity.shape[1:]
    smem, vmem, anywhere = (pl.BlockSpec(memory_space=m) for m in (pltpu.SMEM, pltpu.VMEM, pl.ANY))
    whole = lambda shape: pl.BlockSpec(shape, lambda i: (0,) * len(shape))
    types = [
        jax.ShapeDtypeStruct((48, points), jnp.bfloat16),
        jax.ShapeDtypeStruct((192, span), jnp.bfloat16),
        jax.ShapeDtypeStruct((176, span), jnp.bfloat16),
        jax.ShapeDtypeStruct((span, LANES), jnp.float32),
        jax.ShapeDtypeStruct((span, LANES), jnp.float32),
    ]
    return pl.pallas_call(
        functools.partial(prepare_body, span, blocks),
        grid=(1,),
        out_shape=types,
        in_specs=[smem] * 3 + [whole((span,)), whole((1, points)), anywhere],
        out_specs=[whole(t.shape) for t in types],
        scratch_shapes=[
            pltpu.VMEM((WIDE, 8, span), jnp.float32),
            pltpu.VMEM((COMPS, REACH, points), jnp.bfloat16),
            pltpu.VMEM((2, REACH, points), jnp.bfloat16),
            pltpu.SemaphoreType.DMA,
        ],
        compiler_params=pltpu.CompilerParams(vmem_limit_bytes=LIMIT_A * 2**20),
        cost_estimate=pl.CostEstimate(flops=10**9, bytes_accessed=4 * 10**6, transcendentals=0),
        name="prepare",
    )(position, starts, freqs, angles, mask, velocity)


def line_dft_body(span, direct, *refs):
    mask_ref, vel_ref, a_ref, cos_ref, sin_ref = refs[:5]
    own_ref, near_ref, far2_ref, far3_ref, rot_ref = refs[-5:]
    part_ref = None if direct else refs[5]
    width = vel_ref.shape[2]
    none = jnp.zeros((24, width), jnp.float32)
    tails = [None] * COMPS

    def send(c, samples):
        sums = jnp.dot(a_ref[...], samples, preferred_element_type=jnp.float32)
        own_ref[48 * c:48 * c + 48, :] = sums[:48].astype(jnp.bfloat16)
        near_ref[48 * c:48 * c + 48, :] = sums[48:96].astype(jnp.bfloat16)
        if direct:
            far2_ref[48 * c:48 * c + 48, :] = sums[96:144].astype(jnp.bfloat16)
            far3_ref[48 * c:48 * c + 48, :] = sums[144:].astype(jnp.bfloat16)
        else:
            part = part_ref[16 * c:16 * c + 16, :].astype(jnp.float32)
            far2 = sums[96:128] + jnp.concatenate([none, part[:8]], axis=0)
            far3 = sums[128:160] + jnp.concatenate([none, part[8:]], axis=0)
            far2_ref[32 * c:32 * c + 32, :] = far2.astype(jnp.bfloat16)
            far3_ref[32 * c:32 * c + 32, :] = far3.astype(jnp.bfloat16)
            tails[c] = sums[160:168]

    send(2, vel_ref[2])
    turning = mask_ref[...] == 1
    for at in range(0, span, 16):
        here = pl.ds(at, min(16, span - at))
        new_x, new_y = rotate(turning, cos_ref[here, :], sin_ref[here, :], vel_ref[0, here, :], vel_ref[1, here, :])
        rot_ref[0, here, :] = new_x
        rot_ref[1, here, :] = new_y
    send(0, rot_ref[0])
    send(1, rot_ref[1])
    if not direct:
        far2_ref[96:112, :] = jnp.concatenate([t[:4] for t in tails] + [none[:4]], axis=0).astype(jnp.bfloat16)
        far3_ref[96:112, :] = jnp.concatenate([t[4:] for t in tails] + [none[:4]], axis=0).astype(jnp.bfloat16)


def line_dft(offset, points, mask, velocity, rows, cosine, sine, part, after):
    span = velocity.shape[1]
    shift = offset // TILE
    direct = part is None
    whole = lambda shape: pl.BlockSpec(shape, lambda i: (0,) * len(shape))
    args = [mask, velocity, rows, cosine, sine]
    in_specs = [
        pl.BlockSpec((1, TILE), lambda i: (0, i + shift)),
        pl.BlockSpec((COMPS, span, TILE), lambda i: (0, 0, i + shift)),
    ] + [whole(x.shape) for x in args[2:]]
    if not direct:
        args.append(part)
        in_specs.append(pl.BlockSpec((48, TILE), lambda i: (0, i + shift)))
    if after is not None:
        args.append(after)
        in_specs.append(pl.BlockSpec(memory_space=pl.ANY))
    heights = [144] * 4 if direct else [144, 144, 112, 112]
    return pl.pallas_call(
        functools.partial(line_dft_body, span, direct),
        grid=(points // TILE,),
        out_shape=[jax.ShapeDtypeStruct((h, points), jnp.bfloat16) for h in heights],
        in_specs=in_specs,
        out_specs=[pl.BlockSpec((h, TILE), lambda i: (0, i)) for h in heights],
        scratch_shapes=[pltpu.VMEM((2, span, TILE), jnp.bfloat16)],
        compiler_params=pltpu.CompilerParams(vmem_limit_bytes=LIMIT_B * 2**20),
        cost_estimate=pl.CostEstimate(
            flops=2 * 192 * span * COMPS * points, bytes_accessed=2 * COMPS * span * points, transcendentals=0
        ),
        name="rotate_dft",
    )(*args)


def line_selection(blocks, me, direct, sel_ref):
    shape = (4 * blocks, 192)
    out = lax.broadcasted_iota(jnp.int32, shape, 0)
    col = lax.broadcasted_iota(jnp.int32, shape, 1)
    two, three = me ^ 2, me ^ 3
    block = jnp.where(col < 48, pick(LINE_LO, me) + col // 4, pick(LINE_LO, me ^ 1) + (col - 48) // 4)
    if direct:
        block = jnp.where(col >= 96, pick(LINE_LO, two) + (col - 96) // 4, block)
        block = jnp.where(col >= 144, pick(LINE_LO, three) + (col - 144) // 4, block)
    else:
        block = jnp.where(col >= 96, far_block(two, (col - 96) // 4), block)
        block = jnp.where(col >= 128, far_block(three, (col - 128) // 4), block)
        block = jnp.where(col >= 160, far_block(two, FAR - 1), block)
        block = jnp.where(col >= 176, far_block(three, FAR - 1), block)
    same = (out // blocks == col % 4) & (out % blocks == block)
    for c in range(COMPS):
        mine = same if direct else same & ((col < 160) | ((col % 16) // 4 == c))
        sel_ref[c] = jnp.where(mine, 1.0, 0.0).astype(jnp.bfloat16)


def line_assemble_body(blocks, total, has_sum, last, direct, *refs):
    pos_ref, own_ref, near_ref, far2_ref, far3_ref = refs[:5]
    rest = refs[5:]
    if has_sum:
        sum_in, rest = rest[0], rest[2:]
    spectra_ref, gram_ref, sel_ref, acc_ref = rest[-4:]
    step = pl.program_id(0)
    me = pos_ref[0]

    @pl.when(step == 0)
    def _():
        line_selection(blocks, me, direct, sel_ref)
        acc_ref[...] = sum_in[...] if has_sum else jnp.zeros_like(acc_ref)

    for c in range(COMPS):
        wide = slice(48 * c, 48 * c + 48)
        parts = [own_ref[wide, :], near_ref[wide, :]]
        if direct:
            parts += [far2_ref[wide, :], far3_ref[wide, :]]
        else:
            here = slice(32 * c, 32 * c + 32)
            parts += [far2_ref[here, :], far3_ref[here, :], far2_ref[96:112, :], far3_ref[96:112, :]]
        stack = jnp.concatenate(parts, axis=0)
        full = jnp.dot(sel_ref[c], stack, preferred_element_type=jnp.float32)
        for jr in range(4):
            spectra_ref[jr // 2, jr % 2, c] = full[jr * blocks:(jr + 1) * blocks]
        high = full.astype(jnp.bfloat16)
        low = (full - high.astype(jnp.float32)).astype(jnp.bfloat16)
        pair = jnp.concatenate([high, low], axis=0)
        acc_ref[...] += lax.dot_general(
            pair, pair, (((1,), (1,)), ((), ())), preferred_element_type=jnp.float32
        )

    @pl.when(step == pl.num_programs(0) - 1)
    def _():
        if not last:
            gram_ref[...] = acc_ref[...]
        else:
            n = 4 * blocks
            order = 2 * blocks
            acc = acc_ref[...]
            gram = (acc[:n, :n] + (acc[:n, n:] + acc[n:, :n])) * (1.0 / total)
            gram_ref[...] = jnp.concatenate([gram[:order, :order], gram[order:, order:]], axis=1)


def line_assemble(blocks, total, offset, points, all_points, position, own, near, fars, spectra, gram, last, after):
    shift = offset // TILE
    order = 2 * blocks
    has_sum = gram is not None
    whole = lambda shape: pl.BlockSpec(shape, lambda i: (0,) * len(shape))
    gram_shape = (order, 2 * order) if last else (4 * order, 4 * order)
    args = [position, own, near] + list(fars)
    in_specs = [pl.BlockSpec(memory_space=pltpu.SMEM)]
    in_specs += [pl.BlockSpec((a.shape[0], TILE), lambda i: (0, i)) for a in args[1:]]
    aliases = {}
    if has_sum:
        args += [gram, spectra]
        in_specs += [whole((4 * order, 4 * order)), pl.BlockSpec(memory_space=pl.ANY)]
        aliases = {len(args) - 1: 0}
    if after is not None:
        args.append(after)
        in_specs.append(pl.BlockSpec(memory_space=pl.ANY))
    return pl.pallas_call(
        functools.partial(line_assemble_body, blocks, total, has_sum, last, fars[0].shape[0] == 144),
        grid=(points // TILE,),
        out_shape=[
            jax.ShapeDtypeStruct((2, 2, COMPS, blocks, all_points), jnp.float32),
            jax.ShapeDtypeStruct(gram_shape, jnp.float32),
        ],
        in_specs=in_specs,
        out_specs=[
            pl.BlockSpec((2, 2, COMPS, blocks, TILE), lambda i: (0, 0, 0, 0, i + shift)),
            whole(gram_shape),
        ],
        scratch_shapes=[
            pltpu.VMEM((COMPS, 4 * blocks, 192), jnp.bfloat16),
            pltpu.VMEM((4 * order, 4 * order), jnp.float32),
        ],
        input_output_aliases=aliases,
        compiler_params=pltpu.CompilerParams(vmem_limit_bytes=LIMIT_C * 2**20),
        cost_estimate=SHORT,
        name="assemble",
    )(*args)


def line_chunks(points):
    cuts = [points * k // 8 for k in (0, 1, 3, 6, 8)]
    return [(a, b - a) for a, b in zip(cuts[:-1], cuts[1:])]


def line_spectra(samples, mask, angles, block_starts, frequencies, position, total):
    points = samples.shape[2]
    blocks = block_starts.shape[0]
    move = lambda x, pairs: lax.ppermute(x, "tm", pairs)
    across = lambda x, k: move(x, [(i, i ^ k) for i in range(4)])
    part, direct_rows, rows, cosine, sine = prepare(
        blocks, position, block_starts, frequencies, angles, mask, samples
    )
    part = move(part, [(1, 0), (2, 3)])
    spectra, gram = None, None
    sent = []

    def assemble(after):
        at, count, own, near, fars = sent.pop(0)
        return line_assemble(
            blocks, total, at, count, points, position, own, near, fars, spectra, gram, at + count == points, after
        )

    for i, (at, count) in enumerate(line_chunks(points)):
        if i >= 2:
            spectra, gram = assemble(own)
        own, near, far2, far3 = line_dft(
            at, count, mask, samples, rows if i else direct_rows, cosine, sine, part if i else None, gram
        )
        sent.append((at, count, own, across(near, 1), [across(far2, 2), across(far3, 3)]))
    while sent:
        spectra, gram = assemble(None)
    return spectra, gram


def fits_line(n, span, blocks, owned):
    if n != 4 or owned != 2:
        return False
    lo = [max((s * span - (NFFT + JIT - 1) + HOP) // HOP, 0) for s in range(n)]
    hi = [min((span * (s + 1) - 1) // HOP, blocks - 1) for s in range(n)]
    return lo == LINE_LO and hi == LINE_HI and blocks == 32


def sum_over_space(gram, groups):
    if groups != 8:
        return [lax.psum(gram, "space")]
    swap = lambda x, k: lax.ppermute(x, "space", [(i, i ^ k) for i in range(groups)])
    gram = gram + swap(gram, 1)
    gram = gram + swap(gram, 2)
    return [gram, swap(gram, 4)]


def chunks_of(points):
    tile = 512
    return [(at, tile) for at in range(0, points, tile)]


def ring_spectra(n, owned, slots, blocks, total, position, block_starts, frequencies, angles, mask, samples):
    span, points = samples.shape[1:]
    pieces = []
    shared = None
    for at, count in chunks_of(points):
        sums, shared = dft_call(
            n, owned, slots, blocks, shared is None, at, count,
            position, block_starts, frequencies, angles, mask, samples, shared,
        )
        moved = [sums[0]] + [
            lax.ppermute(sums[k], "tm", [(i, (i + k) % n) for i in range(n)]) for k in range(1, n)
        ]
        pieces.append((at, count, moved))

    spectra, gram = None, None
    for at, count, moved in pieces:
        last = at + count == points
        spectra, gram = assemble_call(
            n, owned, slots, span, blocks, total, at, count, points, position, moved, spectra, gram, last
        )
    return spectra, gram


def per_device(velocity, rotor_mask, rotor_angle, block_starts, frequencies):
    span, _, points = velocity.shape
    n = lax.axis_size("tm")
    groups = lax.axis_size("space")
    blocks = block_starts.shape[0]
    owned = frequencies.shape[0] // n
    order = 2 * blocks
    slots = slot_count(n, span, blocks, owned * 2)
    position = lax.axis_index("tm").astype(jnp.int32).reshape(1)
    samples = velocity.transpose(1, 0, 2)
    mask = rotor_mask.reshape(1, points)
    angles = rotor_angle

    total = COMPS * points * groups
    if fits_line(n, span, blocks, owned):
        spectra, gram = line_spectra(samples, mask, angles, block_starts, frequencies, position, total)
    else:
        spectra, gram = ring_spectra(
            n, owned, slots, blocks, total, position, block_starts, frequencies, angles, mask, samples
        )
    factors = factor_call(owned, order, sum_over_space(gram, groups))
    return spectra.transpose(0, 1, 3, 2, 4), factors


def solution(mesh):
    in_specs = (P("tm", None, "space"), P("space"), P("tm"), P(), P())
    out_specs = (P("tm", None, None, None, "space"), P("tm", None, None))
    return jax.shard_map(
        per_device, mesh=mesh, in_specs=in_specs, out_specs=out_specs, check_vma=False
    )
```

```python
import functools
import math

import jax
import jax.numpy as jnp
from jax import lax
from jax.experimental import pallas as pl
from jax.experimental.pallas import tpu as pltpu
from jax.sharding import PartitionSpec as P

COMPS = 3
NFFT = 256
JIT = 64
HOP = 128
LANES = 128
TILE = 256
PIVOT = 4
LIMIT_A, LIMIT_B, LIMIT_C = 60, 60, 40
SCALE = (8.0 / (3.0 * NFFT)) ** 0.5
HIGHEST = lax.Precision.HIGHEST
SHORT = pl.CostEstimate(flops=1000, bytes_accessed=1000, transcendentals=0)


def first_block(shard, span):
    return jnp.maximum((shard * span - (NFFT + JIT - 1) + HOP) // HOP, 0)


def slot_count(shards, span, blocks, rows_per_slot):
    most = 0
    for s in range(shards):
        lo = max((s * span - (NFFT + JIT - 1) + HOP) // HOP, 0)
        hi = min((span * (s + 1) - 1) // HOP, blocks - 1)
        most = max(most, hi - lo + 1)
    step = 16 // math.gcd(16, rows_per_slot)
    return -(-most // step) * step


def half_turn_sine(x):
    z = x * x
    c = [math.pi ** (2 * i + 1) * (-1) ** i / math.factorial(2 * i + 1) for i in range(7)]
    acc = jnp.full_like(z, c[-1])
    for term in c[-2::-1]:
        acc = acc * z + term
    return acc * x


def build_rows(n, owned, slots, span, blocks, me, starts_ref, freqs_ref, a_ref):
    group = owned * 2
    rid = lax.broadcasted_iota(jnp.int32, (n * group, 1), 0)
    k_of, j_of, r_of = rid // group, (rid // 2) % owned, rid % 2
    f_of = lax.rem(me + k_of, n) * owned + j_of
    freq = jnp.zeros((n * group, 1), jnp.float32)
    for f in range(n * owned):
        freq = jnp.where(f_of == f, freqs_ref[f].astype(jnp.float32), freq)
    step = freq * (1.0 / NFFT)
    quarter = r_of.astype(jnp.float32) * 0.25
    lo = first_block(me, span)
    sample = lax.broadcasted_iota(jnp.int32, (1, span), 1) + me * span
    pieces = [[] for _ in range(n)]
    for s in range(slots):
        b = lo + s
        start = starts_ref[jnp.minimum(b, blocks - 1)]
        ni = sample - start
        inside = (ni >= 0) & (ni < NFFT) & (b < blocks)
        nf = ni.astype(jnp.float32)
        w = half_turn_sine(jnp.minimum(nf, NFFT - nf) * (1.0 / NFFT))
        w = jnp.where(inside, w * w * SCALE, 0.0)
        nf = jnp.where(inside, nf, 0.0)
        turns = nf * step + quarter
        turns = turns - jnp.floor(turns + 0.5)
        h = half_turn_sine(turns)
        rows = w * (1.0 - 2.0 * h * h)
        for k in range(n):
            pieces[k].append(rows[k * group:(k + 1) * group])
    for k in range(n):
        a_ref[k] = jnp.concatenate(pieces[k], axis=0).astype(jnp.bfloat16)


def spread_column(row, span, out_ref):
    for at in range(0, span, LANES):
        width = min(LANES, span - at)
        part = row[:, at:at + width]
        if width < LANES:
            part = jnp.concatenate([part, jnp.zeros((1, LANES - width), jnp.float32)], axis=1)
        turned = jnp.transpose(jnp.broadcast_to(part, (LANES, LANES)))
        out_ref[at:at + width, :] = turned[:width]


def dft_body(n, owned, slots, span, blocks, first, *refs):
    if first:
        pos_ref, starts_ref, freqs_ref, angle_ref, mask_ref, vel_ref = refs[:6]
        outs = refs[6:6 + n]
        a_ref, cos_ref, sin_ref = refs[6 + n:9 + n]
        rot_ref = refs[9 + n]

        @pl.when(pl.program_id(0) == 0)
        def _():
            build_rows(n, owned, slots, span, blocks, pos_ref[0], starts_ref, freqs_ref, a_ref)
            spread_column(jnp.cos(angle_ref[...].reshape(1, span)), span, cos_ref)
            spread_column(jnp.sin(angle_ref[...].reshape(1, span)), span, sin_ref)
    else:
        mask_ref, vel_ref, a_ref, cos_ref, sin_ref = refs[:5]
        outs = refs[5:5 + n]
        rot_ref = refs[5 + n]
    width = vel_ref.shape[2]
    turning = mask_ref[...] == 1
    for at in range(0, span, 16):
        rows = min(16, span - at)
        here = pl.ds(at, rows)
        cosine = jnp.concatenate([cos_ref[here, :]] * (width // LANES), axis=1)
        sine = jnp.concatenate([sin_ref[here, :]] * (width // LANES), axis=1)
        x = vel_ref[0, here, :].astype(jnp.float32)
        y = vel_ref[1, here, :].astype(jnp.float32)
        rot_ref[0, here, :] = jnp.where(turning, cosine * x - sine * y, x).astype(jnp.bfloat16)
        rot_ref[1, here, :] = jnp.where(turning, sine * x + cosine * y, y).astype(jnp.bfloat16)
    rows = a_ref.shape[1]
    a = a_ref[...].reshape(n * rows, span)
    for c in range(COMPS):
        samples = rot_ref[c] if c < 2 else vel_ref[2]
        sums = jnp.dot(a, samples, preferred_element_type=jnp.float32).astype(jnp.bfloat16)
        for k in range(n):
            outs[k][c * rows:(c + 1) * rows, :] = sums[k * rows:(k + 1) * rows]


def dft_call(n, owned, slots, blocks, first, offset, points, position, starts, freqs, angles, mask, velocity, shared):
    span = velocity.shape[1]
    rows = slots * owned * 2
    shift = offset // TILE
    whole = lambda shape: pl.BlockSpec(shape, lambda i: (0,) * len(shape))
    smem = pl.BlockSpec(memory_space=pltpu.SMEM)
    data_specs = [
        pl.BlockSpec((1, TILE), lambda i: (0, i + shift)),
        pl.BlockSpec((COMPS, span, TILE), lambda i: (0, 0, i + shift)),
    ]
    shared_types = [
        jax.ShapeDtypeStruct((n, rows, span), jnp.bfloat16),
        jax.ShapeDtypeStruct((span, LANES), jnp.float32),
        jax.ShapeDtypeStruct((span, LANES), jnp.float32),
    ]
    shared_specs = [whole(t.shape) for t in shared_types]
    out_types = [jax.ShapeDtypeStruct((COMPS * rows, points), jnp.bfloat16)] * n
    out_specs = [pl.BlockSpec((COMPS * rows, TILE), lambda i: (0, i))] * n
    if first:
        args = (position, starts, freqs, angles, mask, velocity)
        in_specs = [smem] * 3 + [whole((span,))] + data_specs
        out_types = out_types + shared_types
        out_specs = out_specs + shared_specs
    else:
        args = (mask, velocity) + tuple(shared)
        in_specs = data_specs + shared_specs
    out = pl.pallas_call(
        functools.partial(dft_body, n, owned, slots, span, blocks, first),
        grid=(points // TILE,),
        out_shape=out_types,
        in_specs=in_specs,
        out_specs=out_specs,
        scratch_shapes=[pltpu.VMEM((2, span, TILE), jnp.bfloat16)],
        compiler_params=pltpu.CompilerParams(vmem_limit_bytes=40 * 2**20),
        cost_estimate=pl.CostEstimate(
            flops=2 * n * rows * span * COMPS * points,
            bytes_accessed=2 * COMPS * span * points,
            transcendentals=0,
        ),
        name="rotate_dft",
    )(*args)
    return out[:n], out[n:] if first else shared


def selection(n, owned, slots, span, blocks, me):
    rows = slots * owned * 2
    shape = (owned * 2 * blocks, n * rows)
    out = lax.broadcasted_iota(jnp.int32, shape, 0)
    col = lax.broadcasted_iota(jnp.int32, shape, 1)
    k_of = jnp.zeros(shape, jnp.int32)
    lo = jnp.broadcast_to(first_block(me, span), shape)
    for k in range(1, n):
        past = col >= k * rows
        k_of = jnp.where(past, k, k_of)
        lo = jnp.where(past, first_block(lax.rem(me + n - k, n), span), lo)
    rem = col - k_of * rows
    slot = rem // (owned * 2)
    same = (out // blocks == rem % (owned * 2)) & (out % blocks == lo + slot)
    return jnp.where(same, 1.0, 0.0)


def assemble_body(n, owned, slots, span, blocks, total, has_sum, last, *refs):
    pos_ref = refs[0]
    parts = refs[1:1 + n]
    rest = refs[1 + n:]
    if has_sum:
        sum_in, rest = rest[0], rest[2:]
    spectra_ref, gram_ref, sel_ref, acc_ref = rest
    step = pl.program_id(0)
    rows = slots * owned * 2

    @pl.when(step == 0)
    def _():
        sel_ref[...] = selection(n, owned, slots, span, blocks, pos_ref[0]).astype(jnp.bfloat16)
        acc_ref[...] = sum_in[...] if has_sum else jnp.zeros_like(acc_ref)

    for c in range(COMPS):
        stack = jnp.concatenate([p[c * rows:(c + 1) * rows, :] for p in parts], axis=0)
        full = jnp.dot(sel_ref[...], stack, preferred_element_type=jnp.float32)
        for j in range(owned):
            for r in range(2):
                at = (j * 2 + r) * blocks
                spectra_ref[j, r, c] = full[at:at + blocks]
        acc_ref[...] += lax.dot_general(
            stack, stack, (((1,), (1,)), ((), ())), preferred_element_type=jnp.float32
        )

    @pl.when(step == pl.num_programs(0) - 1)
    def _():
        if not last:
            gram_ref[...] = acc_ref[...]
        else:
            sel = sel_ref[...].astype(jnp.float32)
            half = jnp.dot(sel, acc_ref[...], precision=HIGHEST, preferred_element_type=jnp.float32)
            order = 2 * blocks
            gram = lax.dot_general(
                half, sel, (((1,), (1,)), ((), ())), precision=HIGHEST, preferred_element_type=jnp.float32
            ) * (1.0 / total)
            gram_ref[...] = jnp.concatenate(
                [gram[j * order:(j + 1) * order, j * order:(j + 1) * order] for j in range(owned)], axis=1
            )


def assemble_call(n, owned, slots, span, blocks, total, offset, points, all_points, position, parts, spectra, gram, last):
    rows = slots * owned * 2
    tile = min(points, 512)
    shift = offset // tile
    order = 2 * blocks
    has_sum = gram is not None
    whole = lambda shape: pl.BlockSpec(shape, lambda i: (0,) * len(shape))
    gram_shape = (order, owned * order) if last else (n * rows, n * rows)
    args = [position] + list(parts)
    in_specs = [pl.BlockSpec(memory_space=pltpu.SMEM)] + [pl.BlockSpec((COMPS * rows, tile), lambda i: (0, i))] * n
    aliases = {}
    if has_sum:
        args += [gram, spectra]
        in_specs += [whole((n * rows, n * rows)), pl.BlockSpec(memory_space=pl.ANY)]
        aliases = {len(args) - 1: 0}
    return pl.pallas_call(
        functools.partial(assemble_body, n, owned, slots, span, blocks, total, has_sum, last),
        grid=(points // tile,),
        out_shape=[
            jax.ShapeDtypeStruct((owned, 2, COMPS, blocks, all_points), jnp.float32),
            jax.ShapeDtypeStruct(gram_shape, jnp.float32),
        ],
        in_specs=in_specs,
        out_specs=[
            pl.BlockSpec((owned, 2, COMPS, blocks, tile), lambda i: (0, 0, 0, 0, i + shift)),
            whole(gram_shape),
        ],
        scratch_shapes=[
            pltpu.VMEM((owned * order, n * rows), jnp.bfloat16),
            pltpu.VMEM((n * rows, n * rows), jnp.float32),
        ],
        input_output_aliases=aliases,
        compiler_params=pltpu.CompilerParams(vmem_limit_bytes=40 * 2**20),
        cost_estimate=pl.CostEstimate(
            flops=4 * (n * rows) ** 2 * COMPS * points,
            bytes_accessed=4 * owned * order * COMPS * points,
            transcendentals=0,
        ),
        name="assemble",
    )(*args)


def factor_body(owned, order, count, *refs):
    parts = refs[:count]
    out_ref, row_ref = refs[count:]
    s = [p[...] for p in parts] if len(parts[0].shape) == 2 else [parts[0][i] for i in range(parts[0].shape[0])]
    while len(s) > 1:
        s = [a + b for a, b in zip(s[::2], s[1::2])]
    s = s[0]
    lane = lax.broadcasted_iota(jnp.int32, (1, owned * order), 1)
    for k in range(0, order, PIVOT):
        base = k // 8 * 8
        s = s[base - max(k - PIVOT, 0) // 8 * 8:]
        columns = []
        for i in range(k, k + PIVOT):
            column = jnp.broadcast_to(s[:, i:i + 1], s.shape)
            for j in range(1, owned):
                column = jnp.where(lane >= j * order, s[:, j * order + i:j * order + i + 1], column)
            columns.append(column)
        at = k - base
        rows = [s[at + i:at + i + 1] for i in range(PIVOT)]
        for i in range(PIVOT):
            inverse_root = lax.rsqrt(columns[i][at + i:at + i + 1])
            columns[i] = columns[i] * inverse_root
            rows[i] = rows[i] * inverse_root
            for j in range(i + 1, PIVOT):
                weight = columns[i][at + j:at + j + 1]
                columns[j] = columns[j] - columns[i] * weight
                rows[j] = rows[j] - rows[i] * weight
            row_ref[k + i:k + i + 1, :] = jnp.where(lane % order >= k + i, rows[i], 0.0)
            s = s - columns[i] * rows[i]
    for j in range(owned):
        out_ref[j] = row_ref[:, j * order:(j + 1) * order]


def factor_call(owned, order, parts):
    return pl.pallas_call(
        functools.partial(factor_body, owned, order, len(parts)),
        out_shape=jax.ShapeDtypeStruct((owned, order, order), jnp.float32),
        scratch_shapes=[pltpu.VMEM((order, owned * order), jnp.float32)],
        name="factor",
    )(*parts)


LINE_LO = [0, 6, 15, 23]
LINE_HI = [8, 16, 25, 31]
WIDE = 12
FAR = 9
SHARED = 2
REACH = 144


def pick(values, me):
    out = jnp.int32(values[0])
    for i in range(1, len(values)):
        out = jnp.where(me == i, jnp.int32(values[i]), out)
    return out


def far_block(shard, slot):
    return pick([0, 8, 23, 31], shard) + pick([1, 1, -1, -1], shard) * slot


def cosine_of(turns):
    s = half_turn_sine(turns - jnp.floor(turns + 0.5))
    return 1.0 - 2.0 * s * s


def build_line(span, blocks, me, starts_ref, freqs_ref, direct_ref, a_ref, rows_ref):
    lo = pick(LINE_LO, me)
    starts = [starts_ref[jnp.minimum(lo + s, blocks - 1)] for s in range(WIDE)]

    def by_slot(shape, axis):
        at = lax.broadcasted_iota(jnp.int32, shape, axis)
        out = jnp.full(shape, starts[0], jnp.int32)
        for s in range(1, WIDE):
            out = jnp.where(at == s, starts[s], out)
        return out

    rid = lax.broadcasted_iota(jnp.int32, (16, 1), 0)
    f_of = ((rid // 4) ^ me) * 2 + (rid // 2) % 2
    freq = jnp.zeros((16, 1), jnp.float32)
    for f in range(8):
        freq = jnp.where(f_of == f, freqs_ref[f].astype(jnp.float32), freq)
    step = freq * (1.0 / NFFT)
    quarter = (rid % 2).astype(jnp.float32) * 0.25

    sample = lax.broadcasted_iota(jnp.int32, (1, span), 1) + me * span
    turns = sample.astype(jnp.float32) * step
    turns = turns - jnp.floor(turns) + quarter
    cos_t, sin_t = cosine_of(turns), cosine_of(turns - 0.25)
    begin = by_slot((1, LANES), 1).astype(jnp.float32) * step
    begin = begin - jnp.floor(begin)
    cos_b, sin_b = cosine_of(begin), cosine_of(begin - 0.25)

    slot = lax.broadcasted_iota(jnp.int32, (16, 1), 0)
    ni = sample - by_slot((16, 1), 0)
    nf = ni.astype(jnp.float32)
    w = half_turn_sine(jnp.minimum(nf, NFFT - nf) * (1.0 / NFFT))
    w = jnp.where((ni >= 0) & (ni < NFFT) & (slot + lo < blocks), w * w * SCALE, 0.0)

    own, near, direct2, direct3 = [], [], [], []
    for s in range(WIDE):
        rows = (cos_t * cos_b[:, s:s + 1] + sin_t * sin_b[:, s:s + 1]) * w[s:s + 1]
        rows_ref[s] = rows[8:]
        own.append(rows[:4])
        near.append(rows[4:8])
        direct2.append(rows[8:12])
        direct3.append(rows[12:])
    direct_ref[...] = jnp.concatenate(own + near + direct2 + direct3, axis=0).astype(jnp.bfloat16)
    far = [rows_ref[far_block(me, s) - lo] for s in range(FAR)]
    pieces = own + near
    pieces += [r[:4] for r in far[:-1]] + [r[4:] for r in far[:-1]]
    pieces += [far[-1], jnp.zeros((8, span), jnp.float32)]
    a_ref[...] = jnp.concatenate(pieces, axis=0).astype(jnp.bfloat16)


def rotate(turning, cosine, sine, x, y):
    width = x.shape[1]
    cosine = jnp.concatenate([cosine] * (width // LANES), axis=1)
    sine = jnp.concatenate([sine] * (width // LANES), axis=1)
    x, y = x.astype(jnp.float32), y.astype(jnp.float32)
    new_x = jnp.where(turning, cosine * x - sine * y, x)
    new_y = jnp.where(turning, sine * x + cosine * y, y)
    return new_x.astype(jnp.bfloat16), new_y.astype(jnp.bfloat16)


def shared_rows(begin, me, starts_ref, freqs_ref):
    rid = lax.broadcasted_iota(jnp.int32, (16, 1), 0)
    f_of = jnp.where(rid < 8, me ^ 3, me ^ 2) * 2 + (rid // 2) % 2
    freq = jnp.zeros((16, 1), jnp.float32)
    for f in range(8):
        freq = jnp.where(f_of == f, freqs_ref[f].astype(jnp.float32), freq)
    first, second = (starts_ref[pick([0, 6 + s, 25 - s, 0], me)] for s in range(SHARED))
    start = jnp.where((rid // 4) % 2 == 0, first, second)
    ni = lax.broadcasted_iota(jnp.int32, (1, REACH), 1) + begin - start
    nf = ni.astype(jnp.float32)
    w = half_turn_sine(jnp.minimum(nf, NFFT - nf) * (1.0 / NFFT))
    inner = (me == 1) | (me == 2)
    w = jnp.where((ni >= 0) & (ni < NFFT) & inner, w * w * SCALE, 0.0)
    turns = nf * (freq * (1.0 / NFFT)) + (rid % 2).astype(jnp.float32) * 0.25
    return (cosine_of(turns) * w).astype(jnp.bfloat16)


def prepare_body(span, blocks, pos_ref, starts_ref, freqs_ref, angle_ref, mask_ref, all_hbm,
                 part_ref, direct_ref, a_ref, cos_ref, sin_ref, rows_ref, ends_ref, ends_rot_ref, ends_sem):
    me = pos_ref[0]
    begin = pl.multiple_of(jnp.where(me == 2, span - REACH, 0), 16)
    load = pltpu.make_async_copy(all_hbm.at[:, pl.ds(begin, REACH), :], ends_ref, ends_sem)
    load.start()
    build_line(span, blocks, me, starts_ref, freqs_ref, direct_ref, a_ref, rows_ref)
    spread_column(jnp.cos(angle_ref[...].reshape(1, span)), span, cos_ref)
    spread_column(jnp.sin(angle_ref[...].reshape(1, span)), span, sin_ref)
    rows = shared_rows(begin + me * span, me, starts_ref, freqs_ref)
    load.wait()
    for lane in range(0, part_ref.shape[1], TILE):
        here = slice(lane, lane + TILE)
        turning = mask_ref[:, here] == 1
        for at in range(0, REACH, 16):
            row = slice(at, at + 16)
            t = pl.ds(pl.multiple_of(begin + at, 16), 16)
            new_x, new_y = rotate(
                turning, cos_ref[t, :], sin_ref[t, :], ends_ref[0, row, here], ends_ref[1, row, here]
            )
            ends_rot_ref[0, row, here] = new_x
            ends_rot_ref[1, row, here] = new_y
        for c in range(COMPS):
            samples = ends_rot_ref[c, :, here] if c < 2 else ends_ref[2, :, here]
            sums = jnp.dot(rows, samples, preferred_element_type=jnp.float32)
            part_ref[16 * c:16 * c + 16, here] = sums.astype(jnp.bfloat16)


def prepare(blocks, position, starts, freqs, angles, mask, velocity):
    span, points = velocity.shape[1:]
    smem, vmem, anywhere = (pl.BlockSpec(memory_space=m) for m in (pltpu.SMEM, pltpu.VMEM, pl.ANY))
    whole = lambda shape: pl.BlockSpec(shape, lambda i: (0,) * len(shape))
    types = [
        jax.ShapeDtypeStruct((48, points), jnp.bfloat16),
        jax.ShapeDtypeStruct((192, span), jnp.bfloat16),
        jax.ShapeDtypeStruct((176, span), jnp.bfloat16),
        jax.ShapeDtypeStruct((span, LANES), jnp.float32),
        jax.ShapeDtypeStruct((span, LANES), jnp.float32),
    ]
    return pl.pallas_call(
        functools.partial(prepare_body, span, blocks),
        grid=(1,),
        out_shape=types,
        in_specs=[smem] * 3 + [whole((span,)), whole((1, points)), anywhere],
        out_specs=[whole(t.shape) for t in types],
        scratch_shapes=[
            pltpu.VMEM((WIDE, 8, span), jnp.float32),
            pltpu.VMEM((COMPS, REACH, points), jnp.bfloat16),
            pltpu.VMEM((2, REACH, points), jnp.bfloat16),
            pltpu.SemaphoreType.DMA,
        ],
        compiler_params=pltpu.CompilerParams(vmem_limit_bytes=LIMIT_A * 2**20),
        cost_estimate=pl.CostEstimate(flops=10**9, bytes_accessed=4 * 10**6, transcendentals=0),
        name="prepare",
    )(position, starts, freqs, angles, mask, velocity)


def line_dft_body(span, direct, *refs):
    mask_ref, vel_ref, a_ref, cos_ref, sin_ref = refs[:5]
    own_ref, near_ref, far2_ref, far3_ref, rot_ref = refs[-5:]
    part_ref = None if direct else refs[5]
    width = vel_ref.shape[2]
    none = jnp.zeros((24, width), jnp.float32)
    tails = [None] * COMPS

    def send(c, samples):
        sums = jnp.dot(a_ref[...], samples, preferred_element_type=jnp.float32)
        own_ref[48 * c:48 * c + 48, :] = sums[:48].astype(jnp.bfloat16)
        near_ref[48 * c:48 * c + 48, :] = sums[48:96].astype(jnp.bfloat16)
        if direct:
            far2_ref[48 * c:48 * c + 48, :] = sums[96:144].astype(jnp.bfloat16)
            far3_ref[48 * c:48 * c + 48, :] = sums[144:].astype(jnp.bfloat16)
        else:
            part = part_ref[16 * c:16 * c + 16, :].astype(jnp.float32)
            far2 = sums[96:128] + jnp.concatenate([none, part[:8]], axis=0)
            far3 = sums[128:160] + jnp.concatenate([none, part[8:]], axis=0)
            far2_ref[32 * c:32 * c + 32, :] = far2.astype(jnp.bfloat16)
            far3_ref[32 * c:32 * c + 32, :] = far3.astype(jnp.bfloat16)
            tails[c] = sums[160:168]

    send(2, vel_ref[2])
    turning = mask_ref[...] == 1
    for at in range(0, span, 16):
        here = pl.ds(at, min(16, span - at))
        new_x, new_y = rotate(turning, cos_ref[here, :], sin_ref[here, :], vel_ref[0, here, :], vel_ref[1, here, :])
        rot_ref[0, here, :] = new_x
        rot_ref[1, here, :] = new_y
    send(0, rot_ref[0])
    send(1, rot_ref[1])
    if not direct:
        far2_ref[96:112, :] = jnp.concatenate([t[:4] for t in tails] + [none[:4]], axis=0).astype(jnp.bfloat16)
        far3_ref[96:112, :] = jnp.concatenate([t[4:] for t in tails] + [none[:4]], axis=0).astype(jnp.bfloat16)


def line_dft(offset, points, mask, velocity, rows, cosine, sine, part, after):
    span = velocity.shape[1]
    shift = offset // TILE
    direct = part is None
    whole = lambda shape: pl.BlockSpec(shape, lambda i: (0,) * len(shape))
    args = [mask, velocity, rows, cosine, sine]
    in_specs = [
        pl.BlockSpec((1, TILE), lambda i: (0, i + shift)),
        pl.BlockSpec((COMPS, span, TILE), lambda i: (0, 0, i + shift)),
    ] + [whole(x.shape) for x in args[2:]]
    if not direct:
        args.append(part)
        in_specs.append(pl.BlockSpec((48, TILE), lambda i: (0, i + shift)))
    if after is not None:
        args.append(after)
        in_specs.append(pl.BlockSpec(memory_space=pl.ANY))
    heights = [144] * 4 if direct else [144, 144, 112, 112]
    return pl.pallas_call(
        functools.partial(line_dft_body, span, direct),
        grid=(points // TILE,),
        out_shape=[jax.ShapeDtypeStruct((h, points), jnp.bfloat16) for h in heights],
        in_specs=in_specs,
        out_specs=[pl.BlockSpec((h, TILE), lambda i: (0, i)) for h in heights],
        scratch_shapes=[pltpu.VMEM((2, span, TILE), jnp.bfloat16)],
        compiler_params=pltpu.CompilerParams(vmem_limit_bytes=LIMIT_B * 2**20),
        cost_estimate=pl.CostEstimate(
            flops=2 * 192 * span * COMPS * points, bytes_accessed=2 * COMPS * span * points, transcendentals=0
        ),
        name="rotate_dft",
    )(*args)


def line_selection(blocks, me, direct, sel_ref):
    shape = (4 * blocks, 192)
    out = lax.broadcasted_iota(jnp.int32, shape, 0)
    col = lax.broadcasted_iota(jnp.int32, shape, 1)
    two, three = me ^ 2, me ^ 3
    block = jnp.where(col < 48, pick(LINE_LO, me) + col // 4, pick(LINE_LO, me ^ 1) + (col - 48) // 4)
    if direct:
        block = jnp.where(col >= 96, pick(LINE_LO, two) + (col - 96) // 4, block)
        block = jnp.where(col >= 144, pick(LINE_LO, three) + (col - 144) // 4, block)
    else:
        block = jnp.where(col >= 96, far_block(two, (col - 96) // 4), block)
        block = jnp.where(col >= 128, far_block(three, (col - 128) // 4), block)
        block = jnp.where(col >= 160, far_block(two, FAR - 1), block)
        block = jnp.where(col >= 176, far_block(three, FAR - 1), block)
    same = (out // blocks == col % 4) & (out % blocks == block)
    for c in range(COMPS):
        mine = same if direct else same & ((col < 160) | ((col % 16) // 4 == c))
        sel_ref[c] = jnp.where(mine, 1.0, 0.0).astype(jnp.bfloat16)


def line_assemble_body(blocks, total, has_sum, last, direct, *refs):
    pos_ref, own_ref, near_ref, far2_ref, far3_ref = refs[:5]
    rest = refs[5:]
    if has_sum:
        sum_in, rest = rest[0], rest[2:]
    spectra_ref, gram_ref, sel_ref, acc_ref = rest[-4:]
    step = pl.program_id(0)
    me = pos_ref[0]

    @pl.when(step == 0)
    def _():
        line_selection(blocks, me, direct, sel_ref)
        acc_ref[...] = sum_in[...] if has_sum else jnp.zeros_like(acc_ref)

    for c in range(COMPS):
        wide = slice(48 * c, 48 * c + 48)
        parts = [own_ref[wide, :], near_ref[wide, :]]
        if direct:
            parts += [far2_ref[wide, :], far3_ref[wide, :]]
        else:
            here = slice(32 * c, 32 * c + 32)
            parts += [far2_ref[here, :], far3_ref[here, :], far2_ref[96:112, :], far3_ref[96:112, :]]
        stack = jnp.concatenate(parts, axis=0)
        full = jnp.dot(sel_ref[c], stack, preferred_element_type=jnp.float32)
        for jr in range(4):
            spectra_ref[jr // 2, jr % 2, c] = full[jr * blocks:(jr + 1) * blocks]
        high = full.astype(jnp.bfloat16)
        low = (full - high.astype(jnp.float32)).astype(jnp.bfloat16)
        pair = jnp.concatenate([high, low], axis=0)
        acc_ref[...] += lax.dot_general(
            pair, pair, (((1,), (1,)), ((), ())), preferred_element_type=jnp.float32
        )

    @pl.when(step == pl.num_programs(0) - 1)
    def _():
        if not last:
            gram_ref[...] = acc_ref[...]
        else:
            n = 4 * blocks
            order = 2 * blocks
            acc = acc_ref[...]
            gram = (acc[:n, :n] + (acc[:n, n:] + acc[n:, :n])) * (1.0 / total)
            gram_ref[...] = jnp.concatenate([gram[:order, :order], gram[order:, order:]], axis=1)


def line_assemble(blocks, total, offset, points, all_points, position, own, near, fars, spectra, gram, last, after):
    shift = offset // TILE
    order = 2 * blocks
    has_sum = gram is not None
    whole = lambda shape: pl.BlockSpec(shape, lambda i: (0,) * len(shape))
    gram_shape = (order, 2 * order) if last else (4 * order, 4 * order)
    args = [position, own, near] + list(fars)
    in_specs = [pl.BlockSpec(memory_space=pltpu.SMEM)]
    in_specs += [pl.BlockSpec((a.shape[0], TILE), lambda i: (0, i)) for a in args[1:]]
    aliases = {}
    if has_sum:
        args += [gram, spectra]
        in_specs += [whole((4 * order, 4 * order)), pl.BlockSpec(memory_space=pl.ANY)]
        aliases = {len(args) - 1: 0}
    if after is not None:
        args.append(after)
        in_specs.append(pl.BlockSpec(memory_space=pl.ANY))
    return pl.pallas_call(
        functools.partial(line_assemble_body, blocks, total, has_sum, last, fars[0].shape[0] == 144),
        grid=(points // TILE,),
        out_shape=[
            jax.ShapeDtypeStruct((2, 2, COMPS, blocks, all_points), jnp.float32),
            jax.ShapeDtypeStruct(gram_shape, jnp.float32),
        ],
        in_specs=in_specs,
        out_specs=[
            pl.BlockSpec((2, 2, COMPS, blocks, TILE), lambda i: (0, 0, 0, 0, i + shift)),
            whole(gram_shape),
        ],
        scratch_shapes=[
            pltpu.VMEM((COMPS, 4 * blocks, 192), jnp.bfloat16),
            pltpu.VMEM((4 * order, 4 * order), jnp.float32),
        ],
        input_output_aliases=aliases,
        compiler_params=pltpu.CompilerParams(vmem_limit_bytes=LIMIT_C * 2**20),
        cost_estimate=SHORT,
        name="assemble",
    )(*args)


def line_chunks(points):
    cuts = [points * k // 8 for k in (0, 2, 6, 8)]
    return [(a, b - a) for a, b in zip(cuts[:-1], cuts[1:])]


def line_spectra(samples, mask, angles, block_starts, frequencies, position, total):
    points = samples.shape[2]
    blocks = block_starts.shape[0]
    move = lambda x, pairs: lax.ppermute(x, "tm", pairs)
    across = lambda x, k: move(x, [(i, i ^ k) for i in range(4)])
    part, direct_rows, rows, cosine, sine = prepare(
        blocks, position, block_starts, frequencies, angles, mask, samples
    )
    part = move(part, [(1, 0), (2, 3)])
    spectra, gram = None, None
    sent = []

    def assemble(after):
        at, count, own, near, fars = sent.pop(0)
        return line_assemble(
            blocks, total, at, count, points, position, own, near, fars, spectra, gram, at + count == points, after
        )

    for i, (at, count) in enumerate(line_chunks(points)):
        if i >= 2:
            spectra, gram = assemble(own)
        own, near, far2, far3 = line_dft(
            at, count, mask, samples, rows if i else direct_rows, cosine, sine, part if i else None, gram
        )
        sent.append((at, count, own, across(near, 1), [across(far2, 2), across(far3, 3)]))
    while sent:
        spectra, gram = assemble(None)
    return spectra, gram


def fits_line(n, span, blocks, owned):
    if n != 4 or owned != 2:
        return False
    lo = [max((s * span - (NFFT + JIT - 1) + HOP) // HOP, 0) for s in range(n)]
    hi = [min((span * (s + 1) - 1) // HOP, blocks - 1) for s in range(n)]
    return lo == LINE_LO and hi == LINE_HI and blocks == 32


def sum_over_space(gram, groups):
    if groups != 8:
        return [lax.psum(gram, "space")]
    swap = lambda x, k: lax.ppermute(x, "space", [(i, i ^ k) for i in range(groups)])
    gram = gram + swap(gram, 1)
    copies = jnp.broadcast_to(gram, (4,) + gram.shape)
    chips = [[0, 2, 4, 6], [1, 3, 5, 7]]
    copies = lax.all_to_all(copies, "space", 0, 0, axis_index_groups=chips, tiled=True)
    return [copies]


def chunks_of(points):
    tile = 512
    return [(at, tile) for at in range(0, points, tile)]


def ring_spectra(n, owned, slots, blocks, total, position, block_starts, frequencies, angles, mask, samples):
    span, points = samples.shape[1:]
    pieces = []
    shared = None
    for at, count in chunks_of(points):
        sums, shared = dft_call(
            n, owned, slots, blocks, shared is None, at, count,
            position, block_starts, frequencies, angles, mask, samples, shared,
        )
        moved = [sums[0]] + [
            lax.ppermute(sums[k], "tm", [(i, (i + k) % n) for i in range(n)]) for k in range(1, n)
        ]
        pieces.append((at, count, moved))

    spectra, gram = None, None
    for at, count, moved in pieces:
        last = at + count == points
        spectra, gram = assemble_call(
            n, owned, slots, span, blocks, total, at, count, points, position, moved, spectra, gram, last
        )
    return spectra, gram


def per_device(velocity, rotor_mask, rotor_angle, block_starts, frequencies):
    span, _, points = velocity.shape
    n = lax.axis_size("tm")
    groups = lax.axis_size("space")
    blocks = block_starts.shape[0]
    owned = frequencies.shape[0] // n
    order = 2 * blocks
    slots = slot_count(n, span, blocks, owned * 2)
    position = lax.axis_index("tm").astype(jnp.int32).reshape(1)
    samples = velocity.transpose(1, 0, 2)
    mask = rotor_mask.reshape(1, points)
    angles = rotor_angle

    total = COMPS * points * groups
    if fits_line(n, span, blocks, owned):
        spectra, gram = line_spectra(samples, mask, angles, block_starts, frequencies, position, total)
    else:
        spectra, gram = ring_spectra(
            n, owned, slots, blocks, total, position, block_starts, frequencies, angles, mask, samples
        )
    factors = factor_call(owned, order, sum_over_space(gram, groups))
    return spectra.transpose(0, 1, 3, 2, 4), factors


def solution(mesh):
    in_specs = (P("tm", None, "space"), P("space"), P("tm"), P(), P())
    out_specs = (P("tm", None, None, None, "space"), P("tm", None, None))
    return jax.shard_map(
        per_device, mesh=mesh, in_specs=in_specs, out_specs=out_specs, check_vma=False
    )
```

```python
import functools
import math

import jax
import jax.numpy as jnp
from jax import lax
from jax.experimental import pallas as pl
from jax.experimental.pallas import tpu as pltpu
from jax.sharding import PartitionSpec as P

COMPS = 3
NFFT = 256
JIT = 64
HOP = 128
LANES = 128
TILE = 256
PIVOT = 8
LIMIT_A, LIMIT_B, LIMIT_C = 60, 60, 40
SCALE = (8.0 / (3.0 * NFFT)) ** 0.5
HIGHEST = lax.Precision.HIGHEST
SHORT = pl.CostEstimate(flops=1000, bytes_accessed=1000, transcendentals=0)


def first_block(shard, span):
    return jnp.maximum((shard * span - (NFFT + JIT - 1) + HOP) // HOP, 0)


def slot_count(shards, span, blocks, rows_per_slot):
    most = 0
    for s in range(shards):
        lo = max((s * span - (NFFT + JIT - 1) + HOP) // HOP, 0)
        hi = min((span * (s + 1) - 1) // HOP, blocks - 1)
        most = max(most, hi - lo + 1)
    step = 16 // math.gcd(16, rows_per_slot)
    return -(-most // step) * step


def half_turn_sine(x):
    z = x * x
    c = [math.pi ** (2 * i + 1) * (-1) ** i / math.factorial(2 * i + 1) for i in range(7)]
    acc = jnp.full_like(z, c[-1])
    for term in c[-2::-1]:
        acc = acc * z + term
    return acc * x


def build_rows(n, owned, slots, span, blocks, me, starts_ref, freqs_ref, a_ref):
    group = owned * 2
    rid = lax.broadcasted_iota(jnp.int32, (n * group, 1), 0)
    k_of, j_of, r_of = rid // group, (rid // 2) % owned, rid % 2
    f_of = lax.rem(me + k_of, n) * owned + j_of
    freq = jnp.zeros((n * group, 1), jnp.float32)
    for f in range(n * owned):
        freq = jnp.where(f_of == f, freqs_ref[f].astype(jnp.float32), freq)
    step = freq * (1.0 / NFFT)
    quarter = r_of.astype(jnp.float32) * 0.25
    lo = first_block(me, span)
    sample = lax.broadcasted_iota(jnp.int32, (1, span), 1) + me * span
    pieces = [[] for _ in range(n)]
    for s in range(slots):
        b = lo + s
        start = starts_ref[jnp.minimum(b, blocks - 1)]
        ni = sample - start
        inside = (ni >= 0) & (ni < NFFT) & (b < blocks)
        nf = ni.astype(jnp.float32)
        w = half_turn_sine(jnp.minimum(nf, NFFT - nf) * (1.0 / NFFT))
        w = jnp.where(inside, w * w * SCALE, 0.0)
        nf = jnp.where(inside, nf, 0.0)
        turns = nf * step + quarter
        turns = turns - jnp.floor(turns + 0.5)
        h = half_turn_sine(turns)
        rows = w * (1.0 - 2.0 * h * h)
        for k in range(n):
            pieces[k].append(rows[k * group:(k + 1) * group])
    for k in range(n):
        a_ref[k] = jnp.concatenate(pieces[k], axis=0).astype(jnp.bfloat16)


def spread_column(row, span, out_ref):
    for at in range(0, span, LANES):
        width = min(LANES, span - at)
        part = row[:, at:at + width]
        if width < LANES:
            part = jnp.concatenate([part, jnp.zeros((1, LANES - width), jnp.float32)], axis=1)
        turned = jnp.transpose(jnp.broadcast_to(part, (LANES, LANES)))
        out_ref[at:at + width, :] = turned[:width]


def dft_body(n, owned, slots, span, blocks, first, *refs):
    if first:
        pos_ref, starts_ref, freqs_ref, angle_ref, mask_ref, vel_ref = refs[:6]
        outs = refs[6:6 + n]
        a_ref, cos_ref, sin_ref = refs[6 + n:9 + n]
        rot_ref = refs[9 + n]

        @pl.when(pl.program_id(0) == 0)
        def _():
            build_rows(n, owned, slots, span, blocks, pos_ref[0], starts_ref, freqs_ref, a_ref)
            spread_column(jnp.cos(angle_ref[...].reshape(1, span)), span, cos_ref)
            spread_column(jnp.sin(angle_ref[...].reshape(1, span)), span, sin_ref)
    else:
        mask_ref, vel_ref, a_ref, cos_ref, sin_ref = refs[:5]
        outs = refs[5:5 + n]
        rot_ref = refs[5 + n]
    width = vel_ref.shape[2]
    turning = mask_ref[...] == 1
    for at in range(0, span, 16):
        rows = min(16, span - at)
        here = pl.ds(at, rows)
        cosine = jnp.concatenate([cos_ref[here, :]] * (width // LANES), axis=1)
        sine = jnp.concatenate([sin_ref[here, :]] * (width // LANES), axis=1)
        x = vel_ref[0, here, :].astype(jnp.float32)
        y = vel_ref[1, here, :].astype(jnp.float32)
        rot_ref[0, here, :] = jnp.where(turning, cosine * x - sine * y, x).astype(jnp.bfloat16)
        rot_ref[1, here, :] = jnp.where(turning, sine * x + cosine * y, y).astype(jnp.bfloat16)
    rows = a_ref.shape[1]
    a = a_ref[...].reshape(n * rows, span)
    for c in range(COMPS):
        samples = rot_ref[c] if c < 2 else vel_ref[2]
        sums = jnp.dot(a, samples, preferred_element_type=jnp.float32).astype(jnp.bfloat16)
        for k in range(n):
            outs[k][c * rows:(c + 1) * rows, :] = sums[k * rows:(k + 1) * rows]


def dft_call(n, owned, slots, blocks, first, offset, points, position, starts, freqs, angles, mask, velocity, shared):
    span = velocity.shape[1]
    rows = slots * owned * 2
    shift = offset // TILE
    whole = lambda shape: pl.BlockSpec(shape, lambda i: (0,) * len(shape))
    smem = pl.BlockSpec(memory_space=pltpu.SMEM)
    data_specs = [
        pl.BlockSpec((1, TILE), lambda i: (0, i + shift)),
        pl.BlockSpec((COMPS, span, TILE), lambda i: (0, 0, i + shift)),
    ]
    shared_types = [
        jax.ShapeDtypeStruct((n, rows, span), jnp.bfloat16),
        jax.ShapeDtypeStruct((span, LANES), jnp.float32),
        jax.ShapeDtypeStruct((span, LANES), jnp.float32),
    ]
    shared_specs = [whole(t.shape) for t in shared_types]
    out_types = [jax.ShapeDtypeStruct((COMPS * rows, points), jnp.bfloat16)] * n
    out_specs = [pl.BlockSpec((COMPS * rows, TILE), lambda i: (0, i))] * n
    if first:
        args = (position, starts, freqs, angles, mask, velocity)
        in_specs = [smem] * 3 + [whole((span,))] + data_specs
        out_types = out_types + shared_types
        out_specs = out_specs + shared_specs
    else:
        args = (mask, velocity) + tuple(shared)
        in_specs = data_specs + shared_specs
    out = pl.pallas_call(
        functools.partial(dft_body, n, owned, slots, span, blocks, first),
        grid=(points // TILE,),
        out_shape=out_types,
        in_specs=in_specs,
        out_specs=out_specs,
        scratch_shapes=[pltpu.VMEM((2, span, TILE), jnp.bfloat16)],
        compiler_params=pltpu.CompilerParams(vmem_limit_bytes=40 * 2**20),
        cost_estimate=pl.CostEstimate(
            flops=2 * n * rows * span * COMPS * points,
            bytes_accessed=2 * COMPS * span * points,
            transcendentals=0,
        ),
        name="rotate_dft",
    )(*args)
    return out[:n], out[n:] if first else shared


def selection(n, owned, slots, span, blocks, me):
    rows = slots * owned * 2
    shape = (owned * 2 * blocks, n * rows)
    out = lax.broadcasted_iota(jnp.int32, shape, 0)
    col = lax.broadcasted_iota(jnp.int32, shape, 1)
    k_of = jnp.zeros(shape, jnp.int32)
    lo = jnp.broadcast_to(first_block(me, span), shape)
    for k in range(1, n):
        past = col >= k * rows
        k_of = jnp.where(past, k, k_of)
        lo = jnp.where(past, first_block(lax.rem(me + n - k, n), span), lo)
    rem = col - k_of * rows
    slot = rem // (owned * 2)
    same = (out // blocks == rem % (owned * 2)) & (out % blocks == lo + slot)
    return jnp.where(same, 1.0, 0.0)


def assemble_body(n, owned, slots, span, blocks, total, has_sum, last, *refs):
    pos_ref = refs[0]
    parts = refs[1:1 + n]
    rest = refs[1 + n:]
    if has_sum:
        sum_in, rest = rest[0], rest[2:]
    spectra_ref, gram_ref, sel_ref, acc_ref = rest
    step = pl.program_id(0)
    rows = slots * owned * 2

    @pl.when(step == 0)
    def _():
        sel_ref[...] = selection(n, owned, slots, span, blocks, pos_ref[0]).astype(jnp.bfloat16)
        acc_ref[...] = sum_in[...] if has_sum else jnp.zeros_like(acc_ref)

    for c in range(COMPS):
        stack = jnp.concatenate([p[c * rows:(c + 1) * rows, :] for p in parts], axis=0)
        full = jnp.dot(sel_ref[...], stack, preferred_element_type=jnp.float32)
        for j in range(owned):
            for r in range(2):
                at = (j * 2 + r) * blocks
                spectra_ref[j, r, c] = full[at:at + blocks]
        acc_ref[...] += lax.dot_general(
            stack, stack, (((1,), (1,)), ((), ())), preferred_element_type=jnp.float32
        )

    @pl.when(step == pl.num_programs(0) - 1)
    def _():
        if not last:
            gram_ref[...] = acc_ref[...]
        else:
            sel = sel_ref[...].astype(jnp.float32)
            half = jnp.dot(sel, acc_ref[...], precision=HIGHEST, preferred_element_type=jnp.float32)
            order = 2 * blocks
            gram = lax.dot_general(
                half, sel, (((1,), (1,)), ((), ())), precision=HIGHEST, preferred_element_type=jnp.float32
            ) * (1.0 / total)
            gram_ref[...] = jnp.concatenate(
                [gram[j * order:(j + 1) * order, j * order:(j + 1) * order] for j in range(owned)], axis=1
            )


def assemble_call(n, owned, slots, span, blocks, total, offset, points, all_points, position, parts, spectra, gram, last):
    rows = slots * owned * 2
    tile = min(points, 512)
    shift = offset // tile
    order = 2 * blocks
    has_sum = gram is not None
    whole = lambda shape: pl.BlockSpec(shape, lambda i: (0,) * len(shape))
    gram_shape = (order, owned * order) if last else (n * rows, n * rows)
    args = [position] + list(parts)
    in_specs = [pl.BlockSpec(memory_space=pltpu.SMEM)] + [pl.BlockSpec((COMPS * rows, tile), lambda i: (0, i))] * n
    aliases = {}
    if has_sum:
        args += [gram, spectra]
        in_specs += [whole((n * rows, n * rows)), pl.BlockSpec(memory_space=pl.ANY)]
        aliases = {len(args) - 1: 0}
    return pl.pallas_call(
        functools.partial(assemble_body, n, owned, slots, span, blocks, total, has_sum, last),
        grid=(points // tile,),
        out_shape=[
            jax.ShapeDtypeStruct((owned, 2, COMPS, blocks, all_points), jnp.float32),
            jax.ShapeDtypeStruct(gram_shape, jnp.float32),
        ],
        in_specs=in_specs,
        out_specs=[
            pl.BlockSpec((owned, 2, COMPS, blocks, tile), lambda i: (0, 0, 0, 0, i + shift)),
            whole(gram_shape),
        ],
        scratch_shapes=[
            pltpu.VMEM((owned * order, n * rows), jnp.bfloat16),
            pltpu.VMEM((n * rows, n * rows), jnp.float32),
        ],
        input_output_aliases=aliases,
        compiler_params=pltpu.CompilerParams(vmem_limit_bytes=40 * 2**20),
        cost_estimate=pl.CostEstimate(
            flops=4 * (n * rows) ** 2 * COMPS * points,
            bytes_accessed=4 * owned * order * COMPS * points,
            transcendentals=0,
        ),
        name="assemble",
    )(*args)


def factor_body(owned, order, count, *refs):
    parts = refs[:count]
    out_ref, row_ref = refs[count:]
    s = [p[...] for p in parts]
    while len(s) > 1:
        s = [a + b for a, b in zip(s[::2], s[1::2])]
    s = s[0]
    lane = lax.broadcasted_iota(jnp.int32, (1, owned * order), 1)
    for k in range(0, order, PIVOT):
        base = k // 8 * 8
        s = s[base - max(k - PIVOT, 0) // 8 * 8:]
        columns = []
        for i in range(k, k + PIVOT):
            column = jnp.broadcast_to(s[:, i:i + 1], s.shape)
            for j in range(1, owned):
                column = jnp.where(lane >= j * order, s[:, j * order + i:j * order + i + 1], column)
            columns.append(column)
        at = k - base
        rows = [s[at + i:at + i + 1] for i in range(PIVOT)]
        for i in range(PIVOT):
            inverse_root = lax.rsqrt(columns[i][at + i:at + i + 1])
            columns[i] = columns[i] * inverse_root
            rows[i] = rows[i] * inverse_root
            for j in range(i + 1, PIVOT):
                weight = columns[i][at + j:at + j + 1]
                columns[j] = columns[j] - columns[i] * weight
                rows[j] = rows[j] - rows[i] * weight
            row_ref[k + i:k + i + 1, :] = jnp.where(lane % order >= k + i, rows[i], 0.0)
            s = s - columns[i] * rows[i]
    for j in range(owned):
        out_ref[j] = row_ref[:, j * order:(j + 1) * order]


def factor_call(owned, order, parts):
    return pl.pallas_call(
        functools.partial(factor_body, owned, order, len(parts)),
        out_shape=jax.ShapeDtypeStruct((owned, order, order), jnp.float32),
        scratch_shapes=[pltpu.VMEM((order, owned * order), jnp.float32)],
        name="factor",
    )(*parts)


LINE_LO = [0, 6, 15, 23]
LINE_HI = [8, 16, 25, 31]
WIDE = 12
FAR = 9
SHARED = 2
REACH = 144


def pick(values, me):
    out = jnp.int32(values[0])
    for i in range(1, len(values)):
        out = jnp.where(me == i, jnp.int32(values[i]), out)
    return out


def far_block(shard, slot):
    return pick([0, 8, 23, 31], shard) + pick([1, 1, -1, -1], shard) * slot


def cosine_of(turns):
    s = half_turn_sine(turns - jnp.floor(turns + 0.5))
    return 1.0 - 2.0 * s * s


def build_line(span, blocks, me, starts_ref, freqs_ref, a_ref, rows_ref):
    lo = pick(LINE_LO, me)
    starts = [starts_ref[jnp.minimum(lo + s, blocks - 1)] for s in range(WIDE)]

    def by_slot(shape, axis):
        at = lax.broadcasted_iota(jnp.int32, shape, axis)
        out = jnp.full(shape, starts[0], jnp.int32)
        for s in range(1, WIDE):
            out = jnp.where(at == s, starts[s], out)
        return out

    rid = lax.broadcasted_iota(jnp.int32, (16, 1), 0)
    f_of = ((rid // 4) ^ me) * 2 + (rid // 2) % 2
    freq = jnp.zeros((16, 1), jnp.float32)
    for f in range(8):
        freq = jnp.where(f_of == f, freqs_ref[f].astype(jnp.float32), freq)
    step = freq * (1.0 / NFFT)
    quarter = (rid % 2).astype(jnp.float32) * 0.25

    sample = lax.broadcasted_iota(jnp.int32, (1, span), 1) + me * span
    turns = sample.astype(jnp.float32) * step
    turns = turns - jnp.floor(turns) + quarter
    cos_t, sin_t = cosine_of(turns), cosine_of(turns - 0.25)
    begin = by_slot((1, LANES), 1).astype(jnp.float32) * step
    begin = begin - jnp.floor(begin)
    cos_b, sin_b = cosine_of(begin), cosine_of(begin - 0.25)

    slot = lax.broadcasted_iota(jnp.int32, (16, 1), 0)
    ni = sample - by_slot((16, 1), 0)
    nf = ni.astype(jnp.float32)
    w = half_turn_sine(jnp.minimum(nf, NFFT - nf) * (1.0 / NFFT))
    w = jnp.where((ni >= 0) & (ni < NFFT) & (slot + lo < blocks), w * w * SCALE, 0.0)

    own, near = [], []
    for s in range(WIDE):
        rows = (cos_t * cos_b[:, s:s + 1] + sin_t * sin_b[:, s:s + 1]) * w[s:s + 1]
        rows_ref[s] = rows[8:]
        own.append(rows[:4])
        near.append(rows[4:8])
    far = [rows_ref[far_block(me, s) - lo] for s in range(FAR)]
    pieces = own + near
    pieces += [r[:4] for r in far[:-1]] + [r[4:] for r in far[:-1]]
    pieces += [far[-1], jnp.zeros((8, span), jnp.float32)]
    a_ref[...] = jnp.concatenate(pieces, axis=0).astype(jnp.bfloat16)


def rotate(turning, cosine, sine, x, y):
    width = x.shape[1]
    cosine = jnp.concatenate([cosine] * (width // LANES), axis=1)
    sine = jnp.concatenate([sine] * (width // LANES), axis=1)
    x, y = x.astype(jnp.float32), y.astype(jnp.float32)
    new_x = jnp.where(turning, cosine * x - sine * y, x)
    new_y = jnp.where(turning, sine * x + cosine * y, y)
    return new_x.astype(jnp.bfloat16), new_y.astype(jnp.bfloat16)


def shared_rows(begin, me, starts_ref, freqs_ref):
    rid = lax.broadcasted_iota(jnp.int32, (16, 1), 0)
    f_of = jnp.where(rid < 8, me ^ 3, me ^ 2) * 2 + (rid // 2) % 2
    freq = jnp.zeros((16, 1), jnp.float32)
    for f in range(8):
        freq = jnp.where(f_of == f, freqs_ref[f].astype(jnp.float32), freq)
    first, second = (starts_ref[pick([0, 6 + s, 25 - s, 0], me)] for s in range(SHARED))
    start = jnp.where((rid // 4) % 2 == 0, first, second)
    ni = lax.broadcasted_iota(jnp.int32, (1, REACH), 1) + begin - start
    nf = ni.astype(jnp.float32)
    w = half_turn_sine(jnp.minimum(nf, NFFT - nf) * (1.0 / NFFT))
    inner = (me == 1) | (me == 2)
    w = jnp.where((ni >= 0) & (ni < NFFT) & inner, w * w * SCALE, 0.0)
    turns = nf * (freq * (1.0 / NFFT)) + (rid % 2).astype(jnp.float32) * 0.25
    return (cosine_of(turns) * w).astype(jnp.bfloat16)


def prepare_body(span, blocks, pos_ref, starts_ref, freqs_ref, angle_ref, mask_ref, all_hbm,
                 part_ref, a_ref, cos_ref, sin_ref, rows_ref, ends_ref, ends_rot_ref, ends_sem):
    me = pos_ref[0]
    begin = pl.multiple_of(jnp.where(me == 2, span - REACH, 0), 16)
    load = pltpu.make_async_copy(all_hbm.at[:, pl.ds(begin, REACH), :], ends_ref, ends_sem)
    load.start()
    build_line(span, blocks, me, starts_ref, freqs_ref, a_ref, rows_ref)
    spread_column(jnp.cos(angle_ref[...].reshape(1, span)), span, cos_ref)
    spread_column(jnp.sin(angle_ref[...].reshape(1, span)), span, sin_ref)
    rows = shared_rows(begin + me * span, me, starts_ref, freqs_ref)
    load.wait()
    for lane in range(0, part_ref.shape[1], TILE):
        here = slice(lane, lane + TILE)
        turning = mask_ref[:, here] == 1
        for at in range(0, REACH, 16):
            row = slice(at, at + 16)
            t = pl.ds(pl.multiple_of(begin + at, 16), 16)
            new_x, new_y = rotate(
                turning, cos_ref[t, :], sin_ref[t, :], ends_ref[0, row, here], ends_ref[1, row, here]
            )
            ends_rot_ref[0, row, here] = new_x
            ends_rot_ref[1, row, here] = new_y
        for c in range(COMPS):
            samples = ends_rot_ref[c, :, here] if c < 2 else ends_ref[2, :, here]
            sums = jnp.dot(rows, samples, preferred_element_type=jnp.float32)
            part_ref[16 * c:16 * c + 16, here] = sums.astype(jnp.bfloat16)


def prepare(blocks, position, starts, freqs, angles, mask, velocity):
    span, points = velocity.shape[1:]
    smem, vmem, anywhere = (pl.BlockSpec(memory_space=m) for m in (pltpu.SMEM, pltpu.VMEM, pl.ANY))
    whole = lambda shape: pl.BlockSpec(shape, lambda i: (0,) * len(shape))
    types = [
        jax.ShapeDtypeStruct((48, points), jnp.bfloat16),
        jax.ShapeDtypeStruct((176, span), jnp.bfloat16),
        jax.ShapeDtypeStruct((span, LANES), jnp.float32),
        jax.ShapeDtypeStruct((span, LANES), jnp.float32),
    ]
    return pl.pallas_call(
        functools.partial(prepare_body, span, blocks),
        grid=(1,),
        out_shape=types,
        in_specs=[smem] * 3 + [whole((span,)), whole((1, points)), anywhere],
        out_specs=[whole(t.shape) for t in types],
        scratch_shapes=[
            pltpu.VMEM((WIDE, 8, span), jnp.float32),
            pltpu.VMEM((COMPS, REACH, points), jnp.bfloat16),
            pltpu.VMEM((2, REACH, points), jnp.bfloat16),
            pltpu.SemaphoreType.DMA,
        ],
        compiler_params=pltpu.CompilerParams(vmem_limit_bytes=LIMIT_A * 2**20),
        cost_estimate=pl.CostEstimate(flops=10**9, bytes_accessed=4 * 10**6, transcendentals=0),
        name="prepare",
    )(position, starts, freqs, angles, mask, velocity)


def line_dft_body(span, has_part, *refs):
    mask_ref, vel_ref, a_ref, cos_ref, sin_ref = refs[:5]
    own_ref, near_ref, far2_ref, far3_ref, rot_ref = refs[-5:]
    part_ref = refs[5] if has_part else None
    width = vel_ref.shape[2]
    none = jnp.zeros((24, width), jnp.float32)
    tails = [None] * COMPS

    def send(c, samples):
        sums = jnp.dot(a_ref[...], samples, preferred_element_type=jnp.float32)
        own_ref[48 * c:48 * c + 48, :] = sums[:48].astype(jnp.bfloat16)
        near_ref[48 * c:48 * c + 48, :] = sums[48:96].astype(jnp.bfloat16)
        far2, far3 = sums[96:128], sums[128:160]
        if has_part:
            part = part_ref[16 * c:16 * c + 16, :].astype(jnp.float32)
            far2 = far2 + jnp.concatenate([none, part[:8]], axis=0)
            far3 = far3 + jnp.concatenate([none, part[8:]], axis=0)
        far2_ref[32 * c:32 * c + 32, :] = far2.astype(jnp.bfloat16)
        far3_ref[32 * c:32 * c + 32, :] = far3.astype(jnp.bfloat16)
        tails[c] = sums[160:168]

    send(2, vel_ref[2])
    turning = mask_ref[...] == 1
    for at in range(0, span, 16):
        here = pl.ds(at, min(16, span - at))
        new_x, new_y = rotate(turning, cos_ref[here, :], sin_ref[here, :], vel_ref[0, here, :], vel_ref[1, here, :])
        rot_ref[0, here, :] = new_x
        rot_ref[1, here, :] = new_y
    send(0, rot_ref[0])
    send(1, rot_ref[1])
    far2_ref[96:112, :] = jnp.concatenate([t[:4] for t in tails] + [none[:4]], axis=0).astype(jnp.bfloat16)
    far3_ref[96:112, :] = jnp.concatenate([t[4:] for t in tails] + [none[:4]], axis=0).astype(jnp.bfloat16)


def line_dft(offset, points, mask, velocity, rows, cosine, sine, part, after):
    span = velocity.shape[1]
    shift = offset // TILE
    whole = lambda shape: pl.BlockSpec(shape, lambda i: (0,) * len(shape))
    args = [mask, velocity, rows, cosine, sine]
    in_specs = [
        pl.BlockSpec((1, TILE), lambda i: (0, i + shift)),
        pl.BlockSpec((COMPS, span, TILE), lambda i: (0, 0, i + shift)),
    ] + [whole(x.shape) for x in args[2:]]
    if part is not None:
        args.append(part)
        in_specs.append(pl.BlockSpec((48, TILE), lambda i: (0, i + shift)))
    if after is not None:
        args.append(after)
        in_specs.append(pl.BlockSpec(memory_space=pl.ANY))
    heights = [144, 144, 112, 112]
    return pl.pallas_call(
        functools.partial(line_dft_body, span, part is not None),
        grid=(points // TILE,),
        out_shape=[jax.ShapeDtypeStruct((h, points), jnp.bfloat16) for h in heights],
        in_specs=in_specs,
        out_specs=[pl.BlockSpec((h, TILE), lambda i: (0, i)) for h in heights],
        scratch_shapes=[pltpu.VMEM((2, span, TILE), jnp.bfloat16)],
        compiler_params=pltpu.CompilerParams(vmem_limit_bytes=LIMIT_B * 2**20),
        cost_estimate=pl.CostEstimate(
            flops=2 * 192 * span * COMPS * points, bytes_accessed=2 * COMPS * span * points, transcendentals=0
        ),
        name="rotate_dft",
    )(*args)


def combine_body(far2_ref, far3_ref, part_ref, out2_ref, out3_ref):
    for c in range(COMPS):
        here = slice(32 * c, 32 * c + 32)
        add = part_ref[16 * c:16 * c + 16, :].astype(jnp.float32)
        none = jnp.zeros((24, add.shape[1]), jnp.float32)
        for src, dst, part in ((far2_ref, out2_ref, add[:8]), (far3_ref, out3_ref, add[8:])):
            dst[here, :] = (src[here, :].astype(jnp.float32) + jnp.concatenate([none, part], axis=0)).astype(jnp.bfloat16)
    out2_ref[96:112, :] = far2_ref[96:112, :]
    out3_ref[96:112, :] = far3_ref[96:112, :]


def combine(far2, far3, part):
    spec = pl.BlockSpec(far2.shape, lambda i: (0, 0))
    return pl.pallas_call(
        combine_body,
        grid=(1,),
        out_shape=[jax.ShapeDtypeStruct(far2.shape, far2.dtype)] * 2,
        in_specs=[spec, spec, pl.BlockSpec((48, far2.shape[1]), lambda i: (0, 0))],
        out_specs=[spec, spec],
        compiler_params=pltpu.CompilerParams(vmem_limit_bytes=LIMIT_B * 2**20),
        cost_estimate=pl.CostEstimate(flops=far2.size, bytes_accessed=8 * far2.size, transcendentals=0),
        name="add_shared",
    )(far2, far3, part)


def line_selection(blocks, me, sel_ref):
    shape = (4 * blocks, 192)
    out = lax.broadcasted_iota(jnp.int32, shape, 0)
    col = lax.broadcasted_iota(jnp.int32, shape, 1)
    two, three = me ^ 2, me ^ 3
    block = jnp.where(col < 48, pick(LINE_LO, me) + col // 4, pick(LINE_LO, me ^ 1) + (col - 48) // 4)
    block = jnp.where(col >= 96, far_block(two, (col - 96) // 4), block)
    block = jnp.where(col >= 128, far_block(three, (col - 128) // 4), block)
    block = jnp.where(col >= 160, far_block(two, FAR - 1), block)
    block = jnp.where(col >= 176, far_block(three, FAR - 1), block)
    same = (out // blocks == col % 4) & (out % blocks == block)
    for c in range(COMPS):
        mine = same & ((col < 160) | ((col % 16) // 4 == c))
        sel_ref[c] = jnp.where(mine, 1.0, 0.0).astype(jnp.bfloat16)


def line_assemble_body(blocks, total, has_sum, last, has_carry, *refs):
    pos_ref, own_ref, near_ref, far2_ref, far3_ref = refs[:5]
    *refs, acc_ref = refs
    if has_carry:
        *refs, carry_out_ref = refs
    if has_sum:
        sum_in, sel_ref = refs[5:7]
        spectra_ref, gram_ref = refs[-2:]
    else:
        spectra_ref, gram_ref, sel_ref = refs[-3:]
    if has_carry:
        carry_ref = refs[8 if has_sum else 5]
    step = pl.program_id(0)

    @pl.when(step == 0)
    def _():
        if not has_sum:
            line_selection(blocks, pos_ref[0], sel_ref)
        acc_ref[...] = sum_in[...] if has_sum else jnp.zeros_like(acc_ref)
        if has_carry:
            carry_out_ref[...] = carry_ref[...]

    for c in range(COMPS):
        wide = slice(48 * c, 48 * c + 48)
        here = slice(32 * c, 32 * c + 32)
        parts = [
            own_ref[wide, :], near_ref[wide, :],
            far2_ref[here, :], far3_ref[here, :], far2_ref[96:112, :], far3_ref[96:112, :],
        ]
        stack = jnp.concatenate(parts, axis=0)
        full = jnp.dot(sel_ref[c], stack, preferred_element_type=jnp.float32)
        for jr in range(4):
            spectra_ref[jr // 2, jr % 2, c] = full[jr * blocks:(jr + 1) * blocks]
        high = full.astype(jnp.bfloat16)
        low = (full - high.astype(jnp.float32)).astype(jnp.bfloat16)
        pair = jnp.concatenate([high, low], axis=0)
        acc_ref[...] += lax.dot_general(
            pair, pair, (((1,), (1,)), ((), ())), preferred_element_type=jnp.float32
        )

    @pl.when(step == pl.num_programs(0) - 1)
    def _():
        if not last:
            gram_ref[...] = acc_ref[...]
        else:
            n = 4 * blocks
            order = 2 * blocks
            acc = acc_ref[...]
            gram = (acc[:n, :n] + (acc[:n, n:] + acc[n:, :n])) * (1.0 / total)
            gram_ref[...] = jnp.concatenate([gram[:order, :order], gram[order:, order:]], axis=1)


def line_assemble(blocks, total, offset, points, all_points, position, own, near, fars, spectra, gram, sel, last, carry):
    shift = offset // TILE
    order = 2 * blocks
    has_sum = gram is not None
    whole = lambda shape: pl.BlockSpec(shape, lambda i: (0,) * len(shape))
    gram_shape = (order, 2 * order) if last else (4 * order, 4 * order)
    args = [position, own, near] + list(fars)
    in_specs = [pl.BlockSpec(memory_space=pltpu.SMEM)]
    in_specs += [pl.BlockSpec((a.shape[0], TILE), lambda i: (0, i)) for a in args[1:]]
    aliases = {}
    if has_sum:
        args += [gram, sel, spectra]
        in_specs += [whole(gram.shape), whole(sel.shape), pl.BlockSpec(memory_space=pl.ANY)]
        aliases = {len(args) - 1: 0}
    if carry is not None:
        args.append(carry)
        in_specs.append(whole(carry.shape))
    out_shape = [
        jax.ShapeDtypeStruct((2, 2, COMPS, blocks, all_points), jnp.float32),
        jax.ShapeDtypeStruct(gram_shape, jnp.float32),
    ]
    out_specs = [
        pl.BlockSpec((2, 2, COMPS, blocks, TILE), lambda i: (0, 0, 0, 0, i + shift)),
        whole(gram_shape),
    ]
    if not has_sum:
        out_shape.append(jax.ShapeDtypeStruct((COMPS, 4 * blocks, 192), jnp.bfloat16))
        out_specs.append(whole((COMPS, 4 * blocks, 192)))
    if carry is not None:
        out_shape.append(jax.ShapeDtypeStruct(carry.shape, carry.dtype))
        out_specs.append(whole(carry.shape))
    out = pl.pallas_call(
        functools.partial(line_assemble_body, blocks, total, has_sum, last, carry is not None),
        grid=(points // TILE,),
        out_shape=out_shape,
        in_specs=in_specs,
        out_specs=out_specs,
        scratch_shapes=[pltpu.VMEM((4 * order, 4 * order), jnp.float32)],
        input_output_aliases=aliases,
        compiler_params=pltpu.CompilerParams(vmem_limit_bytes=LIMIT_C * 2**20),
        cost_estimate=pl.CostEstimate(
            flops=4 * 256 * 256 * COMPS * points, bytes_accessed=8 * order * COMPS * points, transcendentals=0
        ),
        name="assemble",
    )(*args)
    return list(out[:2]) + [sel if has_sum else out[2], out[-1]]


def line_chunks(points):
    cuts = [points * k // 8 for k in (0, 3, 6, 8)]
    return [(a, b - a) for a, b in zip(cuts[:-1], cuts[1:])]


def line_spectra(samples, mask, angles, block_starts, frequencies, position, total):
    points = samples.shape[2]
    blocks = block_starts.shape[0]
    move = lambda x, pairs: lax.ppermute(x, "tm", pairs)
    across = lambda x, k: move(x, [(i, i ^ k) for i in range(4)])
    part, rows, cosine, sine = prepare(blocks, position, block_starts, frequencies, angles, mask, samples)
    part = move(part, [(1, 0), (2, 3)])
    spectra, gram, sel, added = None, None, None, None
    sent = []

    def assemble(carry):
        at, count, own, near, fars = sent.pop(0)
        return line_assemble(
            blocks, total, at, count, points, position, own, across(near, 1), fars,
            spectra, gram, sel, at + count == points, carry,
        )

    for i, (at, count) in enumerate(line_chunks(points)):
        if i >= 2:
            spectra, gram, sel, _ = assemble(None)

        wait = gram if i >= 2 else added
        own, near, far2, far3 = line_dft(at, count, mask, samples, rows, cosine, sine, part if i else None, wait)
        if i == 0:
            far2, far3 = combine(far2, far3, part)
            added = far2
        sent.append([at, count, own, near, [across(far2, 2), across(far3, 3)]])
    while sent:
        spectra, gram, sel, _ = assemble(None)
    return spectra, gram


def fits_line(n, span, blocks, owned):
    if n != 4 or owned != 2:
        return False
    lo = [max((s * span - (NFFT + JIT - 1) + HOP) // HOP, 0) for s in range(n)]
    hi = [min((span * (s + 1) - 1) // HOP, blocks - 1) for s in range(n)]
    return lo == LINE_LO and hi == LINE_HI and blocks == 32


def sum_over_space(gram, groups):
    if groups != 8:
        return [lax.psum(gram, "space")]
    swap = lambda x, k: lax.ppermute(x, "space", [(i, i ^ k) for i in range(groups)])
    gram = gram + swap(gram, 1)
    side = [(i, i ^ (4 if i % 2 else 2)) for i in range(groups)]
    corner = [(i, i ^ 6) for i in range(1, groups, 2)]
    beside, across = lax.ppermute(gram, "space", side), lax.ppermute(gram, "space", corner)
    half = beside + jnp.where(lax.axis_index("space") % 2 == 0, gram, across)
    return [half, swap(half, 1)]


def chunks_of(points):
    tile = 512
    return [(at, tile) for at in range(0, points, tile)]


def ring_spectra(n, owned, slots, blocks, total, position, block_starts, frequencies, angles, mask, samples):
    span, points = samples.shape[1:]
    pieces = []
    shared = None
    for at, count in chunks_of(points):
        sums, shared = dft_call(
            n, owned, slots, blocks, shared is None, at, count,
            position, block_starts, frequencies, angles, mask, samples, shared,
        )
        moved = [sums[0]] + [
            lax.ppermute(sums[k], "tm", [(i, (i + k) % n) for i in range(n)]) for k in range(1, n)
        ]
        pieces.append((at, count, moved))

    spectra, gram = None, None
    for at, count, moved in pieces:
        last = at + count == points
        spectra, gram = assemble_call(
            n, owned, slots, span, blocks, total, at, count, points, position, moved, spectra, gram, last
        )
    return spectra, gram


def per_device(velocity, rotor_mask, rotor_angle, block_starts, frequencies):
    span, _, points = velocity.shape
    n = lax.axis_size("tm")
    groups = lax.axis_size("space")
    blocks = block_starts.shape[0]
    owned = frequencies.shape[0] // n
    order = 2 * blocks
    slots = slot_count(n, span, blocks, owned * 2)
    position = lax.axis_index("tm").astype(jnp.int32).reshape(1)
    samples = velocity.transpose(1, 0, 2)
    mask = rotor_mask.reshape(1, points)
    angles = rotor_angle

    total = COMPS * points * groups
    if fits_line(n, span, blocks, owned):
        spectra, gram = line_spectra(samples, mask, angles, block_starts, frequencies, position, total)
    else:
        spectra, gram = ring_spectra(
            n, owned, slots, blocks, total, position, block_starts, frequencies, angles, mask, samples
        )
    factors = factor_call(owned, order, sum_over_space(gram, groups))
    return spectra.transpose(0, 1, 3, 2, 4), factors


def solution(mesh):
    in_specs = (P("tm", None, "space"), P("space"), P("tm"), P(), P())
    out_specs = (P("tm", None, None, None, "space"), P("tm", None, None))
    return jax.shard_map(
        per_device, mesh=mesh, in_specs=in_specs, out_specs=out_specs, check_vma=False
    )
```

```python
import functools
import math

import jax
import jax.numpy as jnp
from jax import lax
from jax.experimental import pallas as pl
from jax.experimental.pallas import tpu as pltpu
from jax.sharding import PartitionSpec as P

COMPS = 3
NFFT = 256
JIT = 64
HOP = 128
LANES = 128
TILE = 256
PIVOT = 8
SCALE = (8.0 / (3.0 * NFFT)) ** 0.5
HIGHEST = lax.Precision.HIGHEST


def first_block(shard, span):
    return jnp.maximum((shard * span - (NFFT + JIT - 1) + HOP) // HOP, 0)


def slot_count(shards, span, blocks):
    most = 0
    for s in range(shards):
        lo = max((s * span - (NFFT + JIT - 1) + HOP) // HOP, 0)
        hi = min((span * (s + 1) - 1) // HOP, blocks - 1)
        most = max(most, hi - lo + 1)
    return most


def half_turn_sine(x):
    z = x * x
    c = [math.pi ** (2 * i + 1) * (-1) ** i / math.factorial(2 * i + 1) for i in range(7)]
    acc = jnp.full_like(z, c[-1])
    for term in c[-2::-1]:
        acc = acc * z + term
    return acc * x


def layout(rows):
    main = rows // 16 * 16
    return main, rows - main, -(-COMPS * rows // 8) * 8


def cosine_of(turns):
    s = half_turn_sine(turns - jnp.floor(turns + 0.5))
    return 1.0 - 2.0 * s * s


def build_rows(n, owned, slots, span, blocks, me, starts_ref, freqs_ref, a_ref):
    group = owned * 2
    lo = first_block(me, span)
    starts = [starts_ref[jnp.minimum(lo + s, blocks - 1)] for s in range(slots)]

    def by_slot(shape, axis):
        at = lax.broadcasted_iota(jnp.int32, shape, axis)
        out = jnp.full(shape, starts[0], jnp.int32)
        for s in range(1, slots):
            out = jnp.where(at == s, starts[s], out)
        return out

    rid = lax.broadcasted_iota(jnp.int32, (n * group, 1), 0)
    f_of = lax.rem(me + rid // group, n) * owned + (rid // 2) % owned
    freq = jnp.zeros((n * group, 1), jnp.float32)
    for f in range(n * owned):
        freq = jnp.where(f_of == f, freqs_ref[f].astype(jnp.float32), freq)
    step = freq * (1.0 / NFFT)
    quarter = (rid % 2).astype(jnp.float32) * 0.25

    sample = lax.broadcasted_iota(jnp.int32, (1, span), 1) + me * span
    turns = sample.astype(jnp.float32) * step
    turns = turns - jnp.floor(turns) + quarter
    cos_t, sin_t = cosine_of(turns), cosine_of(turns - 0.25)
    begin = by_slot((1, LANES), 1).astype(jnp.float32) * step
    begin = begin - jnp.floor(begin)
    cos_b, sin_b = cosine_of(begin), cosine_of(begin - 0.25)

    slot = lax.broadcasted_iota(jnp.int32, (16, 1), 0)
    ni = sample - by_slot((16, 1), 0)
    nf = ni.astype(jnp.float32)
    w = half_turn_sine(jnp.minimum(nf, NFFT - nf) * (1.0 / NFFT))
    w = jnp.where((ni >= 0) & (ni < NFFT) & (slot + lo < blocks), w * w * SCALE, 0.0)

    pieces = [[] for _ in range(n)]
    for s in range(slots):
        rows = (cos_t * cos_b[:, s:s + 1] + sin_t * sin_b[:, s:s + 1]) * w[s:s + 1]
        for k in range(n):
            pieces[k].append(rows[k * group:(k + 1) * group])
    padding = a_ref.shape[1] - slots * group
    for k in range(n):
        if padding:
            pieces[k].append(jnp.zeros((padding, span), jnp.float32))
        a_ref[k] = jnp.concatenate(pieces[k], axis=0).astype(jnp.bfloat16)


def spread_column(row, span, out_ref):
    for at in range(0, span, LANES):
        width = min(LANES, span - at)
        part = row[:, at:at + width]
        if width < LANES:
            part = jnp.concatenate([part, jnp.zeros((1, LANES - width), jnp.float32)], axis=1)
        turned = jnp.transpose(jnp.broadcast_to(part, (LANES, LANES)))
        out_ref[at:at + width, :] = turned[:width]


def dft_body(n, owned, slots, span, blocks, first, *refs):
    if first:
        pos_ref, starts_ref, freqs_ref, angle_ref, mask_ref, vel_ref = refs[:6]
        outs = refs[6:6 + n]
        a_ref, cos_ref, sin_ref = refs[6 + n:9 + n]
        rot_ref = refs[9 + n]

        @pl.when(pl.program_id(0) == 0)
        def _():
            build_rows(n, owned, slots, span, blocks, pos_ref[0], starts_ref, freqs_ref, a_ref)
            spread_column(jnp.cos(angle_ref[...].reshape(1, span)), span, cos_ref)
            spread_column(jnp.sin(angle_ref[...].reshape(1, span)), span, sin_ref)
    else:
        mask_ref, vel_ref, a_ref, cos_ref, sin_ref = refs[:5]
        outs = refs[5:5 + n]
        rot_ref = refs[5 + n]
    width = vel_ref.shape[2]
    turning = mask_ref[...] == 1
    for at in range(0, span, 16):
        rows = min(16, span - at)
        here = pl.ds(at, rows)
        cosine = jnp.concatenate([cos_ref[here, :]] * (width // LANES), axis=1)
        sine = jnp.concatenate([sin_ref[here, :]] * (width // LANES), axis=1)
        x = vel_ref[0, here, :].astype(jnp.float32)
        y = vel_ref[1, here, :].astype(jnp.float32)
        rot_ref[0, here, :] = jnp.where(turning, cosine * x - sine * y, x).astype(jnp.bfloat16)
        rot_ref[1, here, :] = jnp.where(turning, sine * x + cosine * y, y).astype(jnp.bfloat16)
    rows = a_ref.shape[1]
    main, tail, height = layout(slots * owned * 2)
    a = a_ref[...].reshape(n * rows, span)
    tails = []
    for c in range(COMPS):
        samples = rot_ref[c] if c < 2 else vel_ref[2]
        sums = jnp.dot(a, samples, preferred_element_type=jnp.float32)
        outs[0][c * rows:(c + 1) * rows, :] = sums[:rows].astype(jnp.bfloat16)
        if main:
            for k in range(1, n):
                outs[k][c * main:(c + 1) * main, :] = sums[k * rows:k * rows + main].astype(jnp.bfloat16)
        tails.append(sums)
    if height > COMPS * main:
        for k in range(1, n):
            parts = [t[k * rows + main:k * rows + main + tail] for t in tails] if tail else []
            padding = height - COMPS * (main + tail)
            if padding:
                parts.append(jnp.zeros((padding, width), jnp.float32))
            outs[k][COMPS * main:, :] = jnp.concatenate(parts, axis=0).astype(jnp.bfloat16)


def dft_call(n, owned, slots, blocks, first, offset, points, position, starts, freqs, angles, mask, velocity, shared):
    span = velocity.shape[1]
    rows = -(-slots * owned * 2 // 16) * 16
    heights = [COMPS * rows] + [layout(slots * owned * 2)[2]] * (n - 1)
    shift = offset // TILE
    whole = lambda shape: pl.BlockSpec(shape, lambda i: (0,) * len(shape))
    smem = pl.BlockSpec(memory_space=pltpu.SMEM)
    data_specs = [
        pl.BlockSpec((1, TILE), lambda i: (0, i + shift)),
        pl.BlockSpec((COMPS, span, TILE), lambda i: (0, 0, i + shift)),
    ]
    shared_types = [
        jax.ShapeDtypeStruct((n, rows, span), jnp.bfloat16),
        jax.ShapeDtypeStruct((span, LANES), jnp.float32),
        jax.ShapeDtypeStruct((span, LANES), jnp.float32),
    ]
    shared_specs = [whole(t.shape) for t in shared_types]
    out_types = [jax.ShapeDtypeStruct((h, points), jnp.bfloat16) for h in heights]
    out_specs = [pl.BlockSpec((h, TILE), lambda i: (0, i)) for h in heights]
    if first:
        args = (position, starts, freqs, angles, mask, velocity)
        in_specs = [smem] * 3 + [whole((span,))] + data_specs
        out_types = out_types + shared_types
        out_specs = out_specs + shared_specs
    else:
        args = (mask, velocity) + tuple(shared)
        in_specs = data_specs + shared_specs
    out = pl.pallas_call(
        functools.partial(dft_body, n, owned, slots, span, blocks, first),
        grid=(points // TILE,),
        out_shape=out_types,
        in_specs=in_specs,
        out_specs=out_specs,
        scratch_shapes=[pltpu.VMEM((2, span, TILE), jnp.bfloat16)],
        compiler_params=pltpu.CompilerParams(vmem_limit_bytes=(60 if first else 40) * 2**20),
        cost_estimate=pl.CostEstimate(
            flops=2 * n * rows * span * COMPS * points,
            bytes_accessed=2 * COMPS * span * points,
            transcendentals=0,
        ),
        name="rotate_dft",
    )(*args)
    return out[:n], out[n:] if first else shared


def stack_width(n, rows):
    main, tail, height = layout(rows)
    return -(-rows // 16) * 16 + (n - 1) * (height - (COMPS - 1) * main)


def selection(n, owned, slots, span, blocks, me, sel_ref):
    group = owned * 2
    main, tail, height = layout(slots * group)
    rest = height - COMPS * main
    shape = sel_ref.shape[1:]
    out = lax.broadcasted_iota(jnp.int32, shape, 0)
    col = lax.broadcasted_iota(jnp.int32, shape, 1)
    at = -(-slots * group // 16) * 16
    lo = jnp.broadcast_to(first_block(me, span), shape)
    row = jnp.where(col < slots * group, col, -1)
    comp = jnp.full(shape, -1, jnp.int32)
    for size, base in ((main, 0), (rest, main)):
        for k in range(1, n):
            here = (col >= at) & (col < at + size)
            lo = jnp.where(here, first_block(lax.rem(me + n - k, n), span), lo)
            if base == 0:
                row = jnp.where(here, col - at, row)
            elif tail:
                piece = (col - at) // tail
                row = jnp.where(here, jnp.where(piece < COMPS, main + (col - at) % tail, -1), row)
                comp = jnp.where(here, piece, comp)
            at += size
    same = (row >= 0) & (out // blocks == row % group) & (out % blocks == lo + row // group)
    for c in range(COMPS):
        sel_ref[c] = jnp.where(same & ((comp < 0) | (comp == c)), 1.0, 0.0).astype(jnp.bfloat16)


def assemble_body(n, owned, slots, span, blocks, total, has_sum, last, *refs):
    pos_ref = refs[0]
    parts = refs[1:1 + n]
    *rest, acc_ref = refs[1 + n:]
    if has_sum:
        sum_in, sel_ref, _, spectra_ref, gram_ref = rest
    else:
        spectra_ref, gram_ref, sel_ref = rest
    step = pl.program_id(0)
    main, tail, height = layout(slots * owned * 2)
    rows = parts[0].shape[0] // COMPS
    order = 2 * blocks

    @pl.when(step == 0)
    def _():
        if not has_sum:
            selection(n, owned, slots, span, blocks, pos_ref[0], sel_ref)
        acc_ref[...] = sum_in[...] if has_sum else jnp.zeros_like(acc_ref)

    for c in range(COMPS):
        pieces = [parts[0][c * rows:(c + 1) * rows, :]]
        if main:
            pieces += [p[c * main:(c + 1) * main, :] for p in parts[1:]]
        if height > COMPS * main:
            pieces += [p[COMPS * main:, :] for p in parts[1:]]
        stack = jnp.concatenate(pieces, axis=0)
        full = jnp.dot(sel_ref[c], stack, preferred_element_type=jnp.float32)
        for j in range(owned):
            for r in range(2):
                at = (j * 2 + r) * blocks
                spectra_ref[j, r, c] = full[at:at + blocks]
        high = full.astype(jnp.bfloat16)
        low = (full - high.astype(jnp.float32)).astype(jnp.bfloat16)
        pair = jnp.concatenate([high, low], axis=0)
        acc_ref[...] += lax.dot_general(
            pair, pair, (((1,), (1,)), ((), ())), preferred_element_type=jnp.float32
        )

    @pl.when(step == pl.num_programs(0) - 1)
    def _():
        if not last:
            gram_ref[...] = acc_ref[...]
        else:
            m = owned * order
            acc = acc_ref[...]
            gram = (acc[:m, :m] + (acc[:m, m:] + acc[m:, :m])) * (1.0 / total)
            gram_ref[...] = jnp.concatenate(
                [gram[j * order:(j + 1) * order, j * order:(j + 1) * order] for j in range(owned)], axis=1
            )


def assemble_call(n, owned, slots, span, blocks, total, offset, points, all_points, position, parts, spectra, gram, sel, last):
    tile = min(points, 512)
    shift = offset // tile
    order = 2 * blocks
    has_sum = gram is not None
    whole = lambda shape: pl.BlockSpec(shape, lambda i: (0,) * len(shape))
    acc_shape = (2 * owned * order, 2 * owned * order)
    gram_shape = (order, owned * order) if last else acc_shape
    sel_shape = (COMPS, owned * order, stack_width(n, slots * owned * 2))
    args = [position] + list(parts)
    in_specs = [pl.BlockSpec(memory_space=pltpu.SMEM)]
    in_specs += [pl.BlockSpec((p.shape[0], tile), lambda i: (0, i)) for p in parts]
    out_shape = [
        jax.ShapeDtypeStruct((owned, 2, COMPS, blocks, all_points), jnp.float32),
        jax.ShapeDtypeStruct(gram_shape, jnp.float32),
    ]
    out_specs = [
        pl.BlockSpec((owned, 2, COMPS, blocks, tile), lambda i: (0, 0, 0, 0, i + shift)),
        whole(gram_shape),
    ]
    aliases = {}
    if has_sum:
        args += [gram, sel, spectra]
        in_specs += [whole(acc_shape), whole(sel_shape), pl.BlockSpec(memory_space=pl.ANY)]
        aliases = {len(args) - 1: 0}
    else:
        out_shape.append(jax.ShapeDtypeStruct(sel_shape, jnp.bfloat16))
        out_specs.append(whole(sel_shape))
    out = pl.pallas_call(
        functools.partial(assemble_body, n, owned, slots, span, blocks, total, has_sum, last),
        grid=(points // tile,),
        out_shape=out_shape,
        in_specs=in_specs,
        out_specs=out_specs,
        scratch_shapes=[pltpu.VMEM(acc_shape, jnp.float32)],
        input_output_aliases=aliases,
        compiler_params=pltpu.CompilerParams(vmem_limit_bytes=40 * 2**20),
        cost_estimate=pl.CostEstimate(
            flops=4 * 192 * 192 * COMPS * points,
            bytes_accessed=4 * owned * order * COMPS * points,
            transcendentals=0,
        ),
        name="assemble",
    )(*args)
    return list(out[:2]) + [sel if has_sum else out[2]]


def factor_body(owned, order, count, *refs):
    parts = refs[:count]
    out_ref, row_ref = refs[count:]
    s = [p[...] for p in parts]
    while len(s) > 1:
        s = [a + b for a, b in zip(s[::2], s[1::2])]
    s = s[0]
    lane = lax.broadcasted_iota(jnp.int32, (1, owned * order), 1)
    for k in range(0, order, PIVOT):
        base = k // 8 * 8
        s = s[base - max(k - PIVOT, 0) // 8 * 8:]
        columns = []
        for i in range(k, k + PIVOT):
            column = jnp.broadcast_to(s[:, i:i + 1], s.shape)
            for j in range(1, owned):
                column = jnp.where(lane >= j * order, s[:, j * order + i:j * order + i + 1], column)
            columns.append(column)
        at = k - base
        rows = [s[at + i:at + i + 1] for i in range(PIVOT)]
        for i in range(PIVOT):
            inverse_root = lax.rsqrt(columns[i][at + i:at + i + 1])
            columns[i] = columns[i] * inverse_root
            rows[i] = rows[i] * inverse_root
            for j in range(i + 1, PIVOT):
                weight = columns[i][at + j:at + j + 1]
                columns[j] = columns[j] - columns[i] * weight
                rows[j] = rows[j] - rows[i] * weight
            row_ref[k + i:k + i + 1, :] = jnp.where(lane % order >= k + i, rows[i], 0.0)
            s = s - columns[i] * rows[i]
    for j in range(owned):
        out_ref[j] = row_ref[:, j * order:(j + 1) * order]


def factor_call(owned, order, parts):
    return pl.pallas_call(
        functools.partial(factor_body, owned, order, len(parts)),
        out_shape=jax.ShapeDtypeStruct((owned, order, order), jnp.float32),
        scratch_shapes=[pltpu.VMEM((order, owned * order), jnp.float32)],
        name="factor",
    )(*parts)


def sum_over_space(gram, groups):
    if groups != 8:
        return [lax.psum(gram, "space")]
    swap = lambda x, k: lax.ppermute(x, "space", [(i, i ^ k) for i in range(groups)])
    gram = gram + swap(gram, 1)
    gram = gram + swap(gram, 2)
    return [gram, swap(gram, 4)]


def chunks_of(points):
    tile = 512
    return [(at, tile) for at in range(0, points, tile)]


def per_device(velocity, rotor_mask, rotor_angle, block_starts, frequencies):
    span, _, points = velocity.shape
    n = lax.axis_size("tm")
    groups = lax.axis_size("space")
    blocks = block_starts.shape[0]
    owned = frequencies.shape[0] // n
    order = 2 * blocks
    slots = slot_count(n, span, blocks)
    position = lax.axis_index("tm").astype(jnp.int32).reshape(1)
    samples = velocity.transpose(1, 0, 2)
    mask = rotor_mask.reshape(1, points)
    angles = rotor_angle

    pieces = []
    shared = None
    for at, count in chunks_of(points):
        sums, shared = dft_call(
            n, owned, slots, blocks, shared is None, at, count,
            position, block_starts, frequencies, angles, mask, samples, shared,
        )
        moved = [sums[0]] + [
            lax.ppermute(sums[k], "tm", [(i, (i + k) % n) for i in range(n)]) for k in range(1, n)
        ]
        pieces.append((at, count, moved))

    spectra, gram, sel = None, None, None
    total = COMPS * points * groups
    for at, count, moved in pieces:
        last = at + count == points
        spectra, gram, sel = assemble_call(
            n, owned, slots, span, blocks, total, at, count, points, position, moved, spectra, gram, sel, last
        )
    factors = factor_call(owned, order, sum_over_space(gram, groups))
    return spectra.transpose(0, 1, 3, 2, 4), factors


def solution(mesh):
    in_specs = (P("tm", None, "space"), P("space"), P("tm"), P(), P())
    out_specs = (P("tm", None, None, None, "space"), P("tm", None, None))
    return jax.shard_map(
        per_device, mesh=mesh, in_specs=in_specs, out_specs=out_specs, check_vma=False
    )
```

```python
import functools
import math

import jax
import jax.numpy as jnp
from jax import lax
from jax.experimental import pallas as pl
from jax.experimental.pallas import tpu as pltpu
from jax.sharding import PartitionSpec as P

COMPS = 3
NFFT = 256
JIT = 64
HOP = 128
LANES = 128
TILE = 256
PIVOT = 16
SCALE = (8.0 / (3.0 * NFFT)) ** 0.5
HIGHEST = lax.Precision.HIGHEST


def first_block(shard, span):
    return jnp.maximum((shard * span - (NFFT + JIT - 1) + HOP) // HOP, 0)


def slot_count(shards, span, blocks):
    most = 0
    for s in range(shards):
        lo = max((s * span - (NFFT + JIT - 1) + HOP) // HOP, 0)
        hi = min((span * (s + 1) - 1) // HOP, blocks - 1)
        most = max(most, hi - lo + 1)
    return most


def half_turn_sine(x):
    z = x * x
    c = [math.pi ** (2 * i + 1) * (-1) ** i / math.factorial(2 * i + 1) for i in range(7)]
    acc = jnp.full_like(z, c[-1])
    for term in c[-2::-1]:
        acc = acc * z + term
    return acc * x


def layout(rows):
    main = rows // 16 * 16
    return main, rows - main, -(-COMPS * rows // 8) * 8


def cosine_of(turns):
    s = half_turn_sine(turns - jnp.floor(turns + 0.5))
    return 1.0 - 2.0 * s * s


def build_rows(n, owned, slots, span, blocks, me, starts_ref, freqs_ref, a_ref):
    group = owned * 2
    lo = first_block(me, span)
    starts = [starts_ref[jnp.minimum(lo + s, blocks - 1)] for s in range(slots)]

    def by_slot(shape, axis):
        at = lax.broadcasted_iota(jnp.int32, shape, axis)
        out = jnp.full(shape, starts[0], jnp.int32)
        for s in range(1, slots):
            out = jnp.where(at == s, starts[s], out)
        return out

    rid = lax.broadcasted_iota(jnp.int32, (n * group, 1), 0)
    f_of = lax.rem(me + rid // group, n) * owned + (rid // 2) % owned
    freq = jnp.zeros((n * group, 1), jnp.float32)
    for f in range(n * owned):
        freq = jnp.where(f_of == f, freqs_ref[f].astype(jnp.float32), freq)
    step = freq * (1.0 / NFFT)
    quarter = (rid % 2).astype(jnp.float32) * 0.25

    sample = lax.broadcasted_iota(jnp.int32, (1, span), 1) + me * span
    turns = sample.astype(jnp.float32) * step
    turns = turns - jnp.floor(turns) + quarter
    cos_t, sin_t = cosine_of(turns), cosine_of(turns - 0.25)
    begin = by_slot((1, LANES), 1).astype(jnp.float32) * step
    begin = begin - jnp.floor(begin)
    cos_b, sin_b = cosine_of(begin), cosine_of(begin - 0.25)

    slot = lax.broadcasted_iota(jnp.int32, (16, 1), 0)
    ni = sample - by_slot((16, 1), 0)
    nf = ni.astype(jnp.float32)
    w = half_turn_sine(jnp.minimum(nf, NFFT - nf) * (1.0 / NFFT))
    w = jnp.where((ni >= 0) & (ni < NFFT) & (slot + lo < blocks), w * w * SCALE, 0.0)

    pieces = [[] for _ in range(n)]
    for s in range(slots):
        rows = (cos_t * cos_b[:, s:s + 1] + sin_t * sin_b[:, s:s + 1]) * w[s:s + 1]
        for k in range(n):
            pieces[k].append(rows[k * group:(k + 1) * group])
    padding = a_ref.shape[1] - slots * group
    for k in range(n):
        if padding:
            pieces[k].append(jnp.zeros((padding, span), jnp.float32))
        a_ref[k] = jnp.concatenate(pieces[k], axis=0).astype(jnp.bfloat16)


def spread_column(row, span, out_ref):
    for at in range(0, span, LANES):
        width = min(LANES, span - at)
        part = row[:, at:at + width]
        if width < LANES:
            part = jnp.concatenate([part, jnp.zeros((1, LANES - width), jnp.float32)], axis=1)
        turned = jnp.transpose(jnp.broadcast_to(part, (LANES, LANES)))
        out_ref[at:at + width, :] = turned[:width]


def dft_body(n, owned, slots, span, blocks, first, *refs):
    if first:
        pos_ref, starts_ref, freqs_ref, angle_ref, mask_ref, vel_ref = refs[:6]
        outs = refs[6:6 + n]
        a_ref, cos_ref, sin_ref = refs[6 + n:9 + n]
        rot_ref = refs[9 + n]

        @pl.when(pl.program_id(0) == 0)
        def _():
            build_rows(n, owned, slots, span, blocks, pos_ref[0], starts_ref, freqs_ref, a_ref)
            spread_column(jnp.cos(angle_ref[...].reshape(1, span)), span, cos_ref)
            spread_column(jnp.sin(angle_ref[...].reshape(1, span)), span, sin_ref)
    else:
        mask_ref, vel_ref, a_ref, cos_ref, sin_ref = refs[:5]
        outs = refs[5:5 + n]
        rot_ref = refs[5 + n]
    width = vel_ref.shape[2]
    turning = mask_ref[...] == 1
    for at in range(0, span, 16):
        rows = min(16, span - at)
        here = pl.ds(at, rows)
        cosine = jnp.concatenate([cos_ref[here, :]] * (width // LANES), axis=1)
        sine = jnp.concatenate([sin_ref[here, :]] * (width // LANES), axis=1)
        x = vel_ref[0, here, :].astype(jnp.float32)
        y = vel_ref[1, here, :].astype(jnp.float32)
        rot_ref[0, here, :] = jnp.where(turning, cosine * x - sine * y, x).astype(jnp.bfloat16)
        rot_ref[1, here, :] = jnp.where(turning, sine * x + cosine * y, y).astype(jnp.bfloat16)
    rows = a_ref.shape[1]
    main, tail, height = layout(slots * owned * 2)
    a = a_ref[...].reshape(n * rows, span)
    tails = []
    for c in range(COMPS):
        samples = rot_ref[c] if c < 2 else vel_ref[2]
        sums = jnp.dot(a, samples, preferred_element_type=jnp.float32)
        outs[0][c * rows:(c + 1) * rows, :] = sums[:rows].astype(jnp.bfloat16)
        if main:
            for k in range(1, n):
                outs[k][c * main:(c + 1) * main, :] = sums[k * rows:k * rows + main].astype(jnp.bfloat16)
        tails.append(sums)
    if height > COMPS * main:
        for k in range(1, n):
            parts = [t[k * rows + main:k * rows + main + tail] for t in tails] if tail else []
            padding = height - COMPS * (main + tail)
            if padding:
                parts.append(jnp.zeros((padding, width), jnp.float32))
            outs[k][COMPS * main:, :] = jnp.concatenate(parts, axis=0).astype(jnp.bfloat16)


def dft_call(n, owned, slots, blocks, first, offset, points, position, starts, freqs, angles, mask, velocity, shared):
    span = velocity.shape[1]
    rows = -(-slots * owned * 2 // 16) * 16
    heights = [COMPS * rows] + [layout(slots * owned * 2)[2]] * (n - 1)
    shift = offset // TILE
    whole = lambda shape: pl.BlockSpec(shape, lambda i: (0,) * len(shape))
    smem = pl.BlockSpec(memory_space=pltpu.SMEM)
    data_specs = [
        pl.BlockSpec((1, TILE), lambda i: (0, i + shift)),
        pl.BlockSpec((COMPS, span, TILE), lambda i: (0, 0, i + shift)),
    ]
    shared_types = [
        jax.ShapeDtypeStruct((n, rows, span), jnp.bfloat16),
        jax.ShapeDtypeStruct((span, LANES), jnp.float32),
        jax.ShapeDtypeStruct((span, LANES), jnp.float32),
    ]
    shared_specs = [whole(t.shape) for t in shared_types]
    out_types = [jax.ShapeDtypeStruct((h, points), jnp.bfloat16) for h in heights]
    out_specs = [pl.BlockSpec((h, TILE), lambda i: (0, i)) for h in heights]
    if first:
        args = (position, starts, freqs, angles, mask, velocity)
        in_specs = [smem] * 3 + [whole((span,))] + data_specs
        out_types = out_types + shared_types
        out_specs = out_specs + shared_specs
    else:
        args = (mask, velocity) + tuple(shared)
        in_specs = data_specs + shared_specs
    out = pl.pallas_call(
        functools.partial(dft_body, n, owned, slots, span, blocks, first),
        grid=(points // TILE,),
        out_shape=out_types,
        in_specs=in_specs,
        out_specs=out_specs,
        scratch_shapes=[pltpu.VMEM((2, span, TILE), jnp.bfloat16)],
        compiler_params=pltpu.CompilerParams(vmem_limit_bytes=(60 if first else 40) * 2**20),
        cost_estimate=pl.CostEstimate(
            flops=2 * n * rows * span * COMPS * points,
            bytes_accessed=2 * COMPS * span * points,
            transcendentals=0,
        ),
        name="rotate_dft",
    )(*args)
    return out[:n], out[n:] if first else shared


def stack_width(n, rows):
    main, tail, height = layout(rows)
    return -(-rows // 16) * 16 + (n - 1) * (height - (COMPS - 1) * main)


def selection(n, owned, slots, span, blocks, me, sel_ref):
    group = owned * 2
    main, tail, height = layout(slots * group)
    rest = height - COMPS * main
    shape = sel_ref.shape[1:]
    out = lax.broadcasted_iota(jnp.int32, shape, 0)
    col = lax.broadcasted_iota(jnp.int32, shape, 1)
    at = -(-slots * group // 16) * 16
    lo = jnp.broadcast_to(first_block(me, span), shape)
    row = jnp.where(col < slots * group, col, -1)
    comp = jnp.full(shape, -1, jnp.int32)
    for size, base in ((main, 0), (rest, main)):
        for k in range(1, n):
            here = (col >= at) & (col < at + size)
            lo = jnp.where(here, first_block(lax.rem(me + n - k, n), span), lo)
            if base == 0:
                row = jnp.where(here, col - at, row)
            elif tail:
                piece = (col - at) // tail
                row = jnp.where(here, jnp.where(piece < COMPS, main + (col - at) % tail, -1), row)
                comp = jnp.where(here, piece, comp)
            at += size
    same = (row >= 0) & (out // blocks == row % group) & (out % blocks == lo + row // group)
    for c in range(COMPS):
        sel_ref[c] = jnp.where(same & ((comp < 0) | (comp == c)), 1.0, 0.0).astype(jnp.bfloat16)


def assemble_body(n, owned, slots, span, blocks, total, has_sum, last, *refs):
    pos_ref = refs[0]
    parts = refs[1:1 + n]
    *rest, acc_ref = refs[1 + n:]
    if has_sum:
        sum_in, sel_ref, _, spectra_ref, gram_ref = rest
    else:
        spectra_ref, gram_ref, sel_ref = rest
    step = pl.program_id(0)
    main, tail, height = layout(slots * owned * 2)
    rows = parts[0].shape[0] // COMPS
    order = 2 * blocks

    @pl.when(step == 0)
    def _():
        if not has_sum:
            selection(n, owned, slots, span, blocks, pos_ref[0], sel_ref)
        acc_ref[...] = sum_in[...] if has_sum else jnp.zeros_like(acc_ref)

    for c in range(COMPS):
        pieces = [parts[0][c * rows:(c + 1) * rows, :]]
        if main:
            pieces += [p[c * main:(c + 1) * main, :] for p in parts[1:]]
        if height > COMPS * main:
            pieces += [p[COMPS * main:, :] for p in parts[1:]]
        stack = jnp.concatenate(pieces, axis=0)
        full = jnp.dot(sel_ref[c], stack, preferred_element_type=jnp.float32)
        for j in range(owned):
            for r in range(2):
                at = (j * 2 + r) * blocks
                spectra_ref[j, r, c] = full[at:at + blocks]
        high = full.astype(jnp.bfloat16)
        low = (full - high.astype(jnp.float32)).astype(jnp.bfloat16)
        pair = jnp.concatenate([high, low], axis=0)
        acc_ref[...] += lax.dot_general(
            pair, pair, (((1,), (1,)), ((), ())), preferred_element_type=jnp.float32
        )

    @pl.when(step == pl.num_programs(0) - 1)
    def _():
        if not last:
            gram_ref[...] = acc_ref[...]
        else:
            m = owned * order
            acc = acc_ref[...]
            gram = (acc[:m, :m] + (acc[:m, m:] + acc[m:, :m])) * (1.0 / total)
            gram_ref[...] = jnp.concatenate(
                [gram[j * order:(j + 1) * order, j * order:(j + 1) * order] for j in range(owned)], axis=1
            )


def assemble_call(n, owned, slots, span, blocks, total, offset, points, all_points, position, parts, spectra, gram, sel, last):
    tile = TILE
    shift = offset // tile
    order = 2 * blocks
    has_sum = gram is not None
    whole = lambda shape: pl.BlockSpec(shape, lambda i: (0,) * len(shape))
    acc_shape = (2 * owned * order, 2 * owned * order)
    gram_shape = (order, owned * order) if last else acc_shape
    sel_shape = (COMPS, owned * order, stack_width(n, slots * owned * 2))
    args = [position] + list(parts)
    in_specs = [pl.BlockSpec(memory_space=pltpu.SMEM)]
    in_specs += [pl.BlockSpec((p.shape[0], tile), lambda i: (0, i)) for p in parts]
    out_shape = [
        jax.ShapeDtypeStruct((owned, 2, COMPS, blocks, all_points), jnp.float32),
        jax.ShapeDtypeStruct(gram_shape, jnp.float32),
    ]
    out_specs = [
        pl.BlockSpec((owned, 2, COMPS, blocks, tile), lambda i: (0, 0, 0, 0, i + shift)),
        whole(gram_shape),
    ]
    aliases = {}
    if has_sum:
        args += [gram, sel, spectra]
        in_specs += [whole(acc_shape), whole(sel_shape), pl.BlockSpec(memory_space=pl.ANY)]
        aliases = {len(args) - 1: 0}
    else:
        out_shape.append(jax.ShapeDtypeStruct(sel_shape, jnp.bfloat16))
        out_specs.append(whole(sel_shape))
    out = pl.pallas_call(
        functools.partial(assemble_body, n, owned, slots, span, blocks, total, has_sum, last),
        grid=(points // tile,),
        out_shape=out_shape,
        in_specs=in_specs,
        out_specs=out_specs,
        scratch_shapes=[pltpu.VMEM(acc_shape, jnp.float32)],
        input_output_aliases=aliases,
        compiler_params=pltpu.CompilerParams(vmem_limit_bytes=40 * 2**20),
        cost_estimate=pl.CostEstimate(
            flops=4 * 192 * 192 * COMPS * points,
            bytes_accessed=4 * owned * order * COMPS * points,
            transcendentals=0,
        ),
        name="assemble",
    )(*args)
    return list(out[:2]) + [sel if has_sum else out[2]]


def factor_body(owned, order, count, *refs):
    parts = refs[:count]
    out_ref, row_ref = refs[count:]
    s = [p[...] for p in parts]
    while len(s) > 1:
        s = [a + b for a, b in zip(s[::2], s[1::2])]
    s = s[0]
    lane = lax.broadcasted_iota(jnp.int32, (1, owned * order), 1)
    for k in range(0, order, PIVOT):
        base = k // 8 * 8
        s = s[base - max(k - PIVOT, 0) // 8 * 8:]
        columns = []
        for i in range(k, k + PIVOT):
            column = jnp.broadcast_to(s[:, i:i + 1], s.shape)
            for j in range(1, owned):
                column = jnp.where(lane >= j * order, s[:, j * order + i:j * order + i + 1], column)
            columns.append(column)
        at = k - base
        rows = [s[at + i:at + i + 1] for i in range(PIVOT)]
        for i in range(PIVOT):
            inverse_root = lax.rsqrt(columns[i][at + i:at + i + 1])
            columns[i] = columns[i] * inverse_root
            rows[i] = rows[i] * inverse_root
            for j in range(i + 1, PIVOT):
                weight = columns[i][at + j:at + j + 1]
                columns[j] = columns[j] - columns[i] * weight
                rows[j] = rows[j] - rows[i] * weight
            row_ref[k + i:k + i + 1, :] = jnp.where(lane % order >= k + i, rows[i], 0.0)
            s = s - columns[i] * rows[i]
    for j in range(owned):
        out_ref[j] = row_ref[:, j * order:(j + 1) * order]


def factor_call(owned, order, parts):
    return pl.pallas_call(
        functools.partial(factor_body, owned, order, len(parts)),
        out_shape=jax.ShapeDtypeStruct((owned, order, order), jnp.float32),
        scratch_shapes=[pltpu.VMEM((order, owned * order), jnp.float32)],
        name="factor",
    )(*parts)


def sum_over_space(gram, groups):
    if groups != 8:
        return [lax.psum(gram, "space")]
    swap = lambda x, k: lax.ppermute(x, "space", [(i, i ^ k) for i in range(groups)])
    gram = gram + swap(gram, 1)
    gram = gram + swap(gram, 2)
    return [gram, swap(gram, 4)]


def chunks_of(points):
    cuts = [points * k // 8 for k in (0, 2, 4, 7, 8)]
    return [(a, b - a) for a, b in zip(cuts[:-1], cuts[1:])]


def per_device(velocity, rotor_mask, rotor_angle, block_starts, frequencies):
    span, _, points = velocity.shape
    n = lax.axis_size("tm")
    groups = lax.axis_size("space")
    blocks = block_starts.shape[0]
    owned = frequencies.shape[0] // n
    order = 2 * blocks
    slots = slot_count(n, span, blocks)
    position = lax.axis_index("tm").astype(jnp.int32).reshape(1)
    samples = velocity.transpose(1, 0, 2)
    mask = rotor_mask.reshape(1, points)
    angles = rotor_angle

    pieces = []
    shared = None
    for at, count in chunks_of(points):
        sums, shared = dft_call(
            n, owned, slots, blocks, shared is None, at, count,
            position, block_starts, frequencies, angles, mask, samples, shared,
        )
        moved = [sums[0]] + [
            lax.ppermute(sums[k], "tm", [(i, (i + k) % n) for i in range(n)]) for k in range(1, n)
        ]
        pieces.append((at, count, moved))

    spectra, gram, sel = None, None, None
    total = COMPS * points * groups
    for at, count, moved in pieces:
        last = at + count == points
        spectra, gram, sel = assemble_call(
            n, owned, slots, span, blocks, total, at, count, points, position, moved, spectra, gram, sel, last
        )
    factors = factor_call(owned, order, sum_over_space(gram, groups))
    return spectra.transpose(0, 1, 3, 2, 4), factors


def solution(mesh):
    in_specs = (P("tm", None, "space"), P("space"), P("tm"), P(), P())
    out_specs = (P("tm", None, None, None, "space"), P("tm", None, None))
    return jax.shard_map(
        per_device, mesh=mesh, in_specs=in_specs, out_specs=out_specs, check_vma=False
    )
```

```python
import functools
import math

import jax
import jax.numpy as jnp
from jax import lax
from jax.experimental import pallas as pl
from jax.experimental.pallas import tpu as pltpu
from jax.sharding import PartitionSpec as P

COMPS = 3
NFFT = 256
JIT = 64
HOP = 128
LANES = 128
TILE = 256
PIVOT = 16
SCALE = (8.0 / (3.0 * NFFT)) ** 0.5
HIGHEST = lax.Precision.HIGHEST


def first_block(shard, span):
    return jnp.maximum((shard * span - (NFFT + JIT - 1) + HOP) // HOP, 0)


def slot_count(shards, span, blocks):
    most = 0
    for s in range(shards):
        lo = max((s * span - (NFFT + JIT - 1) + HOP) // HOP, 0)
        hi = min((span * (s + 1) - 1) // HOP, blocks - 1)
        most = max(most, hi - lo + 1)
    return most


def half_turn_sine(x):
    z = x * x
    c = [math.pi ** (2 * i + 1) * (-1) ** i / math.factorial(2 * i + 1) for i in range(7)]
    acc = jnp.full_like(z, c[-1])
    for term in c[-2::-1]:
        acc = acc * z + term
    return acc * x


def layout(rows):
    main = rows // 16 * 16
    return main, rows - main, -(-COMPS * rows // 8) * 8


def cosine_of(turns):
    s = half_turn_sine(turns - jnp.floor(turns + 0.5))
    return 1.0 - 2.0 * s * s


def build_rows(n, owned, slots, span, blocks, me, starts_ref, freqs_ref, a_ref):
    group = owned * 2
    lo = first_block(me, span)
    starts = [starts_ref[jnp.minimum(lo + s, blocks - 1)] for s in range(slots)]

    def by_slot(shape, axis):
        at = lax.broadcasted_iota(jnp.int32, shape, axis)
        out = jnp.full(shape, starts[0], jnp.int32)
        for s in range(1, slots):
            out = jnp.where(at == s, starts[s], out)
        return out

    rid = lax.broadcasted_iota(jnp.int32, (n * group, 1), 0)
    f_of = lax.rem(me + rid // group, n) * owned + (rid // 2) % owned
    freq = jnp.zeros((n * group, 1), jnp.float32)
    for f in range(n * owned):
        freq = jnp.where(f_of == f, freqs_ref[f].astype(jnp.float32), freq)
    step = freq * (1.0 / NFFT)
    quarter = (rid % 2).astype(jnp.float32) * 0.25

    sample = lax.broadcasted_iota(jnp.int32, (1, span), 1) + me * span
    turns = sample.astype(jnp.float32) * step
    turns = turns - jnp.floor(turns) + quarter
    cos_t, sin_t = cosine_of(turns), cosine_of(turns - 0.25)
    begin = by_slot((1, LANES), 1).astype(jnp.float32) * step
    begin = begin - jnp.floor(begin)
    cos_b, sin_b = cosine_of(begin), cosine_of(begin - 0.25)

    slot = lax.broadcasted_iota(jnp.int32, (16, 1), 0)
    ni = sample - by_slot((16, 1), 0)
    nf = ni.astype(jnp.float32)
    w = half_turn_sine(jnp.minimum(nf, NFFT - nf) * (1.0 / NFFT))
    w = jnp.where((ni >= 0) & (ni < NFFT) & (slot + lo < blocks), w * w * SCALE, 0.0)

    pieces = [[] for _ in range(n)]
    for s in range(slots):
        rows = (cos_t * cos_b[:, s:s + 1] + sin_t * sin_b[:, s:s + 1]) * w[s:s + 1]
        for k in range(n):
            pieces[k].append(rows[k * group:(k + 1) * group])
    padding = a_ref.shape[1] - slots * group
    for k in range(n):
        if padding:
            pieces[k].append(jnp.zeros((padding, span), jnp.float32))
        a_ref[k] = jnp.concatenate(pieces[k], axis=0).astype(jnp.bfloat16)


def spread_column(row, span, out_ref):
    for at in range(0, span, LANES):
        width = min(LANES, span - at)
        part = row[:, at:at + width]
        if width < LANES:
            part = jnp.concatenate([part, jnp.zeros((1, LANES - width), jnp.float32)], axis=1)
        turned = jnp.transpose(jnp.broadcast_to(part, (LANES, LANES)))
        out_ref[at:at + width, :] = turned[:width]


def dft_body(n, owned, slots, span, blocks, offset, mode, *refs):
    *refs, rot_ref = refs
    step = pl.program_id(0)
    if mode == "use":
        mask_ref, vel_ref, a_ref, cos_ref, sin_ref = refs[:5]
        outs = refs[5:]
    else:
        pos_ref, starts_ref, freqs_ref, angle_ref, mask_ref, vel_ref = refs[:6]
        outs = refs[6:6 + n]
        a_ref, cos_ref, sin_ref = refs[6 + n:9 + n]
    if mode == "lead":
        vel_hbm, (held_ref, sem) = vel_ref, refs[9 + n:]

        def load(i):
            columns = pl.ds(pl.multiple_of(offset + i * TILE, TILE), TILE)
            return pltpu.make_async_copy(vel_hbm.at[:, :, columns], held_ref.at[i], sem.at[i])

        @pl.when(step == 0)
        def _():
            for i in range(held_ref.shape[0]):
                load(i).start()

    if mode != "use":

        @pl.when(step == 0)
        def _():
            build_rows(n, owned, slots, span, blocks, pos_ref[0], starts_ref, freqs_ref, a_ref)
            spread_column(jnp.cos(angle_ref[...].reshape(1, span)), span, cos_ref)
            spread_column(jnp.sin(angle_ref[...].reshape(1, span)), span, sin_ref)

    if mode == "lead":
        load(step).wait()
        vel_ref = held_ref.at[step]
    width = vel_ref.shape[2]
    turning = mask_ref[...] == 1
    for at in range(0, span, 16):
        rows = min(16, span - at)
        here = pl.ds(at, rows)
        cosine = jnp.concatenate([cos_ref[here, :]] * (width // LANES), axis=1)
        sine = jnp.concatenate([sin_ref[here, :]] * (width // LANES), axis=1)
        x = vel_ref[0, here, :].astype(jnp.float32)
        y = vel_ref[1, here, :].astype(jnp.float32)
        rot_ref[0, here, :] = jnp.where(turning, cosine * x - sine * y, x).astype(jnp.bfloat16)
        rot_ref[1, here, :] = jnp.where(turning, sine * x + cosine * y, y).astype(jnp.bfloat16)
    rows = a_ref.shape[1]
    main, tail, height = layout(slots * owned * 2)
    a = a_ref[...].reshape(n * rows, span)
    tails = []
    for c in range(COMPS):
        samples = rot_ref[c] if c < 2 else vel_ref[2]
        sums = jnp.dot(a, samples, preferred_element_type=jnp.float32)
        outs[0][c * rows:(c + 1) * rows, :] = sums[:rows].astype(jnp.bfloat16)
        if main:
            for k in range(1, n):
                outs[k][c * main:(c + 1) * main, :] = sums[k * rows:k * rows + main].astype(jnp.bfloat16)
        tails.append(sums)
    if height > COMPS * main:
        for k in range(1, n):
            parts = [t[k * rows + main:k * rows + main + tail] for t in tails] if tail else []
            padding = height - COMPS * (main + tail)
            if padding:
                parts.append(jnp.zeros((padding, width), jnp.float32))
            outs[k][COMPS * main:, :] = jnp.concatenate(parts, axis=0).astype(jnp.bfloat16)


def dft_call(n, owned, slots, blocks, mode, offset, points, position, starts, freqs, angles, mask, velocity, shared):
    span = velocity.shape[1]
    rows = -(-slots * owned * 2 // 16) * 16
    heights = [COMPS * rows] + [layout(slots * owned * 2)[2]] * (n - 1)
    shift = offset // TILE
    whole = lambda shape: pl.BlockSpec(shape, lambda i: (0,) * len(shape))
    smem = pl.BlockSpec(memory_space=pltpu.SMEM)
    data_specs = [
        pl.BlockSpec((1, TILE), lambda i: (0, i + shift)),
        pl.BlockSpec((COMPS, span, TILE), lambda i: (0, 0, i + shift)),
    ]
    shared_types = [
        jax.ShapeDtypeStruct((n, rows, span), jnp.bfloat16),
        jax.ShapeDtypeStruct((span, LANES), jnp.float32),
        jax.ShapeDtypeStruct((span, LANES), jnp.float32),
    ]
    shared_specs = [whole(t.shape) for t in shared_types]
    out_types = [jax.ShapeDtypeStruct((h, points), jnp.bfloat16) for h in heights]
    out_specs = [pl.BlockSpec((h, TILE), lambda i: (0, i)) for h in heights]
    scratch = []
    if mode != "use":
        args = (position, starts, freqs, angles, mask, velocity)
        in_specs = [smem] * 3 + [whole((span,))] + data_specs
    if mode == "lead":
        in_specs[-1] = pl.BlockSpec(memory_space=pl.ANY)
        scratch += [pltpu.VMEM(t.shape, t.dtype) for t in shared_types]
        scratch.append(pltpu.VMEM((points // TILE, COMPS, span, TILE), jnp.bfloat16))
        scratch.append(pltpu.SemaphoreType.DMA((points // TILE,)))
    elif mode == "build":
        out_types = out_types + shared_types
        out_specs = out_specs + shared_specs
    else:
        args = (mask, velocity) + tuple(shared)
        in_specs = data_specs + shared_specs
    out = pl.pallas_call(
        functools.partial(dft_body, n, owned, slots, span, blocks, offset, mode),
        grid=(points // TILE,),
        out_shape=out_types,
        in_specs=in_specs,
        out_specs=out_specs,
        scratch_shapes=scratch + [pltpu.VMEM((2, span, TILE), jnp.bfloat16)],
        compiler_params=pltpu.CompilerParams(vmem_limit_bytes=(60 if mode == "lead" else 40) * 2**20),
        cost_estimate=pl.CostEstimate(
            flops=2 * n * rows * span * COMPS * points,
            bytes_accessed=2 * COMPS * span * points,
            transcendentals=0,
        ),
        name="rotate_dft",
    )(*args)
    return out[:n], out[n:] if mode == "build" else shared


def stack_width(n, rows):
    main, tail, height = layout(rows)
    return -(-rows // 16) * 16 + (n - 1) * (height - (COMPS - 1) * main)


def selection(n, owned, slots, span, blocks, me, sel_ref):
    group = owned * 2
    main, tail, height = layout(slots * group)
    rest = height - COMPS * main
    shape = sel_ref.shape[1:]
    out = lax.broadcasted_iota(jnp.int32, shape, 0)
    col = lax.broadcasted_iota(jnp.int32, shape, 1)
    at = -(-slots * group // 16) * 16
    lo = jnp.broadcast_to(first_block(me, span), shape)
    row = jnp.where(col < slots * group, col, -1)
    comp = jnp.full(shape, -1, jnp.int32)
    for size, base in ((main, 0), (rest, main)):
        for k in range(1, n):
            here = (col >= at) & (col < at + size)
            lo = jnp.where(here, first_block(lax.rem(me + n - k, n), span), lo)
            if base == 0:
                row = jnp.where(here, col - at, row)
            elif tail:
                piece = (col - at) // tail
                row = jnp.where(here, jnp.where(piece < COMPS, main + (col - at) % tail, -1), row)
                comp = jnp.where(here, piece, comp)
            at += size
    same = (row >= 0) & (out // blocks == row % group) & (out % blocks == lo + row // group)
    for c in range(COMPS):
        sel_ref[c] = jnp.where(same & ((comp < 0) | (comp == c)), 1.0, 0.0).astype(jnp.bfloat16)


def assemble_body(n, owned, slots, span, blocks, total, has_sum, last, *refs):
    pos_ref = refs[0]
    parts = refs[1:1 + n]
    *rest, acc_ref = refs[1 + n:]
    if has_sum:
        sum_in, sel_ref, _, spectra_ref, gram_ref = rest
    else:
        spectra_ref, gram_ref, sel_ref = rest
    step = pl.program_id(0)
    main, tail, height = layout(slots * owned * 2)
    rows = parts[0].shape[0] // COMPS
    order = 2 * blocks

    @pl.when(step == 0)
    def _():
        if not has_sum:
            selection(n, owned, slots, span, blocks, pos_ref[0], sel_ref)
        acc_ref[...] = sum_in[...] if has_sum else jnp.zeros_like(acc_ref)

    for c in range(COMPS):
        pieces = [parts[0][c * rows:(c + 1) * rows, :]]
        if main:
            pieces += [p[c * main:(c + 1) * main, :] for p in parts[1:]]
        if height > COMPS * main:
            pieces += [p[COMPS * main:, :] for p in parts[1:]]
        stack = jnp.concatenate(pieces, axis=0)
        full = jnp.dot(sel_ref[c], stack, preferred_element_type=jnp.float32)
        for j in range(owned):
            for r in range(2):
                at = (j * 2 + r) * blocks
                spectra_ref[j, r, c] = full[at:at + blocks]
        high = full.astype(jnp.bfloat16)
        low = (full - high.astype(jnp.float32)).astype(jnp.bfloat16)
        pair = jnp.concatenate([high, low], axis=0)
        acc_ref[...] += lax.dot_general(
            pair, pair, (((1,), (1,)), ((), ())), preferred_element_type=jnp.float32
        )

    @pl.when(step == pl.num_programs(0) - 1)
    def _():
        if not last:
            gram_ref[...] = acc_ref[...]
        else:
            m = owned * order
            acc = acc_ref[...]
            gram = (acc[:m, :m] + (acc[:m, m:] + acc[m:, :m])) * (1.0 / total)
            gram_ref[...] = jnp.concatenate(
                [gram[j * order:(j + 1) * order, j * order:(j + 1) * order] for j in range(owned)], axis=1
            )


def assemble_call(n, owned, slots, span, blocks, total, offset, points, all_points, position, parts, spectra, gram, sel, last):
    tile = min(points, 512)
    shift = offset // tile
    order = 2 * blocks
    has_sum = gram is not None
    whole = lambda shape: pl.BlockSpec(shape, lambda i: (0,) * len(shape))
    acc_shape = (2 * owned * order, 2 * owned * order)
    gram_shape = (order, owned * order) if last else acc_shape
    sel_shape = (COMPS, owned * order, stack_width(n, slots * owned * 2))
    args = [position] + list(parts)
    in_specs = [pl.BlockSpec(memory_space=pltpu.SMEM)]
    in_specs += [pl.BlockSpec((p.shape[0], tile), lambda i: (0, i)) for p in parts]
    out_shape = [
        jax.ShapeDtypeStruct((owned, 2, COMPS, blocks, all_points), jnp.float32),
        jax.ShapeDtypeStruct(gram_shape, jnp.float32),
    ]
    out_specs = [
        pl.BlockSpec((owned, 2, COMPS, blocks, tile), lambda i: (0, 0, 0, 0, i + shift)),
        whole(gram_shape),
    ]
    aliases = {}
    if has_sum:
        args += [gram, sel, spectra]
        in_specs += [whole(acc_shape), whole(sel_shape), pl.BlockSpec(memory_space=pl.ANY)]
        aliases = {len(args) - 1: 0}
    else:
        out_shape.append(jax.ShapeDtypeStruct(sel_shape, jnp.bfloat16))
        out_specs.append(whole(sel_shape))
    out = pl.pallas_call(
        functools.partial(assemble_body, n, owned, slots, span, blocks, total, has_sum, last),
        grid=(points // tile,),
        out_shape=out_shape,
        in_specs=in_specs,
        out_specs=out_specs,
        scratch_shapes=[pltpu.VMEM(acc_shape, jnp.float32)],
        input_output_aliases=aliases,
        compiler_params=pltpu.CompilerParams(vmem_limit_bytes=40 * 2**20),
        cost_estimate=pl.CostEstimate(
            flops=4 * 192 * 192 * COMPS * points,
            bytes_accessed=4 * owned * order * COMPS * points,
            transcendentals=0,
        ),
        name="assemble",
    )(*args)
    return list(out[:2]) + [sel if has_sum else out[2]]


def factor_body(owned, order, count, *refs):
    parts = refs[:count]
    out_ref, row_ref = refs[count:]
    s = [p[...] for p in parts]
    while len(s) > 1:
        s = [a + b for a, b in zip(s[::2], s[1::2])]
    s = s[0]
    lane = lax.broadcasted_iota(jnp.int32, (1, owned * order), 1)
    for k in range(0, order, PIVOT):
        base = k // 8 * 8
        s = s[base - max(k - PIVOT, 0) // 8 * 8:]
        columns = []
        for i in range(k, k + PIVOT):
            column = jnp.broadcast_to(s[:, i:i + 1], s.shape)
            for j in range(1, owned):
                column = jnp.where(lane >= j * order, s[:, j * order + i:j * order + i + 1], column)
            columns.append(column)
        at = k - base
        rows = [s[at + i:at + i + 1] for i in range(PIVOT)]
        for i in range(PIVOT):
            inverse_root = lax.rsqrt(columns[i][at + i:at + i + 1])
            columns[i] = columns[i] * inverse_root
            rows[i] = rows[i] * inverse_root
            for j in range(i + 1, PIVOT):
                weight = columns[i][at + j:at + j + 1]
                columns[j] = columns[j] - columns[i] * weight
                rows[j] = rows[j] - rows[i] * weight
            row_ref[k + i:k + i + 1, :] = jnp.where(lane % order >= k + i, rows[i], 0.0)
            s = s - columns[i] * rows[i]
    for j in range(owned):
        out_ref[j] = row_ref[:, j * order:(j + 1) * order]


def factor_call(owned, order, parts):
    return pl.pallas_call(
        functools.partial(factor_body, owned, order, len(parts)),
        out_shape=jax.ShapeDtypeStruct((owned, order, order), jnp.float32),
        scratch_shapes=[pltpu.VMEM((order, owned * order), jnp.float32)],
        name="factor",
    )(*parts)


def sum_over_space(gram, groups):
    if groups != 8:
        return [lax.psum(gram, "space")]
    swap = lambda x, k: lax.ppermute(x, "space", [(i, i ^ k) for i in range(groups)])
    gram = gram + swap(gram, 1)
    gram = gram + swap(gram, 2)
    return [gram, swap(gram, 4)]


def chunks_of(points):
    tile = 512
    return [(at, tile) for at in range(0, points, tile)]


def per_device(velocity, rotor_mask, rotor_angle, block_starts, frequencies):
    span, _, points = velocity.shape
    n = lax.axis_size("tm")
    groups = lax.axis_size("space")
    blocks = block_starts.shape[0]
    owned = frequencies.shape[0] // n
    order = 2 * blocks
    slots = slot_count(n, span, blocks)
    position = lax.axis_index("tm").astype(jnp.int32).reshape(1)
    samples = velocity.transpose(1, 0, 2)
    mask = rotor_mask.reshape(1, points)
    angles = rotor_angle

    pieces = []
    shared = None
    for i, (at, count) in enumerate(chunks_of(points)):
        sums, shared = dft_call(
            n, owned, slots, blocks, ("lead", "build")[i] if i < 2 else "use", at, count,
            position, block_starts, frequencies, angles, mask, samples, shared,
        )
        moved = [sums[0]] + [
            lax.ppermute(sums[k], "tm", [(j, (j + k) % n) for j in range(n)]) for k in range(1, n)
        ]
        pieces.append((at, count, moved))

    spectra, gram, sel = None, None, None
    total = COMPS * points * groups
    for at, count, moved in pieces:
        last = at + count == points
        spectra, gram, sel = assemble_call(
            n, owned, slots, span, blocks, total, at, count, points, position, moved, spectra, gram, sel, last
        )
    factors = factor_call(owned, order, sum_over_space(gram, groups))
    return spectra.transpose(0, 1, 3, 2, 4), factors


def solution(mesh):
    in_specs = (P("tm", None, "space"), P("space"), P("tm"), P(), P())
    out_specs = (P("tm", None, None, None, "space"), P("tm", None, None))
    return jax.shard_map(
        per_device, mesh=mesh, in_specs=in_specs, out_specs=out_specs, check_vma=False
    )
```

```python
import functools
import math

import jax
import jax.numpy as jnp
from jax import lax
from jax.experimental import pallas as pl
from jax.experimental.pallas import tpu as pltpu
from jax.sharding import PartitionSpec as P

COMPS = 3
NFFT = 256
JIT = 64
HOP = 128
LANES = 128
TILE = 256
PIVOT = 16
SCALE = (8.0 / (3.0 * NFFT)) ** 0.5
HIGHEST = lax.Precision.HIGHEST


def first_block(shard, span):
    return jnp.maximum((shard * span - (NFFT + JIT - 1) + HOP) // HOP, 0)


def slot_count(shards, span, blocks):
    most = 0
    for s in range(shards):
        lo = max((s * span - (NFFT + JIT - 1) + HOP) // HOP, 0)
        hi = min((span * (s + 1) - 1) // HOP, blocks - 1)
        most = max(most, hi - lo + 1)
    return most


def half_turn_sine(x):
    z = x * x
    c = [math.pi ** (2 * i + 1) * (-1) ** i / math.factorial(2 * i + 1) for i in range(7)]
    acc = jnp.full_like(z, c[-1])
    for term in c[-2::-1]:
        acc = acc * z + term
    return acc * x


def layout(rows):
    main = rows // 16 * 16
    return main, rows - main, -(-COMPS * rows // 8) * 8


def cosine_of(turns):
    s = half_turn_sine(turns - jnp.floor(turns + 0.5))
    return 1.0 - 2.0 * s * s


def build_rows(n, owned, slots, blocks, me, lo, sample, known, starts_ref, freqs_ref, a_ref):
    group = owned * 2
    width = a_ref.shape[2]
    starts = [starts_ref[jnp.minimum(lo + s, blocks - 1)] for s in range(slots)]

    def by_slot(shape, axis):
        at = lax.broadcasted_iota(jnp.int32, shape, axis)
        out = jnp.full(shape, starts[0], jnp.int32)
        for s in range(1, slots):
            out = jnp.where(at == s, starts[s], out)
        return out

    rid = lax.broadcasted_iota(jnp.int32, (n * group, 1), 0)
    f_of = lax.rem(me + rid // group, n) * owned + (rid // 2) % owned
    freq = jnp.zeros((n * group, 1), jnp.float32)
    for f in range(n * owned):
        freq = jnp.where(f_of == f, freqs_ref[f].astype(jnp.float32), freq)
    step = freq * (1.0 / NFFT)
    quarter = (rid % 2).astype(jnp.float32) * 0.25

    turns = sample.astype(jnp.float32) * step
    turns = turns - jnp.floor(turns) + quarter
    cos_t, sin_t = cosine_of(turns), cosine_of(turns - 0.25)
    begin = by_slot((1, LANES), 1).astype(jnp.float32) * step
    begin = begin - jnp.floor(begin)
    cos_b, sin_b = cosine_of(begin), cosine_of(begin - 0.25)

    slot = lax.broadcasted_iota(jnp.int32, (16, 1), 0)
    ni = sample - by_slot((16, 1), 0)
    nf = ni.astype(jnp.float32)
    w = half_turn_sine(jnp.minimum(nf, NFFT - nf) * (1.0 / NFFT))
    w = jnp.where((ni >= 0) & (ni < NFFT) & (slot + lo < blocks) & known, w * w * SCALE, 0.0)

    pieces = [[] for _ in range(n)]
    for s in range(slots):
        rows = (cos_t * cos_b[:, s:s + 1] + sin_t * sin_b[:, s:s + 1]) * w[s:s + 1]
        for k in range(n):
            pieces[k].append(rows[k * group:(k + 1) * group])
    padding = a_ref.shape[1] - slots * group
    for k in range(n):
        if padding:
            pieces[k].append(jnp.zeros((padding, width), jnp.float32))
        a_ref[k] = jnp.concatenate(pieces[k], axis=0).astype(jnp.bfloat16)


LINE_LO = [0, 6, 15, 23]
LINE_HI = [8, 16, 25, 31]
SHORT = 10
EDGE = 16


def skipped(shard):
    return jnp.where(shard == 1, 1, 0)


def fits_line(n, span, blocks, owned):
    if n != 4 or owned != 2 or blocks != 32 or span < 1072:
        return False
    lo = [max((s * span - (NFFT + JIT - 1) + HOP) // HOP, 0) for s in range(n)]
    hi = [min((span * (s + 1) - 1) // HOP, blocks - 1) for s in range(n)]
    reach = max(HOP * LINE_LO[1] + JIT - 1 + NFFT - span, 3 * span - HOP * LINE_HI[2])
    return lo == LINE_LO and hi == LINE_HI and reach <= EDGE


def spread_column(row, span, out_ref):
    for at in range(0, span, LANES):
        width = min(LANES, span - at)
        part = row[:, at:at + width]
        if width < LANES:
            part = jnp.concatenate([part, jnp.zeros((1, LANES - width), jnp.float32)], axis=1)
        turned = jnp.transpose(jnp.broadcast_to(part, (LANES, LANES)))
        out_ref[at:at + width, :] = turned[:width]


def dft_body(n, owned, slots, span, blocks, offset, mode, line, *refs):
    *refs, rot_ref = refs
    step = pl.program_id(0)
    if mode == "use":
        mask_ref, vel_ref, a_ref, cos_ref, sin_ref = refs[:5]
        if line:
            near_ref, edge_ref = refs[5:7]
            slots = SHORT
        outs = refs[-n:]
    else:
        pos_ref, starts_ref, freqs_ref, angle_ref, mask_ref, vel_ref = refs[:6]
        outs = refs[6:6 + n]
        a_ref, cos_ref, sin_ref = refs[6 + n:9 + n]
        if mode == "build" and line:
            short_ref, cos_ref, sin_ref, near_ref, a_ref = refs[6 + n:]
    if mode == "lead":
        if line:
            edge_mask_ref, edge_out_ref = refs[6], refs[7 + n]
            outs = refs[7:7 + n]
            a_ref, cos_ref, sin_ref, held_ref, sem, edge_ref, edge_sem = refs[8 + n:]
        else:
            held_ref, sem = refs[9 + n:]
        vel_hbm = vel_ref

        def load(i):
            columns = pl.ds(pl.multiple_of(offset + i * TILE, TILE), TILE)
            return pltpu.make_async_copy(vel_hbm.at[:, :, columns], held_ref.at[i], sem.at[i])

        if line:
            begin = pl.multiple_of(jnp.where(pos_ref[0] == 2, span - EDGE, 0), EDGE)
            count = edge_ref.shape[2]
            half = vel_hbm.shape[2] - count

            def load_edge():
                return pltpu.make_async_copy(vel_hbm.at[:, pl.ds(begin, EDGE), pl.ds(half, count)], edge_ref, edge_sem)

        @pl.when(step == 0)
        def _():
            for i in range(held_ref.shape[0]):
                load(i).start()
            if line:
                load_edge().start()

    if mode != "use":

        @pl.when(step == 0)
        def _():
            me = pos_ref[0]
            lo = first_block(me, span)
            sample = lax.broadcasted_iota(jnp.int32, (1, span), 1) + me * span
            build_rows(n, owned, slots, blocks, me, lo, sample, True, starts_ref, freqs_ref, a_ref)
            if line and mode == "build":
                lo = lo + skipped(me)
                build_rows(n, owned, SHORT, blocks, me, lo, sample, True, starts_ref, freqs_ref, short_ref)
                edge = lax.broadcasted_iota(jnp.int32, (1, EDGE), 1) + jnp.where(me == 3, me * span - EDGE, span)
                left = jnp.where(me == 0, LINE_LO[1], LINE_HI[2])
                mine = (lax.broadcasted_iota(jnp.int32, (16, 1), 0) + lo == left) & ((me == 0) | (me == 3))
                build_rows(n, owned, SHORT, blocks, me, lo, edge, mine, starts_ref, freqs_ref, near_ref)
            spread_column(jnp.cos(angle_ref[...].reshape(1, span)), span, cos_ref)
            spread_column(jnp.sin(angle_ref[...].reshape(1, span)), span, sin_ref)
            if line and mode == "lead":
                load_edge().wait()
                cosine = jnp.concatenate([cos_ref[pl.ds(begin, EDGE), :]] * (count // LANES), axis=1)
                sine = jnp.concatenate([sin_ref[pl.ds(begin, EDGE), :]] * (count // LANES), axis=1)
                x, y = edge_ref[0].astype(jnp.float32), edge_ref[1].astype(jnp.float32)
                there = edge_mask_ref[...] == 1
                edge_out_ref[:EDGE, :] = jnp.where(there, cosine * x - sine * y, x).astype(jnp.bfloat16)
                edge_out_ref[EDGE:2 * EDGE, :] = jnp.where(there, sine * x + cosine * y, y).astype(jnp.bfloat16)
                edge_out_ref[2 * EDGE:, :] = edge_ref[2]

    if mode == "lead":
        load(step).wait()
        vel_ref = held_ref.at[step]
    width = vel_ref.shape[2]
    turning = mask_ref[...] == 1
    for at in range(0, span, 16):
        rows = min(16, span - at)
        here = pl.ds(at, rows)
        cosine = jnp.concatenate([cos_ref[here, :]] * (width // LANES), axis=1)
        sine = jnp.concatenate([sin_ref[here, :]] * (width // LANES), axis=1)
        x = vel_ref[0, here, :].astype(jnp.float32)
        y = vel_ref[1, here, :].astype(jnp.float32)
        rot_ref[0, here, :] = jnp.where(turning, cosine * x - sine * y, x).astype(jnp.bfloat16)
        rot_ref[1, here, :] = jnp.where(turning, sine * x + cosine * y, y).astype(jnp.bfloat16)
    rows = a_ref.shape[1]
    main, tail, height = layout(slots * owned * 2)
    a = a_ref[...].reshape(n * rows, span)
    tails = []
    for c in range(COMPS):
        samples = rot_ref[c] if c < 2 else vel_ref[2]
        sums = jnp.dot(a, samples, preferred_element_type=jnp.float32)
        if mode == "use" and line:
            sums += jnp.dot(
                near_ref[...].reshape(n * rows, EDGE), edge_ref[c * EDGE:(c + 1) * EDGE, :],
                preferred_element_type=jnp.float32,
            )
        outs[0][c * rows:(c + 1) * rows, :] = sums[:rows].astype(jnp.bfloat16)
        if main:
            for k in range(1, n):
                outs[k][c * main:(c + 1) * main, :] = sums[k * rows:k * rows + main].astype(jnp.bfloat16)
        tails.append(sums)
    if height > COMPS * main:
        for k in range(1, n):
            parts = [t[k * rows + main:k * rows + main + tail] for t in tails] if tail else []
            padding = height - COMPS * (main + tail)
            if padding:
                parts.append(jnp.zeros((padding, width), jnp.float32))
            outs[k][COMPS * main:, :] = jnp.concatenate(parts, axis=0).astype(jnp.bfloat16)


def dft_call(n, owned, slots, blocks, mode, offset, points, position, starts, freqs, angles, mask, velocity, shared, line=False, edge=None):
    span, all_points = velocity.shape[1:]
    if line and mode == "use":
        slots = SHORT
    rows = -(-slots * owned * 2 // 16) * 16
    heights = [COMPS * rows] + [layout(slots * owned * 2)[2]] * (n - 1)
    shift = offset // TILE
    whole = lambda shape: pl.BlockSpec(shape, lambda i: (0,) * len(shape))
    smem = pl.BlockSpec(memory_space=pltpu.SMEM)
    data_specs = [
        pl.BlockSpec((1, TILE), lambda i: (0, i + shift)),
        pl.BlockSpec((COMPS, span, TILE), lambda i: (0, 0, i + shift)),
    ]
    shared_types = [
        jax.ShapeDtypeStruct((n, rows, span), jnp.bfloat16),
        jax.ShapeDtypeStruct((span, LANES), jnp.float32),
        jax.ShapeDtypeStruct((span, LANES), jnp.float32),
    ]
    shared_specs = [whole(t.shape) for t in shared_types]
    out_types = [jax.ShapeDtypeStruct((h, points), jnp.bfloat16) for h in heights]
    out_specs = [pl.BlockSpec((h, TILE), lambda i: (0, i)) for h in heights]
    scratch = []
    if mode != "use":
        args = (position, starts, freqs, angles, mask, velocity)
        in_specs = [smem] * 3 + [whole((span,))] + data_specs
    if mode == "lead":
        in_specs[-1] = pl.BlockSpec(memory_space=pl.ANY)
        scratch += [pltpu.VMEM(t.shape, t.dtype) for t in shared_types]
        scratch.append(pltpu.VMEM((points // TILE, COMPS, span, TILE), jnp.bfloat16))
        scratch.append(pltpu.SemaphoreType.DMA((points // TILE,)))
        if line:
            half = all_points // 2
            args += (mask,)
            in_specs.append(pl.BlockSpec((1, half), lambda i: (0, 1)))
            out_types = out_types + [jax.ShapeDtypeStruct((COMPS * EDGE, half), jnp.bfloat16)]
            out_specs = out_specs + [whole((COMPS * EDGE, half))]
            scratch += [pltpu.VMEM((COMPS, EDGE, half), jnp.bfloat16), pltpu.SemaphoreType.DMA]
    elif mode == "build":
        if line:
            shared_types.append(jax.ShapeDtypeStruct((n, rows, EDGE), jnp.bfloat16))
            shared_specs.append(whole((n, rows, EDGE)))
            scratch.append(pltpu.VMEM((n, rows, span), jnp.bfloat16))
        out_types = out_types + shared_types
        out_specs = out_specs + shared_specs
    else:
        args = (mask, velocity) + tuple(shared)
        in_specs = data_specs + shared_specs
        if line:
            first_edge = (all_points - edge.shape[1]) // TILE
            args += (edge,)
            in_specs.append(whole(shared[3].shape))
            in_specs.append(pl.BlockSpec((edge.shape[0], TILE), lambda i: (0, i + shift - first_edge)))
    out = pl.pallas_call(
        functools.partial(dft_body, n, owned, slots, span, blocks, offset, mode, line),
        grid=(points // TILE,),
        out_shape=out_types,
        in_specs=in_specs,
        out_specs=out_specs,
        scratch_shapes=scratch + [pltpu.VMEM((2, span, TILE), jnp.bfloat16)],
        compiler_params=pltpu.CompilerParams(vmem_limit_bytes=(60 if mode == "lead" else 40) * 2**20),
        cost_estimate=pl.CostEstimate(
            flops=2 * n * rows * span * COMPS * points,
            bytes_accessed=2 * COMPS * span * points,
            transcendentals=0,
        ),
        name="rotate_dft",
    )(*args)
    return out[:n], out[n:] if mode != "use" else shared


def stack_width(n, rows):
    main, tail, height = layout(rows)
    return -(-rows // 16) * 16 + (n - 1) * (height - (COMPS - 1) * main)


def selection(n, owned, slots, span, blocks, short, me, sel_ref):
    group = owned * 2
    main, tail, height = layout(slots * group)
    rest = height - COMPS * main
    shape = sel_ref.shape[1:]
    out = lax.broadcasted_iota(jnp.int32, shape, 0)
    col = lax.broadcasted_iota(jnp.int32, shape, 1)
    at = -(-slots * group // 16) * 16
    begin = lambda shard: first_block(shard, span) + (skipped(shard) if short else 0)
    lo = jnp.broadcast_to(begin(me), shape)
    row = jnp.where(col < slots * group, col, -1)
    comp = jnp.full(shape, -1, jnp.int32)
    for size, base in ((main, 0), (rest, main)):
        for k in range(1, n):
            here = (col >= at) & (col < at + size)
            lo = jnp.where(here, begin(lax.rem(me + n - k, n)), lo)
            if base == 0:
                row = jnp.where(here, col - at, row)
            elif tail:
                piece = (col - at) // tail
                row = jnp.where(here, jnp.where(piece < COMPS, main + (col - at) % tail, -1), row)
                comp = jnp.where(here, piece, comp)
            at += size
    same = (row >= 0) & (out // blocks == row % group) & (out % blocks == lo + row // group)
    for c in range(COMPS):
        sel_ref[c] = jnp.where(same & ((comp < 0) | (comp == c)), 1.0, 0.0).astype(jnp.bfloat16)


def assemble_body(n, owned, slots, span, blocks, total, short, has_sum, has_sel, last, *refs):
    pos_ref = refs[0]
    parts = refs[1:1 + n]
    *rest, acc_ref = refs[1 + n:]
    if has_sum:
        sum_in, *rest = rest
    if has_sel:
        sel_ref, *rest = rest
    else:
        *rest, sel_ref = rest
    spectra_ref, gram_ref = rest[-2:]
    step = pl.program_id(0)
    main, tail, height = layout(slots * owned * 2)
    rows = parts[0].shape[0] // COMPS
    order = 2 * blocks

    @pl.when(step == 0)
    def _():
        if not has_sel:
            selection(n, owned, slots, span, blocks, short, pos_ref[0], sel_ref)
        acc_ref[...] = sum_in[...] if has_sum else jnp.zeros_like(acc_ref)

    for c in range(COMPS):
        pieces = [parts[0][c * rows:(c + 1) * rows, :]]
        if main:
            pieces += [p[c * main:(c + 1) * main, :] for p in parts[1:]]
        if height > COMPS * main:
            pieces += [p[COMPS * main:, :] for p in parts[1:]]
        stack = jnp.concatenate(pieces, axis=0)
        full = jnp.dot(sel_ref[c], stack, preferred_element_type=jnp.float32)
        for j in range(owned):
            for r in range(2):
                at = (j * 2 + r) * blocks
                spectra_ref[j, r, c] = full[at:at + blocks]
        high = full.astype(jnp.bfloat16)
        low = (full - high.astype(jnp.float32)).astype(jnp.bfloat16)
        pair = jnp.concatenate([high, low], axis=0)
        acc_ref[...] += lax.dot_general(
            pair, pair, (((1,), (1,)), ((), ())), preferred_element_type=jnp.float32
        )

    @pl.when(step == pl.num_programs(0) - 1)
    def _():
        if not last:
            gram_ref[...] = acc_ref[...]
        else:
            m = owned * order
            acc = acc_ref[...]
            gram = (acc[:m, :m] + (acc[:m, m:] + acc[m:, :m])) * (1.0 / total)
            gram_ref[...] = jnp.concatenate(
                [gram[j * order:(j + 1) * order, j * order:(j + 1) * order] for j in range(owned)], axis=1
            )


def assemble_call(n, owned, slots, span, blocks, total, offset, points, all_points, position, parts, spectra, gram, sel, last, short):
    tile = min(points, 512)
    shift = offset // tile
    order = 2 * blocks
    has_sum = gram is not None
    has_sel = sel is not None
    whole = lambda shape: pl.BlockSpec(shape, lambda i: (0,) * len(shape))
    acc_shape = (2 * owned * order, 2 * owned * order)
    gram_shape = (order, owned * order) if last else acc_shape
    sel_shape = (COMPS, owned * order, stack_width(n, slots * owned * 2))
    args = [position] + list(parts)
    in_specs = [pl.BlockSpec(memory_space=pltpu.SMEM)]
    in_specs += [pl.BlockSpec((p.shape[0], tile), lambda i: (0, i)) for p in parts]
    out_shape = [
        jax.ShapeDtypeStruct((owned, 2, COMPS, blocks, all_points), jnp.float32),
        jax.ShapeDtypeStruct(gram_shape, jnp.float32),
    ]
    out_specs = [
        pl.BlockSpec((owned, 2, COMPS, blocks, tile), lambda i: (0, 0, 0, 0, i + shift)),
        whole(gram_shape),
    ]
    aliases = {}
    if has_sum:
        args.append(gram)
        in_specs.append(whole(acc_shape))
    if has_sel:
        args.append(sel)
        in_specs.append(whole(sel_shape))
    if has_sum:
        args.append(spectra)
        in_specs.append(pl.BlockSpec(memory_space=pl.ANY))
        aliases = {len(args) - 1: 0}
    if not has_sel:
        out_shape.append(jax.ShapeDtypeStruct(sel_shape, jnp.bfloat16))
        out_specs.append(whole(sel_shape))
    out = pl.pallas_call(
        functools.partial(assemble_body, n, owned, slots, span, blocks, total, short, has_sum, has_sel, last),
        grid=(points // tile,),
        out_shape=out_shape,
        in_specs=in_specs,
        out_specs=out_specs,
        scratch_shapes=[pltpu.VMEM(acc_shape, jnp.float32)],
        input_output_aliases=aliases,
        compiler_params=pltpu.CompilerParams(vmem_limit_bytes=40 * 2**20),
        cost_estimate=pl.CostEstimate(
            flops=4 * 192 * 192 * COMPS * points,
            bytes_accessed=4 * owned * order * COMPS * points,
            transcendentals=0,
        ),
        name="assemble",
    )(*args)
    return list(out[:2]) + [sel if has_sel else out[2]]


def factor_body(owned, order, count, *refs):
    parts = refs[:count]
    out_ref, row_ref = refs[count:]
    s = [p[...] for p in parts]
    while len(s) > 1:
        s = [a + b for a, b in zip(s[::2], s[1::2])]
    s = s[0]
    lane = lax.broadcasted_iota(jnp.int32, (1, owned * order), 1)
    for k in range(0, order, PIVOT):
        base = k // 8 * 8
        s = s[base - max(k - PIVOT, 0) // 8 * 8:]
        columns = []
        for i in range(k, k + PIVOT):
            column = jnp.broadcast_to(s[:, i:i + 1], s.shape)
            for j in range(1, owned):
                column = jnp.where(lane >= j * order, s[:, j * order + i:j * order + i + 1], column)
            columns.append(column)
        at = k - base
        rows = [s[at + i:at + i + 1] for i in range(PIVOT)]
        for i in range(PIVOT):
            inverse_root = lax.rsqrt(columns[i][at + i:at + i + 1])
            columns[i] = columns[i] * inverse_root
            rows[i] = rows[i] * inverse_root
            for j in range(i + 1, PIVOT):
                weight = columns[i][at + j:at + j + 1]
                columns[j] = columns[j] - columns[i] * weight
                rows[j] = rows[j] - rows[i] * weight
            row_ref[k + i:k + i + 1, :] = jnp.where(lane % order >= k + i, rows[i], 0.0)
            s = s - columns[i] * rows[i]
    for j in range(owned):
        out_ref[j] = row_ref[:, j * order:(j + 1) * order]


def factor_call(owned, order, parts):
    return pl.pallas_call(
        functools.partial(factor_body, owned, order, len(parts)),
        out_shape=jax.ShapeDtypeStruct((owned, order, order), jnp.float32),
        scratch_shapes=[pltpu.VMEM((order, owned * order), jnp.float32)],
        name="factor",
    )(*parts)


def sum_over_space(gram, groups):
    if groups != 8:
        return [lax.psum(gram, "space")]
    swap = lambda x, k: lax.ppermute(x, "space", [(i, i ^ k) for i in range(groups)])
    gram = gram + swap(gram, 1)
    gram = gram + swap(gram, 2)
    return [gram, swap(gram, 4)]


def chunks_of(points):
    tile = 512
    return [(at, tile) for at in range(0, points, tile)]


def per_device(velocity, rotor_mask, rotor_angle, block_starts, frequencies):
    span, _, points = velocity.shape
    n = lax.axis_size("tm")
    groups = lax.axis_size("space")
    blocks = block_starts.shape[0]
    owned = frequencies.shape[0] // n
    order = 2 * blocks
    slots = slot_count(n, span, blocks)
    position = lax.axis_index("tm").astype(jnp.int32).reshape(1)
    samples = velocity.transpose(1, 0, 2)
    mask = rotor_mask.reshape(1, points)
    angles = rotor_angle

    pieces = []
    shared, edge = None, None
    line = fits_line(n, span, blocks, owned)
    half = points // 2
    for i, (at, count) in enumerate(chunks_of(points)):
        sums, shared = dft_call(
            n, owned, slots, blocks, ("lead", "build")[i] if i < 2 else "use", at, count,
            position, block_starts, frequencies, angles, mask, samples, shared, line, edge,
        )
        if line and i == 0:
            edge = lax.ppermute(shared[0], "tm", [(1, 0), (2, 3)])
        moved = [sums[0]] + [
            lax.ppermute(sums[k], "tm", [(j, (j + k) % n) for j in range(n)]) for k in range(1, n)
        ]
        pieces.append((at, count, moved))

    spectra, gram, sel = None, None, None
    total = COMPS * points * groups
    for at, count, moved in pieces:
        short = line and at >= half
        if short and at == half:
            sel = None
        spectra, gram, sel = assemble_call(
            n, owned, SHORT if short else slots, span, blocks, total, at, count, points, position, moved,
            spectra, gram, sel, at + count == points, short,
        )
    factors = factor_call(owned, order, sum_over_space(gram, groups))
    return spectra.transpose(0, 1, 3, 2, 4), factors


def solution(mesh):
    in_specs = (P("tm", None, "space"), P("space"), P("tm"), P(), P())
    out_specs = (P("tm", None, None, None, "space"), P("tm", None, None))
    return jax.shard_map(
        per_device, mesh=mesh, in_specs=in_specs, out_specs=out_specs, check_vma=False
    )
```
